32 devices in a mesh: ens: 4 (over x, core), dom: 8 (over z, y).
Axes of the slice: x: 2, y: 2, z: 4, core: 2. Of those that a mesh axis runs over, the one named last changes fastest.
Arguments:
- nodes: bfloat16 [4, 4096, 512], P('ens', 'dom'), may hold values from -6 to 6
- senders: int32 [6, 4096], P(None, 'dom'), may hold values from 0 to 767
- send_next: int32 [1024], P('dom'), may hold values from 0 to 511
- send_prev: int32 [1024], P('dom'), may hold values from 0 to 511
- readout_vertex_list: int32 [3, 32768], P(None, 'dom'), may hold values from 0 to 767
- dec_weights: float32 [3, 32768], P(None, 'dom'), may hold values from 0.2 to 1
- base: bfloat16 [32768, 128], P('dom'), may hold values from -6 to 6
- observed_analysis: bfloat16 [32768, 128], P('dom'), may hold values from -8 to 8
- w_send: bfloat16 [512, 512], replicated, may hold values from -0.25 to 0.25
- w_recv: bfloat16 [512, 512], replicated, may hold values from -0.25 to 0.25
- vertex_refresh_matrix: bfloat16 [512, 512], replicated, may hold values from -0.25 to 0.25
- w_decode: bfloat16 [512, 128], replicated, may hold values from -0.25 to 0.25
Outputs:
- g_send: float32 [512, 512], replicated
- g_recv: float32 [512, 512], replicated
- g_update: float32 [512, 512], replicated
- g_decode: float32 [512, 128], replicated
- loss: float32 [], replicated
The draws below stay inside these ranges and needn't reach their ends.
All inputs are finite; a program needn't handle non-finite values.
Results may differ from the reference program's by a relative error of at most 0.0045.
Values may be sent and summed in bfloat16 or wider, within the bound.
No kernel may reach another device: no remote copies, remote signals or barrier semaphores. Data moves between devices by JAX's collectives and lax.ppermute only.
A program may use at most 64 MiB of HBM per device.

```python
import jax
import jax.numpy as jnp
from jax import lax

W = 512
V = 128
DEG = 6
K = 3
NODE_DEV = 512
GRID_DEV = 4096
HALO = 128
MEMBERS = 4
NODES = 4096
GRID = 32768
N_DOM = 8


def plant(entries, rng, smallest, high):
    dims = entries.shape
    spot = [jax.random.randint(jax.random.fold_in(rng, axis), (), 0, dims[axis]) for axis in range(len(dims))]
    entries = entries.at[tuple(spot)].set(smallest)
    longest = dims.index(max(dims))
    spot[longest] = (spot[longest] + 1) % dims[longest]
    return entries.at[tuple(spot)].set(high)


def steps_of(own_key, shape, shards, smallest, largest):
    level = 1.0
    for dim, shards_of in shards:
        steps = jax.random.uniform(jax.random.fold_in(jax.random.fold_in(own_key, 6), dim), (shards_of,), jnp.float32, smallest / len(shards), largest / len(shards))
        level = level * jnp.repeat(jnp.exp(steps), shape[dim] // shards_of).reshape((-1,) + (1,) * (len(shape) - 1 - dim))
    return level


def bell_draw(rng, dims, width, bound, cuts=(), dtype=jnp.bfloat16):
    gain = steps_of(rng, dims, cuts, -0.22, 0.18) if cuts else 1.0
    drawn = jax.random.normal(rng, dims, jnp.float32) * width * gain
    return jnp.minimum(jnp.maximum(drawn, -bound), bound).astype(dtype)


def setup_inputs(seed: int = 0) -> dict:
    keys = jax.random.split(jax.random.key(seed), 13)
    return {
        "nodes": bell_draw(keys[0], (MEMBERS, NODES, W), 1.0, 6.0, ((0, 4), (1, 8))),
        "senders": plant(jax.random.randint(keys[1], (DEG, NODES), 0, NODE_DEV + 2 * HALO), jax.random.fold_in(keys[1], 1), 0, (NODE_DEV + 2 * HALO) - 1).astype(jnp.int32),
        "send_next": plant(jax.random.randint(keys[2], (HALO * N_DOM,), 0, NODE_DEV), jax.random.fold_in(keys[2], 1), 0, NODE_DEV - 1).astype(jnp.int32),
        "send_prev": plant(jax.random.randint(keys[3], (HALO * N_DOM,), 0, NODE_DEV), jax.random.fold_in(keys[3], 1), 0, NODE_DEV - 1).astype(jnp.int32),
        "readout_vertex_list": plant(jax.random.randint(keys[4], (K, GRID), 0, NODE_DEV + 2 * HALO), jax.random.fold_in(keys[4], 1), 0, (NODE_DEV + 2 * HALO) - 1).astype(jnp.int32),
        "dec_weights": jnp.clip(0.2 + 0.8 * jax.random.uniform(keys[5], (K, GRID), jnp.float32) ** steps_of(keys[5], (K, GRID), ((1, 8),), -0.2, 0.2), 0.2, 1.0),
        "base": bell_draw(keys[6], (GRID, V), 1.0, 6.0, ((0, 8),)),
        "observed_analysis": bell_draw(keys[7], (GRID, V), 1.5, 8.0, ((0, 8),)),
        "w_send": bell_draw(keys[8], (W, W), W ** -0.5, 0.25),
        "w_recv": bell_draw(keys[9], (W, W), W ** -0.5, 0.25),
        "vertex_refresh_matrix": bell_draw(keys[10], (W, W), W ** -0.5, 0.25),
        "w_decode": bell_draw(keys[11], (W, V), W ** -0.5, 0.25),
    }


smoothing_epsilon = 0.04

def smooth_abs(diff):
    return jnp.sqrt(diff * diff + smoothing_epsilon)

def smooth_slope(diff):
    return diff / jnp.sqrt(diff * diff + smoothing_epsilon)

def silu_slope(value):
    sigma = jax.nn.sigmoid(value)
    return sigma * (1.0 + value * (1.0 - sigma))

def process(latent, extended, senders, w_send, w_recv, vertex_refresh_matrix):
    sent = jnp.dot(extended, w_send, preferred_element_type=jnp.float32)
    recv = jnp.dot(latent, w_recv, preferred_element_type=jnp.float32)
    pre = sent[senders] + recv[None]
    agg = (lax.optimization_barrier(jnp.sum(jax.nn.silu(pre), axis=0)) / senders.shape[0]).astype(jnp.bfloat16)
    upd = jnp.dot(agg, vertex_refresh_matrix, preferred_element_type=jnp.float32)
    hidden = (latent.astype(jnp.float32) + jax.nn.silu(upd)).astype(jnp.bfloat16)
    return (pre, agg, upd, hidden)

def backward(latent, extended, senders, pre, agg, upd, hidden, w_send, w_recv, vertex_refresh_matrix, w_decode, grad_z):
    g_decode = jnp.dot(hidden.T, grad_z, preferred_element_type=jnp.float32)
    grad_hidden = jnp.dot(grad_z, w_decode.T, preferred_element_type=jnp.float32)
    grad_upd = (grad_hidden * silu_slope(upd)).astype(jnp.bfloat16)
    g_update = jnp.dot(agg.T, grad_upd, preferred_element_type=jnp.float32)
    grad_agg = jnp.dot(grad_upd, vertex_refresh_matrix.T, preferred_element_type=jnp.float32)
    grad_pre = (grad_agg / senders.shape[0])[None] * silu_slope(pre)
    grad_recv = lax.optimization_barrier(jnp.sum(grad_pre, axis=0)).astype(jnp.bfloat16)
    g_recv = jnp.dot(latent.T, grad_recv, preferred_element_type=jnp.float32)
    grad_sent = jnp.zeros(extended.shape, jnp.float32).at[senders].add(grad_pre).astype(jnp.bfloat16)
    g_send = jnp.dot(extended.T, grad_sent, preferred_element_type=jnp.float32)
    return (g_send, g_recv, g_update, g_decode)

def member_parts(own, whole_ensemble_set, truth, line_span):
    count = whole_ensemble_set.shape[0]
    term = smooth_abs(own - truth) / count
    slope = smooth_slope(own - truth) / count
    for other in range(count):
        diff = own - whole_ensemble_set[other]
        term = term - smooth_abs(diff) / (2.0 * count * (count - 1))
        slope = slope - smooth_slope(diff) / (count * (count - 1.0))
    return (term, slope / line_span)

def adjacent_nodes(table, send_next, send_prev):
    pick = jax.vmap(lambda block, line_span: block[:, line_span], in_axes=(1, 0), out_axes=1)
    from_prev = jnp.roll(pick(table, send_next), 1, axis=1)
    from_next = jnp.roll(pick(table, send_prev), -1, axis=1)
    return (from_prev, from_next)

def reference(nodes, senders, send_next, send_prev, readout_vertex_list, dec_weights, base, observed_analysis, w_send, w_recv, vertex_refresh_matrix, w_decode):
    members = nodes.shape[0]
    parts = N_DOM
    count = NODE_DEV
    halo_rows = HALO
    line_span = GRID_DEV
    latent = nodes.reshape(members, parts, count, W)
    senders_p = senders.reshape(DEG, parts, count).transpose(1, 0, 2)
    next_p = send_next.reshape(parts, halo_rows)
    prev_p = send_prev.reshape(parts, halo_rows)
    dec_p = readout_vertex_list.reshape(K, parts, line_span).transpose(1, 0, 2)
    weights_p = dec_weights.reshape(K, parts, line_span).transpose(1, 0, 2)
    base_p = base.reshape(parts, line_span, V)
    target_p = observed_analysis.reshape(parts, line_span, V)
    lat_prev, lat_next = adjacent_nodes(latent, next_p, prev_p)

    def extended_of(part):
        return jnp.concatenate([latent[:, part], lat_prev[:, part], lat_next[:, part]], axis=1)

    def forward_part(part):
        extended = extended_of(part)
        run = lambda one, ext: process(one, ext, senders_p[part], w_send, w_recv, vertex_refresh_matrix)[3]
        hidden = jax.vmap(run)(latent[:, part], extended)
        return jnp.dot(hidden.reshape(-1, W), w_decode, preferred_element_type=jnp.float32).astype(jnp.bfloat16).reshape(members, count, V)
    field = lax.map(forward_part, jnp.arange(parts)).transpose(1, 0, 2, 3)
    field_prev, field_next = adjacent_nodes(field, next_p, prev_p)

    def readout_piece(part):
        ext = jnp.concatenate([field[:, part], field_prev[:, part], field_next[:, part]], axis=1)
        overall_aggregate = base_p[part].astype(jnp.float32)[None]
        for k in range(K):
            overall_aggregate = overall_aggregate + weights_p[part, k][None, :, None] * ext[:, dec_p[part, k]].astype(jnp.float32)
        whole_ensemble_set = overall_aggregate.astype(jnp.bfloat16).astype(jnp.float32)
        truth = target_p[part].astype(jnp.float32)
        loss_part = jnp.float32(0.0)
        slopes = []
        for own in range(members):
            term, slope = member_parts(whole_ensemble_set[own], whole_ensemble_set, truth, line_span)
            loss_part = loss_part + jnp.sum(term) / line_span
            slopes.append(slope)
        grad_x = jnp.stack(slopes)
        grad_ext = jnp.zeros((members, count + 2 * halo_rows, V), jnp.float32)
        for k in range(K):
            grad_ext = grad_ext.at[:, dec_p[part, k]].add(weights_p[part, k][None, :, None] * grad_x)
        return (grad_ext, loss_part)
    grad_ext, losses = lax.map(readout_piece, jnp.arange(parts))
    grad_ext = grad_ext.transpose(1, 0, 2, 3)
    loss = jnp.sum(losses)
    back_a = jnp.roll(grad_ext[:, :, count:count + halo_rows], -1, axis=1)
    backward_second = jnp.roll(grad_ext[:, :, count + halo_rows:], 1, axis=1)
    settle = jax.vmap(lambda own, got_a, got_b, rows_a, rows_b: own.at[:, rows_a].add(got_a).at[:, rows_b].add(got_b), in_axes=(1, 1, 1, 0, 0), out_axes=1)
    grad_z = settle(grad_ext[:, :, :count], back_a, backward_second, next_p, prev_p).astype(jnp.bfloat16)

    def grad_step(carry, part):
        extended = extended_of(part)

        def one_member(one, ext, gz):
            pre, agg, upd, hidden = process(one, ext, senders_p[part], w_send, w_recv, vertex_refresh_matrix)
            return backward(one, ext, senders_p[part], pre, agg, upd, hidden, w_send, w_recv, vertex_refresh_matrix, w_decode, gz)
        grads = jax.vmap(one_member)(latent[:, part], extended, grad_z[:, part])
        return (tuple((c + lax.optimization_barrier(jnp.sum(g, axis=0)) for c, g in zip(carry, grads))), None)
    start = (jnp.zeros((W, W), jnp.float32), jnp.zeros((W, W), jnp.float32), jnp.zeros((W, W), jnp.float32), jnp.zeros((W, V), jnp.float32))
    totals, _ = lax.scan(grad_step, start, jnp.arange(parts))
    return (totals[0], totals[1], totals[2], totals[3], loss)
```

```python
import functools

import jax
import jax.numpy as jnp
from jax import lax
from jax.experimental import pallas as pl
from jax.experimental.pallas import tpu as pltpu
from jax.sharding import PartitionSpec as P

EPS = 0.04
F32 = jnp.float32
BF16 = jnp.bfloat16
VMEM_BYTES = 56 * 1024 * 1024


def dot(a, b, ca=1, cb=0):
    return lax.dot_general(a, b, (((ca,), (cb,)), ((), ())), preferred_element_type=F32)


def dot_nt(a, b):
    return dot(a, b, 1, 1)


def one_hot(rows, index_row):
    shape = (rows, index_row.shape[1])
    hit = lax.broadcasted_iota(jnp.int32, shape, 0) == index_row
    return jnp.where(hit, 1.0, 0.0).astype(BF16)


def params(**kw):
    return pltpu.CompilerParams(vmem_limit_bytes=VMEM_BYTES, **kw)


def vmem(n):
    return [pl.BlockSpec(memory_space=pltpu.VMEM)] * n


def cost(flops, size):
    return pl.CostEstimate(flops=int(flops), bytes_accessed=int(size), transcendentals=0)


def sds(shape, dtype):
    return jax.ShapeDtypeStruct(shape, dtype)


def lend_kernel(nodes, to_next, to_prev, nodes_t, next_t, prev_t):
    table = nodes[...].T
    nodes_t[...] = table
    count = table.shape[1]
    next_t[...] = dot(table, one_hot(count, to_next[...])).astype(BF16)
    prev_t[...] = dot(table, one_hot(count, to_prev[...])).astype(BF16)


def prepare_kernel(
    w_send, w_recv, vertex, w_decode, nodes_t, vertices, weights, base, truth,
    w_send_t, vertex_t, w_decode_t, recv_t, mat_hi, mat_lo, base_t, truth_t,
):
    @pl.when(pl.program_id(0) == 0)
    def _():
        w_send_t[...] = w_send[...].T
        vertex_t[...] = vertex[...].T
        w_decode_t[...] = w_decode[...].T
        recv_t[...] = dot(w_recv[...].T, nodes_t[...])

    shape = mat_hi.shape
    row = lax.broadcasted_iota(jnp.int32, shape, 0)
    mat = jnp.zeros(shape, F32)
    for k in range(vertices.shape[0]):
        mat += jnp.where(row == vertices[k : k + 1, :], weights[k : k + 1, :], 0.0)
    hi = mat.astype(BF16)
    mat_hi[...] = hi
    mat_lo[...] = (mat - hi.astype(F32)).astype(BF16)
    base_t[...] = base[...].T
    truth_t[...] = truth[...].T


def forward_kernel(
    nodes_t, from_prev, from_next, senders, w_send_t, recv_t, vertex_t, w_decode_t, to_next, to_prev,
    picked_t, slope_t, slope_sum_t, agg_t, upd_slope_t, hidden_t, field_t, next_t, prev_t,
):
    degree, count = senders.shape
    halo = from_prev.shape[1]
    ext = jnp.concatenate([nodes_t[...], from_prev[...], from_next[...]], axis=1)
    total = jnp.zeros(recv_t.shape, F32)
    slopes = jnp.zeros(recv_t.shape, F32)
    for k in range(degree):
        picked = dot(ext, one_hot(count + 2 * halo, senders[k : k + 1, :])).astype(BF16)
        picked_t[k] = picked
        pre = dot(w_send_t[...], picked) + recv_t[...]
        sigma = 0.5 * jnp.tanh(0.5 * pre) + 0.5
        value = pre * sigma
        total += value
        slope = sigma * (1.0 + (pre - value)) * (1.0 / degree)
        slopes += slope
        slope_t[k] = slope.astype(slope_t.dtype)
    slope_sum_t[...] = slopes
    agg = (total * (1.0 / degree)).astype(BF16)
    agg_t[...] = agg
    upd = dot(vertex_t[...], agg)
    sigma = 0.5 * jnp.tanh(0.5 * upd) + 0.5
    value = upd * sigma
    upd_slope_t[...] = sigma * (1.0 + (upd - value))
    hidden = (nodes_t[...].astype(F32) + value).astype(BF16)
    hidden_t[...] = hidden
    field = dot(w_decode_t[...], hidden).astype(BF16)
    field_t[...] = field
    next_t[...] = dot(field, one_hot(count, to_next[...])).astype(BF16)
    prev_t[...] = dot(field, one_hot(count, to_prev[...])).astype(BF16)


def readout_kernel(line_span, own_index, fields, mat_hi, mat_lo, base_t, truth_t, grad_t, loss, states):
    step = pl.program_id(0)
    members = states.shape[0]
    variables = base_t.shape[0]

    @pl.when(step == 0)
    def _():
        grad_t[...] = jnp.zeros_like(grad_t)
        loss[...] = jnp.zeros_like(loss)

    ready = base_t[...].astype(F32)
    for m in range(members):
        table = fields[m * variables : (m + 1) * variables, :]
        x = ready + (dot(table, mat_hi[...]) + dot(table, mat_lo[...]))
        states[m] = x.astype(BF16).astype(F32)
    own = states[own_index[0]]
    diff = own - truth_t[...].astype(F32)
    square = diff * diff + EPS
    inverse = lax.rsqrt(square)
    term = square * inverse * (1.0 / members)
    slope = diff * inverse * (1.0 / members)
    spread = jnp.zeros_like(term)
    push = jnp.zeros_like(term)
    for m in range(members):
        diff = own - states[m]
        square = diff * diff + EPS
        inverse = lax.rsqrt(square)
        spread += square * inverse
        push += diff * inverse
    term = term - spread * (1.0 / (2.0 * members * (members - 1)))
    slope = (slope - push * (1.0 / (members * (members - 1.0)))) * (1.0 / line_span)
    grad_t[...] += dot_nt(slope.astype(BF16), mat_hi[...])
    loss[...] += jnp.sum(term.reshape(-1, 8, term.shape[1]), axis=0)


def split(value):
    hi = value.astype(BF16)
    return hi, (value - hi.astype(F32)).astype(BF16)


def backward_kernel(
    half, grad_ext_t, from_next, from_prev, to_next, to_prev, w_decode, vertex, nodes_t, picked_t,
    slope_t, slope_sum_t, agg_t, upd_slope_t, hidden_t,
    keep, send, whole,
):
    count = nodes_t.shape[1]
    width = nodes_t.shape[0]
    grad_z = grad_ext_t[:, :count]
    for got, rows in ((from_next, to_next), (from_prev, to_prev)):
        place = one_hot(count, rows[...])
        hi, lo = split(got[...])
        grad_z += dot_nt(hi, place) + dot_nt(lo, place)
    grad_z = grad_z.astype(BF16)
    whole[:, 3 * width :] = dot_nt(hidden_t[...], grad_z)
    grad_upd = (dot(w_decode[...], grad_z) * upd_slope_t[...]).astype(BF16)
    whole[:, 2 * width : 3 * width] = dot_nt(agg_t[...], grad_upd)
    grad_agg = dot(vertex[...], grad_upd)
    grad_recv = (grad_agg * slope_sum_t[...]).astype(BF16)
    whole[:, width : 2 * width] = dot_nt(nodes_t[...], grad_recv)
    total = jnp.zeros((width, width), F32)
    for k in range(picked_t.shape[0]):
        grad_pre = (grad_agg * slope_t[k].astype(F32)).astype(BF16)
        total += dot_nt(picked_t[k], grad_pre)
    whole[:, :width] = total
    rows = keep.shape[0]
    keep[...] = whole[pl.ds(pl.multiple_of(half[0] * rows, rows), rows), :]
    send[...] = whole[pl.ds(pl.multiple_of((1 - half[0]) * rows, rows), rows), :].astype(BF16)


def halve_kernel(half, mine, got, keep, send, total):
    total[...] = mine[...] + got[...].astype(F32)
    rows = keep.shape[0]
    keep[...] = total[pl.ds(pl.multiple_of(half[0] * rows, rows), rows), :]
    send[...] = total[pl.ds(pl.multiple_of((1 - half[0]) * rows, rows), rows), :].astype(BF16)


def shares_kernel(here, mine, got, *outs):
    total = outs[-1]
    total[...] = mine[...] + got[...].astype(F32)
    parts = len(outs) - 1
    rows = outs[0].shape[0]
    for k in range(parts):
        place = lax.rem(here[0] + k, parts)
        block = total[pl.ds(pl.multiple_of(place * rows, rows), rows), :]
        outs[k][...] = block.astype(outs[k].dtype)


def sum_kernel(*refs):
    total = refs[0][...]
    for ref in refs[1:-1]:
        total += ref[...].astype(F32)
    refs[-1][...] = total.astype(BF16)


def line_up_kernel(here, *refs):
    out = refs[-1]
    parts = len(refs) - 1
    rows = refs[0].shape[0]
    for k in range(parts):
        place = lax.rem(here[0] + (parts - k), parts)
        out[pl.ds(pl.multiple_of(place * rows, rows), rows), :] = refs[k][...]


def finish_kernel(order, p0, p1, p2, p3, g_send, g_recv, g_update, g_decode):
    rows, width = p0.shape[0], g_send.shape[1]
    for k, piece in enumerate((p0, p1, p2, p3)):
        place = pl.ds(pl.multiple_of(order[k] * rows, rows), rows)
        g_send[place, :] = piece[:, :width].astype(F32)
        g_recv[place, :] = piece[:, width : 2 * width].astype(F32)
        g_update[place, :] = piece[:, 2 * width : 3 * width].astype(F32)
        g_decode[place, :] = piece[:, 3 * width :].astype(F32)


SCALAR = pl.BlockSpec(memory_space=pltpu.SMEM)


def along(value, axis, steps):
    size = lax.axis_size(axis)
    return lax.ppermute(value, axis, [(i, (i + steps) % size) for i in range(size)])


def flip(value, axis, bit):
    size = lax.axis_size(axis)
    return lax.ppermute(value, axis, [(i, i ^ bit) for i in range(size)])


def call(kernel, ins, outs, scratch=(), flops=0, scalars=0):
    size = sum(x.size * x.dtype.itemsize for x in list(ins) + list(outs))
    many = isinstance(outs, (list, tuple))
    return pl.pallas_call(
        kernel,
        out_shape=outs,
        in_specs=[SCALAR] * scalars + vmem(len(ins) - scalars),
        out_specs=vmem(len(outs)),
        scratch_shapes=list(scratch),
        compiler_params=params(),
        cost_estimate=cost(flops, size),
    )(*ins)


def scalar(value):
    return jnp.reshape(value, (1,)).astype(jnp.int32)


def spread(quarter):
    across = flip(quarter, "ens", 2)
    beside = flip(quarter, "ens", 1)
    corner = flip(across, "ens", 1)
    return quarter, across, beside, corner


def reduced(keep, send, ens, dom):
    parts = lax.axis_size("dom")
    rows, cols = keep.shape
    got = flip(send, "ens", 1)
    keep, send = call(
        halve_kernel,
        [scalar(ens // 2), keep, got],
        [sds((rows // 2, cols), F32), sds((rows // 2, cols), BF16)],
        [pltpu.VMEM((rows, cols), F32)],
        scalars=1,
    )
    rows //= 2
    got = flip(send, "ens", 2)
    share = rows // parts
    if share % 16:
        quarter = lax.psum(keep + got.astype(F32), "dom").astype(BF16)
        return spread(quarter)
    shares = call(
        shares_kernel,
        [scalar(dom), keep, got],
        [sds((share, cols), F32)] + [sds((share, cols), BF16)] * (parts - 1),
        [pltpu.VMEM((rows, cols), F32)],
        scalars=1,
    )
    terms = [shares[0]] + [along(shares[k], "dom", k) for k in range(1, parts)]
    (own,) = call(sum_kernel, terms, [sds((share, cols), BF16)])
    pieces = [own] + [along(own, "dom", k) for k in range(1, parts)]
    (quarter,) = call(line_up_kernel, [scalar(dom)] + pieces, [sds((rows, cols), BF16)], scalars=1)
    return spread(quarter)


def per_device(
    nodes, senders, send_next, send_prev, readout_vertex_list, dec_weights, base, observed_analysis,
    w_send, w_recv, vertex_refresh_matrix, w_decode,
):
    latent = nodes[0]
    count, width = latent.shape
    halo = send_next.shape[0]
    line_span, variables = base.shape
    degree = senders.shape[0]
    fan = readout_vertex_list.shape[0]
    ext_rows = count + 2 * halo
    members = lax.axis_size("ens")
    ens, dom = lax.axis_index("ens"), lax.axis_index("dom")
    to_next, to_prev = send_next.reshape(1, halo), send_prev.reshape(1, halo)

    nodes_t, next_t, prev_t = call(
        lend_kernel,
        [latent, to_next, to_prev],
        [sds((width, count), BF16), sds((width, halo), BF16), sds((width, halo), BF16)],
        flops=4 * width * count * halo,
    )
    lat_prev = along(next_t, "dom", 1)
    lat_next = along(prev_t, "dom", -1)

    block = 512
    steps = line_span // block
    fixed = lambda shape: pl.BlockSpec(shape, lambda i: (0,) * len(shape))
    tall = lambda rows: pl.BlockSpec((rows, block), lambda i: (0, i))
    flat = pl.BlockSpec((block, variables), lambda i: (i, 0))
    w_send_t, vertex_t, w_decode_t, recv_t, mat_hi, mat_lo, base_t, truth_t = pl.pallas_call(
        prepare_kernel,
        grid=(steps,),
        out_shape=[
            sds((width, width), BF16), sds((width, width), BF16), sds((variables, width), BF16),
            sds((width, count), F32), sds((ext_rows, line_span), BF16), sds((ext_rows, line_span), BF16),
            sds((variables, line_span), BF16), sds((variables, line_span), BF16),
        ],
        in_specs=[
            fixed((width, width)), fixed((width, width)), fixed((width, width)), fixed((width, variables)),
            fixed((width, count)), tall(fan), tall(fan), flat, flat,
        ],
        out_specs=[
            fixed((width, width)), fixed((width, width)), fixed((variables, width)), fixed((width, count)),
            tall(ext_rows), tall(ext_rows), tall(variables), tall(variables),
        ],
        compiler_params=params(),
        cost_estimate=cost(2 * width * width * count, 20e6),
    )(w_send, w_recv, vertex_refresh_matrix, w_decode, nodes_t, readout_vertex_list, dec_weights, base, observed_analysis)

    picked_t, slope_t, slope_sum_t, agg_t, upd_slope_t, hidden_t, field_t, next_t, prev_t = call(
        forward_kernel,
        [nodes_t, lat_prev, lat_next, senders, w_send_t, recv_t, vertex_t, w_decode_t, to_next, to_prev],
        [
            sds((degree, width, count), BF16), sds((degree, width, count), BF16), sds((width, count), F32),
            sds((width, count), BF16), sds((width, count), F32), sds((width, count), BF16),
            sds((variables, count), BF16), sds((variables, halo), BF16), sds((variables, halo), BF16),
        ],
        flops=2 * degree * width * count * (ext_rows + width),
    )
    field_ext = jnp.concatenate([field_t, along(next_t, "dom", 1), along(prev_t, "dom", -1)], axis=1)
    fields = lax.all_gather(field_ext, "ens", axis=0, tiled=True)

    grad_ext_t, term = pl.pallas_call(
        functools.partial(readout_kernel, line_span),
        grid=(steps,),
        out_shape=[sds((variables, ext_rows), F32), sds((8, block), F32)],
        in_specs=[
            SCALAR, fixed((members * variables, ext_rows)), tall(ext_rows), tall(ext_rows),
            tall(variables), tall(variables),
        ],
        out_specs=[fixed((variables, ext_rows)), fixed((8, block))],
        scratch_shapes=[pltpu.VMEM((members, variables, block), F32)],
        compiler_params=params(),
        cost_estimate=cost(4 * members * variables * ext_rows * line_span, 14e6),
    )(scalar(ens), fields, mat_hi, mat_lo, base_t, truth_t)

    got_next = along(grad_ext_t[:, count : count + halo], "dom", -1)
    got_prev = along(grad_ext_t[:, count + halo :], "dom", 1)
    losses = lax.all_gather(term[:, :128] + term[:, 128:256] + term[:, 256:384] + term[:, 384:], ("ens", "dom"), axis=0, tiled=True)
    loss = jnp.sum(losses) / line_span

    cols = 3 * width + variables
    keep, send = call(
        backward_kernel,
        [
            scalar(lax.rem(ens, 2)), grad_ext_t, got_next, got_prev, to_next, to_prev, w_decode, vertex_refresh_matrix,
            nodes_t, picked_t, slope_t, slope_sum_t, agg_t, upd_slope_t, hidden_t,
        ],
        [sds((width // 2, cols), F32), sds((width // 2, cols), BF16)],
        [pltpu.VMEM((width, cols), F32)],
        flops=2 * (degree + 3) * width * width * count,
        scalars=1,
    )
    pieces = reduced(keep, send, ens, dom)
    spot = 2 * lax.rem(ens, 2) + ens // 2
    order = jnp.stack([spot, spot ^ 1, spot ^ 2, spot ^ 3]).astype(jnp.int32)
    g_send, g_recv, g_update, g_decode = call(
        finish_kernel,
        [order] + list(pieces),
        [sds((width, width), F32)] * 3 + [sds((width, variables), F32)],
        scalars=1,
    )
    return g_send, g_recv, g_update, g_decode, loss


def solution(mesh):
    return jax.shard_map(
        per_device,
        mesh=mesh,
        in_specs=(
            P("ens", "dom", None), P(None, "dom"), P("dom"), P("dom"), P(None, "dom"), P(None, "dom"),
            P("dom", None), P("dom", None), P(), P(), P(), P(),
        ),
        out_specs=(P(), P(), P(), P(), P()),
        check_vma=False,
    )
```

```python
import functools

import jax
import jax.numpy as jnp
from jax import lax
from jax.experimental import pallas as pl
from jax.experimental.pallas import tpu as pltpu
from jax.sharding import PartitionSpec as P

EPS = 0.04
F32 = jnp.float32
BF16 = jnp.bfloat16
VMEM_BYTES = 56 * 1024 * 1024


def dot(a, b, ca=1, cb=0):
    return lax.dot_general(a, b, (((ca,), (cb,)), ((), ())), preferred_element_type=F32)


def dot_nt(a, b):
    return dot(a, b, 1, 1)


def one_hot(rows, index_row):
    shape = (rows, index_row.shape[1])
    hit = lax.broadcasted_iota(jnp.int32, shape, 0) == index_row
    return jnp.where(hit, 1.0, 0.0).astype(BF16)


def params(**kw):
    return pltpu.CompilerParams(vmem_limit_bytes=VMEM_BYTES, **kw)


def vmem(n):
    return [pl.BlockSpec(memory_space=pltpu.VMEM)] * n


def cost(flops, size):
    return pl.CostEstimate(flops=int(flops), bytes_accessed=int(size), transcendentals=0)


def sds(shape, dtype):
    return jax.ShapeDtypeStruct(shape, dtype)


def lend_kernel(nodes, to_next, to_prev, nodes_t, next_t, prev_t):
    table = nodes[...].T
    nodes_t[...] = table
    count = table.shape[1]
    next_t[...] = dot(table, one_hot(count, to_next[...])).astype(BF16)
    prev_t[...] = dot(table, one_hot(count, to_prev[...])).astype(BF16)


def weights_kernel(w_send, w_recv, vertex, w_decode, nodes_t, w_send_t, vertex_t, w_decode_t, recv_t):
    w_send_t[...] = w_send[...].T
    vertex_t[...] = vertex[...].T
    w_decode_t[...] = w_decode[...].T
    recv_t[...] = dot(w_recv[...].T, nodes_t[...])


def decoder_kernel(core, vertices, weights, base, truth, after, mat_hi, mat_lo, base_t, truth_t):
    del core, after
    shape = mat_hi.shape
    row = lax.broadcasted_iota(jnp.int32, shape, 0)
    mat = jnp.zeros(shape, F32)
    for k in range(vertices.shape[0]):
        mat += jnp.where(row == vertices[k : k + 1, :], weights[k : k + 1, :], 0.0)
    mat_hi[...], mat_lo[...] = split(mat)
    base_t[...] = base[...].T
    truth_t[...] = truth[...].T


def forward_kernel(
    nodes_t, from_prev, from_next, senders, w_send_t, recv_t, vertex_t, w_decode_t, to_next, to_prev,
    picked_t, slope_t, slope_sum_t, agg_t, upd_slope_t, hidden_t, field_t, next_t, prev_t,
):
    degree, count = senders.shape
    halo = from_prev.shape[1]
    ext = jnp.concatenate([nodes_t[...], from_prev[...], from_next[...]], axis=1)
    total = jnp.zeros(recv_t.shape, F32)
    slopes = jnp.zeros(recv_t.shape, F32)
    for k in range(degree):
        picked = dot(ext, one_hot(count + 2 * halo, senders[k : k + 1, :])).astype(BF16)
        picked_t[k] = picked
        pre = dot(w_send_t[...], picked) + recv_t[...]
        sigma = 0.5 * jnp.tanh(0.5 * pre) + 0.5
        value = pre * sigma
        total += value
        slope = sigma * (1.0 + (pre - value)) * (1.0 / degree)
        slopes += slope
        slope_t[k] = slope.astype(slope_t.dtype)
    slope_sum_t[...] = slopes
    agg = (total * (1.0 / degree)).astype(BF16)
    agg_t[...] = agg
    upd = dot(vertex_t[...], agg)
    sigma = 0.5 * jnp.tanh(0.5 * upd) + 0.5
    value = upd * sigma
    upd_slope_t[...] = sigma * (1.0 + (upd - value))
    hidden = (nodes_t[...].astype(F32) + value).astype(BF16)
    hidden_t[...] = hidden
    field = dot(w_decode_t[...], hidden).astype(BF16)
    field_t[...] = field
    next_t[...] = dot(field, one_hot(count, to_next[...])).astype(BF16)
    prev_t[...] = dot(field, one_hot(count, to_prev[...])).astype(BF16)


def readout_kernel(line_span, *refs):
    mids, ends = refs[0:4], refs[4:8]
    mat_hi, mat_lo, base_t, truth_t = refs[8:12]
    own_mid, own_next, own_prev, pair_mid, pair_next, pair_prev, loss = refs[12:19]
    table, grad = refs[19:21]
    step = pl.program_id(0)
    members = len(mids)
    variables, count = own_mid.shape
    halo = own_next.shape[1]

    @pl.when(step == 0)
    def _():
        grad[...] = jnp.zeros_like(grad)
        loss[...] = jnp.zeros_like(loss)
        for m in range(members):
            table[m * variables : (m + 1) * variables, :count] = mids[m][...]
            table[m * variables : (m + 1) * variables, count:] = ends[m][...]

    ready = base_t[...].astype(F32)
    states = []
    for m in range(members):
        one = table[m * variables : (m + 1) * variables, :]
        x = ready + (dot(one, mat_hi[...]) + dot(one, mat_lo[...]))
        states.append(x.astype(BF16).astype(F32))
    truth = truth_t[...].astype(F32)

    def bend(diff):
        square = diff * diff + EPS
        inverse = lax.rsqrt(square)
        return square * inverse, diff * inverse

    sizes = {}
    for i in range(2):
        for j in range(i + 1, members):
            sizes[i, j] = bend(states[i] - states[j])
    alone = EPS**0.5
    total = jnp.zeros_like(truth)
    slopes = []
    for i in range(2):
        near, push = bend(states[i] - truth)
        apart, pull = alone, 0.0
        for j in range(members):
            if j != i:
                size, slope = sizes[min(i, j), max(i, j)]
                apart = apart + size
                pull = pull + slope if i < j else pull - slope
        total += near * (1.0 / members) - apart * (1.0 / (2.0 * members * (members - 1)))
        slope = push * (1.0 / members) - pull * (1.0 / (members * (members - 1.0)))
        slopes.append((slope * (1.0 / line_span)).astype(BF16))
    grad[...] += dot_nt(jnp.concatenate(slopes, axis=0), mat_hi[...])
    loss[...] += jnp.sum(total.reshape(-1, 8, total.shape[1]), axis=0)

    @pl.when(step == pl.num_programs(0) - 1)
    def _():
        for i, (mid, after, before) in enumerate(((own_mid, own_next, own_prev), (pair_mid, pair_next, pair_prev))):
            rows = slice(i * variables, (i + 1) * variables)
            mid[...] = grad[rows, :count]
            after[...] = grad[rows, count : count + halo]
            before[...] = grad[rows, count + halo :]


def split(value):
    hi = value.astype(BF16)
    return hi, (value - hi.astype(F32)).astype(BF16)


LANES = 128


def encoded(total):
    tile = total[:, -LANES:]
    value = tile + pltpu.roll(tile, LANES // 2, 1)
    hi = value.astype(BF16).astype(F32)
    lane = lax.broadcasted_iota(jnp.int32, tile.shape, 1)
    tile = jnp.where(lane < LANES // 2, hi, value - hi)
    return jnp.concatenate([total[:, :-LANES].astype(BF16), tile.astype(BF16)], axis=1)


def backward_kernel(
    half, own_mid, pair_mid, next_a, next_b, prev_a, prev_b, to_next, to_prev, term, w_decode, vertex, nodes_t,
    picked_t, slope_t, slope_sum_t, agg_t, upd_slope_t, hidden_t,
    keep, send, whole,
):
    count = nodes_t.shape[1]
    width = nodes_t.shape[0]
    grad_z = own_mid[...] + pair_mid[...]
    for got, rows in ((next_a[...] + next_b[...], to_next), (prev_a[...] + prev_b[...], to_prev)):
        place = one_hot(count, rows[...])
        hi, lo = split(got)
        grad_z += dot_nt(hi, place) + dot_nt(lo, place)
    grad_z = grad_z.astype(BF16)
    main = whole.shape[1] - LANES
    whole[:, 3 * width : main] = dot_nt(hidden_t[...], grad_z)
    grad_upd = (dot(w_decode[...], grad_z) * upd_slope_t[...]).astype(BF16)
    whole[:, 2 * width : 3 * width] = dot_nt(agg_t[...], grad_upd)
    grad_agg = dot(vertex[...], grad_upd)
    grad_recv = (grad_agg * slope_sum_t[...]).astype(BF16)
    whole[:, width : 2 * width] = dot_nt(nodes_t[...], grad_recv)
    total = jnp.zeros((width, width), F32)
    for k in range(picked_t.shape[0]):
        grad_pre = (grad_agg * slope_t[k].astype(F32)).astype(BF16)
        total += dot_nt(picked_t[k], grad_pre)
    whole[:, :width] = total
    whole[:, main:] = jnp.zeros((width, LANES), F32)
    spot = (lax.broadcasted_iota(jnp.int32, (8, LANES), 0) == 0) & (lax.broadcasted_iota(jnp.int32, (8, LANES), 1) == 0)
    whole[0:8, main:] = jnp.where(spot, jnp.sum(term[...]), 0.0)
    rows = keep.shape[0]
    keep[...] = whole[pl.ds(pl.multiple_of(half[0] * rows, rows), rows), :]
    send[...] = encoded(whole[pl.ds(pl.multiple_of((1 - half[0]) * rows, rows), rows), :])


def halve_kernel(half, mine, got, keep, send, total):
    total[...] = mine[...] + got[...].astype(F32)
    rows = keep.shape[0]
    keep[...] = total[pl.ds(pl.multiple_of(half[0] * rows, rows), rows), :]
    send[...] = encoded(total[pl.ds(pl.multiple_of((1 - half[0]) * rows, rows), rows), :])


def shares_kernel(here, mine, got, *outs):
    total = outs[-1]
    total[...] = mine[...] + got[...].astype(F32)
    parts = len(outs) - 1
    rows = outs[0].shape[0]
    for k in range(parts):
        place = lax.rem(here[0] + k, parts)
        block = total[pl.ds(pl.multiple_of(place * rows, rows), rows), :]
        outs[k][...] = encoded(block) if k else block


def sum_kernel(*refs):
    total = refs[0][...]
    for ref in refs[1:-1]:
        total += ref[...].astype(F32)
    refs[-1][...] = encoded(total)


def line_up_kernel(here, *refs):
    out = refs[-1]
    parts = len(refs) - 1
    rows = refs[0].shape[0]
    for k in range(parts):
        place = lax.rem(here[0] + (parts - k), parts)
        out[pl.ds(pl.multiple_of(place * rows, rows), rows), :] = refs[k][...]


def finish_kernel(scale, place, piece, *refs):
    g_send, g_recv, g_update, g_decode, loss = refs[-5:]
    width = g_send.shape[1]
    g_send[...] = piece[:, :width].astype(F32)
    g_recv[...] = piece[:, width : 2 * width].astype(F32)
    g_update[...] = piece[:, 2 * width : 3 * width].astype(F32)
    g_decode[...] = piece[:, 3 * width : -LANES].astype(F32)
    part = jnp.sum(piece[:, -LANES:].astype(F32)) * scale
    loss[0, 0] = part if len(refs) == 5 else refs[4][0, 0] + part


def finish(piece, place, shapes, scale, before=()):
    rows = piece.shape[0]
    block = lambda shape: pl.BlockSpec((rows, shape.shape[1]), lambda i, at: (at[0], 0))
    cell = pl.BlockSpec(memory_space=pltpu.SMEM)
    whole = pl.BlockSpec(memory_space=pl.ANY)
    return pl.pallas_call(
        functools.partial(finish_kernel, scale),
        grid_spec=pltpu.PrefetchScalarGridSpec(
            num_scalar_prefetch=1,
            grid=(1,),
            in_specs=[pl.BlockSpec(piece.shape, lambda i, at: (0, 0))] + ([whole] * 4 + [cell] if before else []),
            out_specs=[block(s) for s in shapes] + [cell],
        ),
        out_shape=list(shapes) + [sds((1, 1), F32)],
        input_output_aliases={2 + i: i for i in range(4)} if before else {},
        compiler_params=params(),
        cost_estimate=cost(0, 6 * piece.size),
    )(scalar(place), piece, *before)


SCALAR = pl.BlockSpec(memory_space=pltpu.SMEM)


def crossed(value, bit, steps):
    ens, dom = lax.axis_size("ens"), lax.axis_size("dom")
    pairs = [(e * dom + d, (e ^ bit) * dom + (d + steps) % dom) for e in range(ens) for d in range(dom)]
    return lax.ppermute(value, ("ens", "dom"), pairs)


def along(value, axis, steps):
    size = lax.axis_size(axis)
    return lax.ppermute(value, axis, [(i, (i + steps) % size) for i in range(size)])


def flip(value, axis, bit):
    size = lax.axis_size(axis)
    return lax.ppermute(value, axis, [(i, i ^ bit) for i in range(size)])


def call(kernel, ins, outs, scratch=(), flops=0, scalars=0):
    size = sum(x.size * x.dtype.itemsize for x in list(ins) + list(outs))
    many = isinstance(outs, (list, tuple))
    return pl.pallas_call(
        kernel,
        out_shape=outs,
        in_specs=[SCALAR] * scalars + vmem(len(ins) - scalars),
        out_specs=vmem(len(outs)),
        scratch_shapes=list(scratch),
        compiler_params=params(),
        cost_estimate=cost(flops, size),
    )(*ins)


def scalar(value):
    return jnp.reshape(value, (1,)).astype(jnp.int32)


def reduced(keep, send, ens, dom):
    parts = lax.axis_size("dom")
    rows, cols = keep.shape
    got = flip(send, "ens", 1)
    keep, send = call(
        halve_kernel,
        [scalar(ens // 2), keep, got],
        [sds((rows // 2, cols), F32), sds((rows // 2, cols), BF16)],
        [pltpu.VMEM((rows, cols), F32)],
        scalars=1,
    )
    rows //= 2
    got = flip(send, "ens", 2)
    share = rows // parts
    if share % 16:
        total = lax.psum(keep + got.astype(F32), "dom")
        return call(sum_kernel, [total], [sds((rows, cols), BF16)])[0]
    shares = call(
        shares_kernel,
        [scalar(dom), keep, got],
        [sds((share, cols), F32)] + [sds((share, cols), BF16)] * (parts - 1),
        [pltpu.VMEM((rows, cols), F32)],
        scalars=1,
    )
    terms = [shares[0]] + [along(shares[k], "dom", k) for k in range(1, parts)]
    (own,) = call(sum_kernel, terms, [sds((share, cols), BF16)])
    pieces = [own] + [along(own, "dom", k) for k in range(1, parts)]
    (quarter,) = call(line_up_kernel, [scalar(dom)] + pieces, [sds((rows, cols), BF16)], scalars=1)
    return quarter


def per_device(
    nodes, senders, send_next, send_prev, readout_vertex_list, dec_weights, base, observed_analysis,
    w_send, w_recv, vertex_refresh_matrix, w_decode,
):
    latent = nodes[0]
    count, width = latent.shape
    halo = send_next.shape[0]
    line_span, variables = base.shape
    degree = senders.shape[0]
    fan = readout_vertex_list.shape[0]
    ext_rows = count + 2 * halo
    members = lax.axis_size("ens")
    ens, dom = lax.axis_index("ens"), lax.axis_index("dom")
    to_next, to_prev = send_next.reshape(1, halo), send_prev.reshape(1, halo)

    nodes_t, next_t, prev_t = call(
        lend_kernel,
        [latent, to_next, to_prev],
        [sds((width, count), BF16), sds((width, halo), BF16), sds((width, halo), BF16)],
        flops=4 * width * count * halo,
    )
    lat_prev = along(next_t, "dom", 1)
    lat_next = along(prev_t, "dom", -1)

    core = scalar(lax.rem(ens, 2))
    w_send_t, vertex_t, w_decode_t, recv_t = call(
        weights_kernel,
        [w_send, w_recv, vertex_refresh_matrix, w_decode, nodes_t],
        [sds((width, width), BF16), sds((width, width), BF16), sds((variables, width), BF16), sds((width, count), F32)],
        flops=2 * width * width * count,
    )

    picked_t, slope_t, slope_sum_t, agg_t, upd_slope_t, hidden_t, field_t, next_t, prev_t = call(
        forward_kernel,
        [nodes_t, lat_prev, lat_next, senders, w_send_t, recv_t, vertex_t, w_decode_t, to_next, to_prev],
        [
            sds((degree, width, count), BF16), sds((degree, width, count), BF16), sds((width, count), F32),
            sds((width, count), BF16), sds((width, count), F32), sds((width, count), BF16),
            sds((variables, count), BF16), sds((variables, halo), BF16), sds((variables, halo), BF16),
        ],
        flops=2 * degree * width * count * (ext_rows + width),
    )
    lent = (along(next_t, "dom", 1), along(prev_t, "dom", -1))
    mids = [field_t] + [flip(field_t, "ens", m) for m in range(1, members)]

    block = 512
    steps = line_span // 2 // block
    fixed = lambda shape: pl.BlockSpec(shape, lambda i, *at: (0,) * len(shape))
    tall = lambda rows: pl.BlockSpec((rows, block), lambda i, *at: (0, i))
    tall_half = lambda rows: pl.BlockSpec((rows, block), lambda i, at: (0, i + at[0] * steps))
    flat_half = pl.BlockSpec((block, variables), lambda i, at: (i + at[0] * steps, 0))
    half_span = line_span // 2
    mat_hi, mat_lo, base_t, truth_t = pl.pallas_call(
        decoder_kernel,
        grid_spec=pltpu.PrefetchScalarGridSpec(
            num_scalar_prefetch=1,
            grid=(steps,),
            in_specs=[tall_half(fan), tall_half(fan), flat_half, flat_half, pl.BlockSpec(memory_space=pl.ANY)],
            out_specs=[tall(ext_rows), tall(ext_rows), tall(variables), tall(variables)],
        ),
        out_shape=[sds((ext_rows, half_span), BF16)] * 2 + [sds((variables, half_span), BF16)] * 2,
        compiler_params=params(),
        cost_estimate=cost(10 * ext_rows * half_span, 16e6),
    )(core, readout_vertex_list, dec_weights, base, observed_analysis, field_t)

    end = jnp.concatenate(lent, axis=1)
    ends = [end] + [flip(end, "ens", m) for m in range(1, members)]

    grads = pl.pallas_call(
        functools.partial(readout_kernel, line_span),
        grid=(steps,),
        out_shape=[sds((variables, count), F32), sds((variables, halo), F32), sds((variables, halo), F32)] * 2 + [sds((8, block), F32)],
        in_specs=[fixed((variables, count))] * members + [fixed((variables, 2 * halo))] * members + [
            tall(ext_rows), tall(ext_rows), tall(variables), tall(variables),
        ],
        out_specs=[fixed((variables, count)), fixed((variables, halo)), fixed((variables, halo))] * 2 + [fixed((8, block))],
        scratch_shapes=[pltpu.VMEM((members * variables, ext_rows), BF16), pltpu.VMEM((2 * variables, ext_rows), F32)],
        compiler_params=params(),
        cost_estimate=cost(4 * members * variables * ext_rows * half_span, 14e6),
    )(*mids, *ends, mat_hi, mat_lo, base_t, truth_t)
    own_mid, own_next, own_prev, pair_mid, pair_next, pair_prev, term = grads
    next_a, prev_a = along(own_next, "dom", -1), along(own_prev, "dom", 1)
    next_b, prev_b = crossed(pair_next, 1, -1), crossed(pair_prev, 1, 1)
    pair_mid = flip(pair_mid, "ens", 1)

    cols = 3 * width + variables + LANES
    keep, send = call(
        backward_kernel,
        [
            core, own_mid, pair_mid, next_a, next_b, prev_a, prev_b, to_next, to_prev, term, w_decode,
            vertex_refresh_matrix, nodes_t, picked_t, slope_t, slope_sum_t, agg_t, upd_slope_t, hidden_t,
        ],
        [sds((width // 2, cols), F32), sds((width // 2, cols), BF16)],
        [pltpu.VMEM((width, cols), F32)],
        flops=2 * (degree + 3) * width * width * count,
        scalars=1,
    )
    quarter = reduced(keep, send, ens, dom)
    across = flip(quarter, "ens", 2)
    beside = flip(quarter, "ens", 1)
    corner = flip(across, "ens", 1)
    spot = 2 * lax.rem(ens, 2) + ens // 2
    shapes = [sds((width, width), F32)] * 3 + [sds((width, variables), F32)]
    scale = 1.0 / line_span
    outs = finish(quarter, spot, shapes, scale)
    outs = finish(beside, spot ^ 2, shapes, scale, outs)
    outs = finish(across, spot ^ 1, shapes, scale, outs)
    g_send, g_recv, g_update, g_decode, loss = finish(corner, spot ^ 3, shapes, scale, outs)
    return g_send, g_recv, g_update, g_decode, loss[0, 0]


def solution(mesh):
    return jax.shard_map(
        per_device,
        mesh=mesh,
        in_specs=(
            P("ens", "dom", None), P(None, "dom"), P("dom"), P("dom"), P(None, "dom"), P(None, "dom"),
            P("dom", None), P("dom", None), P(), P(), P(), P(),
        ),
        out_specs=(P(), P(), P(), P(), P()),
        check_vma=False,
    )
```

```python
import functools

import jax
import jax.numpy as jnp
from jax import lax
from jax.experimental import pallas as pl
from jax.experimental.pallas import tpu as pltpu
from jax.sharding import PartitionSpec as P

EPS = 0.04
F32 = jnp.float32
BF16 = jnp.bfloat16
VMEM_BYTES = 56 * 1024 * 1024


def dot(a, b, ca=1, cb=0):
    return lax.dot_general(a, b, (((ca,), (cb,)), ((), ())), preferred_element_type=F32)


def dot_nt(a, b):
    return dot(a, b, 1, 1)


def one_hot(rows, index_row):
    shape = (rows, index_row.shape[1])
    hit = lax.broadcasted_iota(jnp.int32, shape, 0) == index_row
    return jnp.where(hit, 1.0, 0.0).astype(BF16)


def params(**kw):
    return pltpu.CompilerParams(vmem_limit_bytes=VMEM_BYTES, **kw)


def vmem(n):
    return [pl.BlockSpec(memory_space=pltpu.VMEM)] * n


def cost(flops, size):
    return pl.CostEstimate(flops=int(flops), bytes_accessed=int(size), transcendentals=0)


def sds(shape, dtype):
    return jax.ShapeDtypeStruct(shape, dtype)


def lend_kernel(nodes, to_next, to_prev, nodes_t, next_t, prev_t):
    table = nodes[...].T
    nodes_t[...] = table
    count = table.shape[1]
    next_t[...] = dot(table, one_hot(count, to_next[...])).astype(BF16)
    prev_t[...] = dot(table, one_hot(count, to_prev[...])).astype(BF16)


def weights_kernel(w_send, w_recv, vertex, w_decode, nodes_t, w_send_t, vertex_t, w_decode_t, recv_t):
    w_send_t[...] = w_send[...].T
    vertex_t[...] = vertex[...].T
    w_decode_t[...] = w_decode[...].T
    recv_t[...] = dot(w_recv[...].T, nodes_t[...])


def decoder_kernel(core, vertices, weights, base, truth, after, mat_hi, mat_lo, base_t, truth_t):
    del core, after
    shape = mat_hi.shape
    row = lax.broadcasted_iota(jnp.int32, shape, 0)
    mat = jnp.zeros(shape, F32)
    for k in range(vertices.shape[0]):
        mat += jnp.where(row == vertices[k : k + 1, :], weights[k : k + 1, :], 0.0)
    mat_hi[...], mat_lo[...] = split(mat)
    base_t[...] = base[...].T
    truth_t[...] = truth[...].T


def forward_kernel(
    nodes_t, from_prev, from_next, senders, w_send_t, recv_t, vertex_t, w_decode_t, to_next, to_prev,
    picked_t, slope_t, slope_sum_t, agg_t, upd_slope_t, hidden_t, field_t, next_t, prev_t,
):
    degree, count = senders.shape
    halo = from_prev.shape[1]
    ext = jnp.concatenate([nodes_t[...], from_prev[...], from_next[...]], axis=1)
    total = jnp.zeros(recv_t.shape, F32)
    slopes = jnp.zeros(recv_t.shape, F32)
    for k in range(degree):
        picked = dot(ext, one_hot(count + 2 * halo, senders[k : k + 1, :])).astype(BF16)
        picked_t[k] = picked
        pre = dot(w_send_t[...], picked) + recv_t[...]
        sigma = 0.5 * jnp.tanh(0.5 * pre) + 0.5
        value = pre * sigma
        total += value
        slope = sigma * (1.0 + (pre - value)) * (1.0 / degree)
        slopes += slope
        slope_t[k] = slope.astype(slope_t.dtype)
    slope_sum_t[...] = slopes
    agg = (total * (1.0 / degree)).astype(BF16)
    agg_t[...] = agg
    upd = dot(vertex_t[...], agg)
    sigma = 0.5 * jnp.tanh(0.5 * upd) + 0.5
    value = upd * sigma
    upd_slope_t[...] = sigma * (1.0 + (upd - value))
    hidden = (nodes_t[...].astype(F32) + value).astype(BF16)
    hidden_t[...] = hidden
    field = dot(w_decode_t[...], hidden).astype(BF16)
    field_t[...] = field
    next_t[...] = dot(field, one_hot(count, to_next[...])).astype(BF16)
    prev_t[...] = dot(field, one_hot(count, to_prev[...])).astype(BF16)


def readout_kernel(line_span, *refs):
    mids, ends = refs[0:4], refs[4:8]
    mat_hi, mat_lo, base_t, truth_t = refs[8:12]
    own_mid, own_end, pair_mid, pair_end, loss = refs[12:17]
    table, grad = refs[17:19]
    step = pl.program_id(0)
    members = len(mids)
    variables, count = own_mid.shape

    @pl.when(step == 0)
    def _():
        grad[...] = jnp.zeros_like(grad)
        loss[...] = jnp.zeros_like(loss)
        for m in range(members):
            table[m * variables : (m + 1) * variables, :count] = mids[m][...]
            table[m * variables : (m + 1) * variables, count:] = ends[m][...]

    ready = base_t[...].astype(F32)
    states = []
    for m in range(members):
        one = table[m * variables : (m + 1) * variables, :]
        x = ready + (dot(one, mat_hi[...]) + dot(one, mat_lo[...]))
        states.append(x.astype(BF16).astype(F32))
    truth = truth_t[...].astype(F32)

    def bend(diff):
        square = diff * diff + EPS
        inverse = lax.rsqrt(square)
        return square * inverse, diff * inverse

    sizes = {}
    for i in range(2):
        for j in range(i + 1, members):
            sizes[i, j] = bend(states[i] - states[j])
    alone = EPS**0.5
    total = jnp.zeros_like(truth)
    slopes = []
    for i in range(2):
        near, push = bend(states[i] - truth)
        apart, pull = alone, 0.0
        for j in range(members):
            if j != i:
                size, slope = sizes[min(i, j), max(i, j)]
                apart = apart + size
                pull = pull + slope if i < j else pull - slope
        total += near * (1.0 / members) - apart * (1.0 / (2.0 * members * (members - 1)))
        slope = push * (1.0 / members) - pull * (1.0 / (members * (members - 1.0)))
        slopes.append((slope * (1.0 / line_span)).astype(BF16))
    grad[...] += dot_nt(jnp.concatenate(slopes, axis=0), mat_hi[...])
    loss[...] += jnp.sum(total.reshape(-1, 8, total.shape[1]), axis=0)

    @pl.when(step == pl.num_programs(0) - 1)
    def _():
        for i, (mid, end) in enumerate(((own_mid, own_end), (pair_mid, pair_end))):
            rows = slice(i * variables, (i + 1) * variables)
            mid[...] = grad[rows, :count]
            end[...] = grad[rows, count:]


def ends_kernel(mine, got, after, before):
    halo = after.shape[1]
    total = mine[...] + got[...]
    after[...] = total[:, :halo]
    before[...] = total[:, halo:]


def split(value):
    hi = value.astype(BF16)
    return hi, (value - hi.astype(F32)).astype(BF16)


LANES = 128


def encoded(total):
    tile = total[:, -LANES:]
    value = tile + pltpu.roll(tile, LANES // 2, 1)
    hi = value.astype(BF16).astype(F32)
    lane = lax.broadcasted_iota(jnp.int32, tile.shape, 1)
    tile = jnp.where(lane < LANES // 2, hi, value - hi)
    return jnp.concatenate([total[:, :-LANES].astype(BF16), tile.astype(BF16)], axis=1)


def backward_kernel(
    parts, own_mid, pair_mid, from_next, from_prev, to_next, to_prev, term, w_decode, vertex, nodes_t,
    picked_t, slope_t, slope_sum_t, agg_t, upd_slope_t, hidden_t,
    keep, send_far, send_near, whole,
):
    count = nodes_t.shape[1]
    width = nodes_t.shape[0]
    grad_z = own_mid[...] + pair_mid[...]
    for got, rows in ((from_next[...], to_next), (from_prev[...], to_prev)):
        place = one_hot(count, rows[...])
        hi, lo = split(got)
        grad_z += dot_nt(hi, place) + dot_nt(lo, place)
    grad_z = grad_z.astype(BF16)
    main = whole.shape[1] - LANES
    whole[:, 3 * width : main] = dot_nt(hidden_t[...], grad_z)
    grad_upd = (dot(w_decode[...], grad_z) * upd_slope_t[...]).astype(BF16)
    whole[:, 2 * width : 3 * width] = dot_nt(agg_t[...], grad_upd)
    grad_agg = dot(vertex[...], grad_upd)
    grad_recv = (grad_agg * slope_sum_t[...]).astype(BF16)
    whole[:, width : 2 * width] = dot_nt(nodes_t[...], grad_recv)
    total = jnp.zeros((width, width), F32)
    for k in range(picked_t.shape[0]):
        grad_pre = (grad_agg * slope_t[k].astype(F32)).astype(BF16)
        total += dot_nt(picked_t[k], grad_pre)
    whole[:, :width] = total
    whole[:, main:] = jnp.zeros((width, LANES), F32)
    spot = (lax.broadcasted_iota(jnp.int32, (8, LANES), 0) == 0) & (lax.broadcasted_iota(jnp.int32, (8, LANES), 1) == 0)
    whole[0:8, main:] = jnp.where(spot, jnp.sum(term[...]), 0.0)
    ens, dom = lax.axis_index("ens"), lax.axis_index("dom")
    core, chip = lax.rem(ens, 2), lax.div(ens, 2)
    rows = send_far.shape[0]
    share = rows // parts

    def block(c, x, k):
        start = ((2 * c + x) * parts + lax.rem(dom + k, parts)) * share
        return whole[pl.ds(pl.multiple_of(start, share), share), :]

    for place, k in enumerate(list(range(1, parts)) + [0]):
        here = slice(place * share, (place + 1) * share)
        there = slice(rows + place * share, rows + (place + 1) * share)
        keep[here, :] = block(core, chip, k)
        keep[there, :] = block(core, 1 - chip, k)
        send_far[here, :] = encoded(block(1 - core, 1 - chip, k))
        send_near[here, :] = encoded(block(1 - core, chip, k))


def chip_kernel(mine, got, first, second):
    total = encoded(mine[...] + got[...].astype(F32))
    rows = first.shape[0]
    first[...] = total[:rows]
    second[...] = total[rows:]


def shares_kernel(mine, near, far, *outs):
    total = mine[...] + near[...].astype(F32) + far[...].astype(F32)
    rows = outs[0].shape[0]
    for k, out in enumerate(outs):
        block = total[k * rows : (k + 1) * rows]
        out[...] = encoded(block) if out.dtype == BF16 else block


def sum_kernel(*refs):
    total = refs[0][...]
    for ref in refs[1:-1]:
        total += ref[...].astype(F32)
    refs[-1][...] = encoded(total)


def join_kernel(*refs):
    rows = refs[0].shape[0]
    for k, ref in enumerate(refs[:-1]):
        refs[-1][k * rows : (k + 1) * rows, :] = ref[...]


def finish_kernel(scale, parts, *refs):
    g_send, g_recv, g_update, g_decode, loss = refs[-5:]
    pieces = refs[:-5]
    width = g_send.shape[1]
    turn = parts if parts > 1 else 2
    share = width // 4 // turn
    ens, dom = lax.axis_index("ens"), lax.axis_index("dom")
    spot = 2 * lax.rem(ens, 2) + lax.div(ens, 2)
    total = jnp.zeros((share, LANES), F32)
    each = len(pieces) // 4
    for q, other in enumerate((0, 2, 1, 3)):
        quarter = lax.bitwise_xor(spot, other)
        step = 0
        for piece in pieces[q * each : (q + 1) * each]:
            for j in range(piece.shape[0] // share):
                spin = lax.rem(dom + parts - step, parts) if parts > 1 else step
                start = (quarter * turn + spin) * share
                place = pl.ds(pl.multiple_of(start, share), share)
                block = piece[j * share : (j + 1) * share, :].astype(F32)
                g_send[place, :] = block[:, :width]
                g_recv[place, :] = block[:, width : 2 * width]
                g_update[place, :] = block[:, 2 * width : 3 * width]
                g_decode[place, :] = block[:, 3 * width : -LANES]
                total += block[:, -LANES:]
                step += 1
    loss[0, 0] = jnp.sum(total) * scale


SCALAR = pl.BlockSpec(memory_space=pltpu.SMEM)


def along(value, axis, steps):
    size = lax.axis_size(axis)
    return lax.ppermute(value, axis, [(i, (i + steps) % size) for i in range(size)])


def flip(value, axis, bit):
    size = lax.axis_size(axis)
    return lax.ppermute(value, axis, [(i, i ^ bit) for i in range(size)])


def call(kernel, ins, outs, scratch=(), flops=0, scalars=0):
    size = sum(x.size * x.dtype.itemsize for x in list(ins) + list(outs))
    many = isinstance(outs, (list, tuple))
    return pl.pallas_call(
        kernel,
        out_shape=outs,
        in_specs=[SCALAR] * scalars + vmem(len(ins) - scalars),
        out_specs=vmem(len(outs)),
        scratch_shapes=list(scratch),
        compiler_params=params(),
        cost_estimate=cost(flops, size),
    )(*ins)


def scalar(value):
    return jnp.reshape(value, (1,)).astype(jnp.int32)


def reduced(keep, send_far, send_near, parts):
    quarter, cols = send_far.shape
    half, share = quarter // 2, quarter // parts
    got_far, got_near = flip(send_far, "ens", 1), flip(send_near, "ens", 1)
    whole = lambda x: pl.BlockSpec(x.shape, lambda i: (0, 0))
    rows = lambda size, at: pl.BlockSpec((size, cols), lambda i: (at, 0))
    piece = sds((half, cols), BF16)
    first, second = pl.pallas_call(
        chip_kernel,
        grid=(1,),
        out_shape=[piece, piece],
        in_specs=[rows(quarter, 1), whole(got_far)],
        out_specs=[whole(piece)] * 2,
        compiler_params=params(),
        cost_estimate=cost(0, 8 * keep.size),
    )(keep, got_far)
    first, second = flip(first, "ens", 2), flip(second, "ens", 2)

    def shares(at, far, outs):
        return pl.pallas_call(
            shares_kernel,
            grid=(1,),
            out_shape=outs,
            in_specs=[rows(half, at), rows(half, at), whole(far)],
            out_specs=[whole(x) for x in outs],
            compiler_params=params(),
            cost_estimate=cost(0, 8 * keep.size),
        )(keep, got_near, far)

    if parts == 1:
        sums = [shares(at, far, [sds((half, cols), F32)])[0] for at, far in enumerate((first, second))]
        return [call(sum_kernel, [lax.psum(x, "dom")], [piece])[0] for x in sums]
    terms = []
    count = half // share
    for at, far in enumerate((first, second)):
        outs = [sds((share, cols), BF16)] * count
        if at == 1:
            outs[-1] = sds((share, cols), F32)
        steps = range(at * count + 1, at * count + 1 + count)
        terms += [along(x, "dom", k) if k < parts else x for k, x in zip(steps, shares(at, far, outs))]
    (own,) = call(sum_kernel, terms[::-1], [sds((share, cols), BF16)])
    pieces = [own] + [along(own, "dom", k) for k in range(1, parts)]
    return [call(join_kernel, pieces[at * count : (at + 1) * count], [piece])[0] for at in range(2)]


def per_device(
    nodes, senders, send_next, send_prev, readout_vertex_list, dec_weights, base, observed_analysis,
    w_send, w_recv, vertex_refresh_matrix, w_decode,
):
    latent = nodes[0]
    count, width = latent.shape
    halo = send_next.shape[0]
    line_span, variables = base.shape
    degree = senders.shape[0]
    fan = readout_vertex_list.shape[0]
    ext_rows = count + 2 * halo
    members = lax.axis_size("ens")
    ens, dom = lax.axis_index("ens"), lax.axis_index("dom")
    to_next, to_prev = send_next.reshape(1, halo), send_prev.reshape(1, halo)

    nodes_t, next_t, prev_t = call(
        lend_kernel,
        [latent, to_next, to_prev],
        [sds((width, count), BF16), sds((width, halo), BF16), sds((width, halo), BF16)],
        flops=4 * width * count * halo,
    )
    lat_prev = along(next_t, "dom", 1)
    lat_next = along(prev_t, "dom", -1)

    core = scalar(lax.rem(ens, 2))
    w_send_t, vertex_t, w_decode_t, recv_t = call(
        weights_kernel,
        [w_send, w_recv, vertex_refresh_matrix, w_decode, nodes_t],
        [sds((width, width), BF16), sds((width, width), BF16), sds((variables, width), BF16), sds((width, count), F32)],
        flops=2 * width * width * count,
    )

    picked_t, slope_t, slope_sum_t, agg_t, upd_slope_t, hidden_t, field_t, next_t, prev_t = call(
        forward_kernel,
        [nodes_t, lat_prev, lat_next, senders, w_send_t, recv_t, vertex_t, w_decode_t, to_next, to_prev],
        [
            sds((degree, width, count), BF16), sds((degree, width, count), BF16), sds((width, count), F32),
            sds((width, count), BF16), sds((width, count), F32), sds((width, count), BF16),
            sds((variables, count), BF16), sds((variables, halo), BF16), sds((variables, halo), BF16),
        ],
        flops=2 * degree * width * count * (ext_rows + width),
    )
    lent = (along(next_t, "dom", 1), along(prev_t, "dom", -1))
    mids = [field_t] + [flip(field_t, "ens", m) for m in range(1, members)]

    block = 512
    steps = line_span // 2 // block
    fixed = lambda shape: pl.BlockSpec(shape, lambda i, *at: (0,) * len(shape))
    tall = lambda rows: pl.BlockSpec((rows, block), lambda i, *at: (0, i))
    tall_half = lambda rows: pl.BlockSpec((rows, block), lambda i, at: (0, i + at[0] * steps))
    flat_half = pl.BlockSpec((block, variables), lambda i, at: (i + at[0] * steps, 0))
    half_span = line_span // 2
    mat_hi, mat_lo, base_t, truth_t = pl.pallas_call(
        decoder_kernel,
        grid_spec=pltpu.PrefetchScalarGridSpec(
            num_scalar_prefetch=1,
            grid=(steps,),
            in_specs=[tall_half(fan), tall_half(fan), flat_half, flat_half, pl.BlockSpec(memory_space=pl.ANY)],
            out_specs=[tall(ext_rows), tall(ext_rows), tall(variables), tall(variables)],
        ),
        out_shape=[sds((ext_rows, half_span), BF16)] * 2 + [sds((variables, half_span), BF16)] * 2,
        compiler_params=params(),
        cost_estimate=cost(10 * ext_rows * half_span, 16e6),
    )(core, readout_vertex_list, dec_weights, base, observed_analysis, field_t)

    end = jnp.concatenate(lent, axis=1)
    ends = [end] + [flip(end, "ens", m) for m in range(1, members)]

    grads = pl.pallas_call(
        functools.partial(readout_kernel, line_span),
        grid=(steps,),
        out_shape=[sds((variables, count), F32), sds((variables, 2 * halo), F32)] * 2 + [sds((8, block), F32)],
        in_specs=[fixed((variables, count))] * members + [fixed((variables, 2 * halo))] * members + [
            tall(ext_rows), tall(ext_rows), tall(variables), tall(variables),
        ],
        out_specs=[fixed((variables, count)), fixed((variables, 2 * halo))] * 2 + [fixed((8, block))],
        scratch_shapes=[pltpu.VMEM((members * variables, ext_rows), BF16), pltpu.VMEM((2 * variables, ext_rows), F32)],
        compiler_params=params(),
        cost_estimate=cost(4 * members * variables * ext_rows * half_span, 14e6),
    )(*mids, *ends, mat_hi, mat_lo, base_t, truth_t)
    own_mid, own_end, pair_mid, pair_end, term = grads
    got_end = flip(pair_end, "ens", 1)
    got_mid = flip(pair_mid, "ens", 1)
    to_before, to_after = call(ends_kernel, [own_end, got_end], [sds((variables, halo), F32)] * 2)
    from_next, from_prev = along(to_before, "dom", -1), along(to_after, "dom", 1)

    cols = 3 * width + variables + LANES
    quarter = width // 4
    parts = lax.axis_size("dom")
    if quarter % (16 * parts):
        parts = 1
    keep, send_far, send_near = call(
        functools.partial(backward_kernel, parts),
        [
            own_mid, got_mid, from_next, from_prev, to_next, to_prev, term, w_decode,
            vertex_refresh_matrix, nodes_t, picked_t, slope_t, slope_sum_t, agg_t, upd_slope_t, hidden_t,
        ],
        [sds((2 * quarter, cols), F32), sds((quarter, cols), BF16), sds((quarter, cols), BF16)],
        [pltpu.VMEM((width, cols), F32)],
        flops=2 * (degree + 3) * width * width * count,
    )
    mine = reduced(keep, send_far, send_near, parts)
    across = [flip(x, "ens", 2) for x in mine]
    beside = [flip(x, "ens", 1) for x in mine]
    corner = [flip(x, "ens", 1) for x in across]
    g_send, g_recv, g_update, g_decode, loss = pl.pallas_call(
        functools.partial(finish_kernel, 1.0 / line_span, parts),
        out_shape=[sds((width, width), F32)] * 3 + [sds((width, variables), F32), sds((1, 1), F32)],
        in_specs=vmem(8),
        out_specs=vmem(4) + [SCALAR],
        compiler_params=params(),
        cost_estimate=cost(0, 6 * width * cols),
    )(*mine, *beside, *across, *corner)
    return g_send, g_recv, g_update, g_decode, loss[0, 0]


def solution(mesh):
    return jax.shard_map(
        per_device,
        mesh=mesh,
        in_specs=(
            P("ens", "dom", None), P(None, "dom"), P("dom"), P("dom"), P(None, "dom"), P(None, "dom"),
            P("dom", None), P("dom", None), P(), P(), P(), P(),
        ),
        out_specs=(P(), P(), P(), P(), P()),
        check_vma=False,
    )
```

```python
import functools

import jax
import jax.numpy as jnp
from jax import lax
from jax.experimental import pallas as pl
from jax.experimental.pallas import tpu as pltpu
from jax.sharding import PartitionSpec as P

EPS = 0.04
F32 = jnp.float32
BF16 = jnp.bfloat16
MIB = 1024 * 1024


def dot(a, b, ca=1, cb=0):
    return lax.dot_general(a, b, (((ca,), (cb,)), ((), ())), preferred_element_type=F32)


def dot_nt(a, b):
    return dot(a, b, 1, 1)


def one_hot(rows, index_row):
    shape = (rows, index_row.shape[1])
    hit = lax.broadcasted_iota(jnp.int32, shape, 0) == index_row
    return jnp.where(hit, 1.0, 0.0).astype(BF16)


def params(mib):
    return pltpu.CompilerParams(vmem_limit_bytes=int(mib * MIB))


def vmem(n):
    return [pl.BlockSpec(memory_space=pltpu.VMEM)] * n


def cost(flops, size):
    return pl.CostEstimate(flops=int(flops), bytes_accessed=int(size), transcendentals=0)


def sds(shape, dtype):
    return jax.ShapeDtypeStruct(shape, dtype)


def lend_kernel(nodes, to_next, to_prev, nodes_t, next_t, prev_t):
    table = nodes[...].T
    nodes_t[...] = table
    count = table.shape[1]
    next_t[...] = dot(table, one_hot(count, to_next[...])).astype(BF16)
    prev_t[...] = dot(table, one_hot(count, to_prev[...])).astype(BF16)


def weights_kernel(w_send, w_recv, vertex, w_decode, nodes_t, w_send_t, vertex_t, w_decode_t, recv_t):
    w_send_t[...] = w_send[...].T * 0.5
    vertex_t[...] = vertex[...].T * 0.5
    w_decode_t[...] = w_decode[...].T
    recv_t[...] = dot(w_recv[...].T, nodes_t[...]) * 0.5


def decoder_kernel(core, vertices, weights, base, truth, after, mat, base_t, truth_t):
    del core, after
    rows, tile = mat.shape[0] // 2, 16
    shape = (tile, mat.shape[1])
    spread = lambda ref, k: jnp.broadcast_to(ref[k : k + 1, :], shape)
    vertex = [spread(vertices, k) for k in range(vertices.shape[0])]
    weight = [spread(weights, k) for k in range(vertices.shape[0])]
    row = lax.broadcasted_iota(jnp.int32, shape, 0)

    for start in range(0, rows, tile):
        here = row + start
        total = jnp.where(here == vertex[0], weight[0], 0.0)
        for k in range(1, len(vertex)):
            total += jnp.where(here == vertex[k], weight[k], 0.0)
        hi, lo = split(total)
        mat[start : start + tile, :] = hi
        mat[rows + start : rows + start + tile, :] = lo
    base_t[...] = base[...].T
    truth_t[...] = truth[...].T


TILE = 16


def bent(half):
    t = jnp.tanh(half)
    u = half * t
    return half + u, (1.0 + t) * (1.0 + half - u)


def forward_kernel(
    nodes_t, from_prev, from_next, senders, w_send_t, recv_t, vertex_t, w_decode_t, to_next, to_prev,
    picked_t, slope_t, slope_sum_t, agg_t, upd_slope_t, hidden_t, field_t, next_t, prev_t,
    pre,
):
    degree, count = senders.shape
    halo = from_prev.shape[1]
    width = nodes_t.shape[0]
    ext = jnp.concatenate([nodes_t[...], from_prev[...], from_next[...]], axis=1)
    for k in range(degree):
        here = slice(k * count, (k + 1) * count)
        picked_t[:, here] = dot(ext, one_hot(count + 2 * halo, senders[k : k + 1, :])).astype(BF16)
        pre[:, here] = dot(w_send_t[...], picked_t[:, here])
    for start in range(0, width, TILE):
        rows = slice(start, start + TILE)
        recv = recv_t[rows, :]
        total = slopes = None
        for k in range(degree):
            here = slice(k * count, (k + 1) * count)
            value, slope = bent(pre[rows, here] + recv)
            slope_t[rows, here] = slope.astype(BF16)
            total = value if k == 0 else total + value
            slopes = slope if k == 0 else slopes + slope
        slope_sum_t[rows, :] = slopes
        agg_t[rows, :] = (total * (1.0 / degree)).astype(BF16)
    pre[:, :count] = dot(vertex_t[...], agg_t[...])
    for start in range(0, width, TILE):
        rows = slice(start, start + TILE)
        value, slope = bent(pre[rows, :count])
        upd_slope_t[rows, :] = slope * 0.5
        hidden_t[rows, :] = (nodes_t[rows, :].astype(F32) + value).astype(BF16)
    field = dot(w_decode_t[...], hidden_t[...]).astype(BF16)
    field_t[...] = field
    next_t[...] = dot(field, one_hot(count, to_next[...])).astype(BF16)
    prev_t[...] = dot(field, one_hot(count, to_prev[...])).astype(BF16)


def readout_kernel(line_span, *refs):
    mids, ends = refs[0:4], refs[4:8]
    mat, base_t, truth_t = refs[8:11]
    own_mid, own_end, pair_mid, pair_end, loss = refs[11:16]
    table, grad, states, slopes = refs[16:20]
    step = pl.program_id(0)
    members = len(mids)
    variables, count = own_mid.shape
    ext_rows = grad.shape[1]

    @pl.when(step == 0)
    def _():
        grad[...] = jnp.zeros_like(grad)
        loss[...] = jnp.zeros_like(loss)
        for m in range(members):
            for base in (0, ext_rows):
                table[m * variables : (m + 1) * variables, base : base + count] = mids[m][...]
                table[m * variables : (m + 1) * variables, base + count : base + ext_rows] = ends[m][...]

    states[...] = dot(table[...], mat[...])

    def bend(diff):
        square = diff * diff + EPS
        inverse = lax.rsqrt(square)
        return square * inverse, diff * inverse

    alone = EPS**0.5
    across = states.shape[1]
    wide = min(256, across)
    for left in range(0, across, wide):
        cols = slice(left, left + wide)
        summed = jnp.zeros((8, wide), F32)
        for start in range(0, variables, TILE):
            rows = slice(start, start + TILE)
            ready = base_t[rows, cols].astype(F32)
            truth = truth_t[rows, cols].astype(F32)
            x = [
                (states[m * variables + start : m * variables + start + TILE, cols] + ready).astype(BF16).astype(F32)
                for m in range(members)
            ]
            apart = [alone, alone]
            pull = [0.0, 0.0]
            for i in range(2):
                for j in range(i + 1, members):
                    size, slope = bend(x[i] - x[j])
                    apart[i] = apart[i] + size
                    pull[i] = pull[i] + slope
                    if j < 2:
                        apart[j] = apart[j] + size
                        pull[j] = pull[j] - slope
            near = 0.0
            for i in range(2):
                size, push = bend(x[i] - truth)
                near = near + size
                slope = push * (1.0 / members / line_span) - pull[i] * (1.0 / (members * (members - 1.0)) / line_span)
                slopes[i * variables + start : i * variables + start + TILE, cols] = slope.astype(BF16)
            term = near * (1.0 / members) - (apart[0] + apart[1]) * (1.0 / (2.0 * members * (members - 1)))
            summed += term[:8] + term[8:]
        loss[:, cols] += summed
    grad[...] += dot_nt(slopes[...], mat[:ext_rows, :])

    @pl.when(step == pl.num_programs(0) - 1)
    def _():
        for i, (mid, end) in enumerate(((own_mid, own_end), (pair_mid, pair_end))):
            rows = slice(i * variables, (i + 1) * variables)
            mid[...] = grad[rows, :count]
            end[...] = grad[rows, count:]


def ends_kernel(mine, got, after, before):
    halo = after.shape[1]
    total = mine[...] + got[...]
    after[...] = total[:, :halo]
    before[...] = total[:, halo:]


def split(value):
    hi = value.astype(BF16)
    return hi, (value - hi.astype(F32)).astype(BF16)


LANES = 128


def encoded(total):
    tile = total[:, -LANES:]
    value = tile + pltpu.roll(tile, LANES // 2, 1)
    hi = value.astype(BF16).astype(F32)
    lane = lax.broadcasted_iota(jnp.int32, tile.shape, 1)
    tile = jnp.where(lane < LANES // 2, hi, value - hi)
    return jnp.concatenate([total[:, :-LANES].astype(BF16), tile.astype(BF16)], axis=1)


def backward_kernel(
    parts, own_mid, pair_mid, from_next, from_prev, to_next, to_prev, term, w_decode, vertex, nodes_t,
    picked_t, slope_t, slope_sum_t, agg_t, upd_slope_t, hidden_t,
    keep, send_far, send_near, whole, back, grad_pre,
):
    count = nodes_t.shape[1]
    width = nodes_t.shape[0]
    grad_z = own_mid[...] + pair_mid[...]
    for got, rows in ((from_next[...], to_next), (from_prev[...], to_prev)):
        place = one_hot(count, rows[...])
        hi, lo = split(got)
        grad_z += dot_nt(hi, place) + dot_nt(lo, place)
    grad_z = grad_z.astype(BF16)
    main = whole.shape[1] - LANES
    whole[:, 3 * width : main] = dot_nt(hidden_t[...], grad_z)
    grad_upd = (dot(w_decode[...], grad_z) * upd_slope_t[...]).astype(BF16)
    whole[:, 2 * width : 3 * width] = dot_nt(agg_t[...], grad_upd)
    degree = slope_t.shape[1] // count
    back[...] = dot(vertex[...], grad_upd)
    for start in range(0, width, TILE):
        rows = slice(start, start + TILE)
        grad_agg = back[rows, :] * (0.5 / degree)
        grad_pre[rows, degree * count :] = (grad_agg * slope_sum_t[rows, :]).astype(BF16)
        for k in range(degree):
            here = slice(k * count, (k + 1) * count)
            grad_pre[rows, here] = (grad_agg * slope_t[rows, here].astype(F32)).astype(BF16)
    whole[:, width : 2 * width] = dot_nt(nodes_t[...], grad_pre[:, degree * count :])
    whole[:, :width] = dot_nt(picked_t[...], grad_pre[:, : degree * count])
    whole[:, main:] = jnp.zeros((width, LANES), F32)
    spot = (lax.broadcasted_iota(jnp.int32, (8, LANES), 0) == 0) & (lax.broadcasted_iota(jnp.int32, (8, LANES), 1) == 0)
    whole[0:8, main:] = jnp.where(spot, jnp.sum(term[...]), 0.0)
    ens, dom = lax.axis_index("ens"), lax.axis_index("dom")
    core, chip = lax.rem(ens, 2), lax.div(ens, 2)
    rows = send_far.shape[0]
    share = rows // parts

    def block(c, x, k):
        start = ((2 * c + x) * parts + lax.rem(dom + k, parts)) * share
        return whole[pl.ds(pl.multiple_of(start, share), share), :]

    for place, k in enumerate(list(range(1, parts)) + [0]):
        here = slice(place * share, (place + 1) * share)
        there = slice(rows + place * share, rows + (place + 1) * share)
        keep[here, :] = block(core, chip, k)
        keep[there, :] = block(core, 1 - chip, k)
        send_far[here, :] = encoded(block(1 - core, 1 - chip, k))
        send_near[here, :] = encoded(block(1 - core, chip, k))


def chip_kernel(mine, got, first, second):
    total = encoded(mine[...] + got[...].astype(F32))
    rows = first.shape[0]
    first[...] = total[:rows]
    second[...] = total[rows:]


def shares_kernel(mine, near, far, *outs):
    total = mine[...] + near[...].astype(F32) + far[...].astype(F32)
    rows = outs[0].shape[0]
    for k, out in enumerate(outs):
        block = total[k * rows : (k + 1) * rows]
        out[...] = encoded(block) if out.dtype == BF16 else block


def sum_kernel(*refs):
    total = refs[0][...]
    for ref in refs[1:-1]:
        total += ref[...].astype(F32)
    refs[-1][...] = encoded(total)


def join_kernel(*refs):
    rows = refs[0].shape[0]
    for k, ref in enumerate(refs[:-1]):
        refs[-1][k * rows : (k + 1) * rows, :] = ref[...]


def finish_kernel(scale, parts, *refs):
    g_send, g_recv, g_update, g_decode, loss = refs[-5:]
    pieces = refs[:-5]
    width = g_send.shape[1]
    turn = parts if parts > 1 else 2
    share = width // 4 // turn
    ens, dom = lax.axis_index("ens"), lax.axis_index("dom")
    spot = 2 * lax.rem(ens, 2) + lax.div(ens, 2)
    total = jnp.zeros((share, LANES), F32)
    each = len(pieces) // 4
    for q, other in enumerate((0, 2, 1, 3)):
        quarter = lax.bitwise_xor(spot, other)
        step = 0
        for piece in pieces[q * each : (q + 1) * each]:
            for j in range(piece.shape[0] // share):
                spin = lax.rem(dom + parts - step, parts) if parts > 1 else step
                start = (quarter * turn + spin) * share
                place = pl.ds(pl.multiple_of(start, share), share)
                block = piece[j * share : (j + 1) * share, :].astype(F32)
                g_send[place, :] = block[:, :width]
                g_recv[place, :] = block[:, width : 2 * width]
                g_update[place, :] = block[:, 2 * width : 3 * width]
                g_decode[place, :] = block[:, 3 * width : -LANES]
                total += block[:, -LANES:]
                step += 1
    loss[0, 0] = jnp.sum(total) * scale


SCALAR = pl.BlockSpec(memory_space=pltpu.SMEM)


def along(value, axis, steps):
    size = lax.axis_size(axis)
    return lax.ppermute(value, axis, [(i, (i + steps) % size) for i in range(size)])


def flip(value, axis, bit):
    size = lax.axis_size(axis)
    return lax.ppermute(value, axis, [(i, i ^ bit) for i in range(size)])


def nbytes(arrays):
    return sum(x.size * x.dtype.itemsize for x in arrays)


def call(kernel, ins, outs, scratch=(), flops=0, room=4):
    size = nbytes(list(ins) + list(outs))
    return pl.pallas_call(
        kernel,
        out_shape=outs,
        in_specs=vmem(len(ins)),
        out_specs=vmem(len(outs)),
        scratch_shapes=list(scratch),
        compiler_params=params(1.1 * size / MIB + room),
        cost_estimate=cost(flops, size),
    )(*ins)


def scalar(value):
    return jnp.reshape(value, (1,)).astype(jnp.int32)


def reduced(keep, send_far, send_near, parts):
    quarter, cols = send_far.shape
    half, share = quarter // 2, quarter // parts
    got_far, got_near = flip(send_far, "ens", 1), flip(send_near, "ens", 1)
    whole = lambda x: pl.BlockSpec(x.shape, lambda i: (0, 0))
    rows = lambda size, at: pl.BlockSpec((size, cols), lambda i: (at, 0))
    piece = sds((half, cols), BF16)
    first, second = pl.pallas_call(
        chip_kernel,
        grid=(1,),
        out_shape=[piece, piece],
        in_specs=[rows(quarter, 1), whole(got_far)],
        out_specs=[whole(piece)] * 2,
        compiler_params=params(12),
        cost_estimate=cost(0, 8 * keep.size),
    )(keep, got_far)
    first, second = flip(first, "ens", 2), flip(second, "ens", 2)

    def shares(at, far, outs):
        return pl.pallas_call(
            shares_kernel,
            grid=(1,),
            out_shape=outs,
            in_specs=[rows(half, at), rows(half, at), whole(far)],
            out_specs=[whole(x) for x in outs],
            compiler_params=params(12),
            cost_estimate=cost(0, 8 * keep.size),
        )(keep, got_near, far)

    if parts == 1:
        sums = [shares(at, far, [sds((half, cols), F32)])[0] for at, far in enumerate((first, second))]
        return [call(sum_kernel, [lax.psum(x, "dom")], [piece])[0] for x in sums]
    terms = []
    count = half // share
    for at, far in enumerate((first, second)):
        outs = [sds((share, cols), BF16)] * count
        if at == 1:
            outs[-1] = sds((share, cols), F32)
        steps = range(at * count + 1, at * count + 1 + count)
        terms += [along(x, "dom", k) if k < parts else x for k, x in zip(steps, shares(at, far, outs))]
    (own,) = call(sum_kernel, terms[::-1], [sds((share, cols), BF16)])
    pieces = [own] + [along(own, "dom", k) for k in range(1, parts)]
    return [call(join_kernel, pieces[at * count : (at + 1) * count], [piece])[0] for at in range(2)]


def per_device(
    nodes, senders, send_next, send_prev, readout_vertex_list, dec_weights, base, observed_analysis,
    w_send, w_recv, vertex_refresh_matrix, w_decode,
):
    latent = nodes[0]
    count, width = latent.shape
    halo = send_next.shape[0]
    line_span, variables = base.shape
    degree = senders.shape[0]
    fan = readout_vertex_list.shape[0]
    ext_rows = count + 2 * halo
    members = lax.axis_size("ens")
    ens, dom = lax.axis_index("ens"), lax.axis_index("dom")
    to_next, to_prev = send_next.reshape(1, halo), send_prev.reshape(1, halo)

    nodes_t, next_t, prev_t = call(
        lend_kernel,
        [latent, to_next, to_prev],
        [sds((width, count), BF16), sds((width, halo), BF16), sds((width, halo), BF16)],
        flops=4 * width * count * halo,
    )
    lat_prev = along(next_t, "dom", 1)
    lat_next = along(prev_t, "dom", -1)

    core = scalar(lax.rem(ens, 2))
    w_send_t, vertex_t, w_decode_t, recv_t = call(
        weights_kernel,
        [w_send, w_recv, vertex_refresh_matrix, w_decode, nodes_t],
        [sds((width, width), BF16), sds((width, width), BF16), sds((variables, width), BF16), sds((width, count), F32)],
        flops=2 * width * width * count,
    )

    picked_t, slope_t, slope_sum_t, agg_t, upd_slope_t, hidden_t, field_t, next_t, prev_t = call(
        forward_kernel,
        [nodes_t, lat_prev, lat_next, senders, w_send_t, recv_t, vertex_t, w_decode_t, to_next, to_prev],
        [
            sds((width, degree * count), BF16), sds((width, degree * count), BF16), sds((width, count), F32),
            sds((width, count), BF16), sds((width, count), F32), sds((width, count), BF16),
            sds((variables, count), BF16), sds((variables, halo), BF16), sds((variables, halo), BF16),
        ],
        [pltpu.VMEM((width, degree * count), F32)],
        flops=2 * degree * width * count * (ext_rows + width),
        room=14,
    )
    lent = (along(next_t, "dom", 1), along(prev_t, "dom", -1))
    mids = [field_t] + [flip(field_t, "ens", m) for m in range(1, members)]

    block = 512
    steps = line_span // 2 // block
    fixed = lambda shape: pl.BlockSpec(shape, lambda i, *at: (0,) * len(shape))
    tall = lambda rows: pl.BlockSpec((rows, block), lambda i, *at: (0, i))
    tall_half = lambda rows: pl.BlockSpec((rows, block), lambda i, at: (0, i + at[0] * steps))
    flat_half = pl.BlockSpec((block, variables), lambda i, at: (i + at[0] * steps, 0))
    half_span = line_span // 2
    mat, base_t, truth_t = pl.pallas_call(
        decoder_kernel,
        grid_spec=pltpu.PrefetchScalarGridSpec(
            num_scalar_prefetch=1,
            grid=(steps,),
            in_specs=[tall_half(fan), tall_half(fan), flat_half, flat_half, pl.BlockSpec(memory_space=pl.ANY)],
            out_specs=[tall(2 * ext_rows), tall(variables), tall(variables)],
        ),
        out_shape=[sds((2 * ext_rows, half_span), BF16)] + [sds((variables, half_span), BF16)] * 2,
        compiler_params=params(12),
        cost_estimate=cost(10 * ext_rows * half_span, 16e6),
    )(core, readout_vertex_list, dec_weights, base, observed_analysis, field_t)

    end = jnp.concatenate(lent, axis=1)
    ends = [end] + [flip(end, "ens", m) for m in range(1, members)]

    grads = pl.pallas_call(
        functools.partial(readout_kernel, line_span),
        grid=(steps,),
        out_shape=[sds((variables, count), F32), sds((variables, 2 * halo), F32)] * 2 + [sds((8, block), F32)],
        in_specs=[fixed((variables, count))] * members + [fixed((variables, 2 * halo))] * members + [
            tall(2 * ext_rows), tall(variables), tall(variables),
        ],
        out_specs=[fixed((variables, count)), fixed((variables, 2 * halo))] * 2 + [fixed((8, block))],
        scratch_shapes=[
            pltpu.VMEM((members * variables, 2 * ext_rows), BF16), pltpu.VMEM((2 * variables, ext_rows), F32),
            pltpu.VMEM((members * variables, block), F32), pltpu.VMEM((2 * variables, block), BF16),
        ],
        compiler_params=params(20),
        cost_estimate=cost(4 * members * variables * ext_rows * half_span, 14e6),
    )(*mids, *ends, mat, base_t, truth_t)
    own_mid, own_end, pair_mid, pair_end, term = grads
    got_end = flip(pair_end, "ens", 1)
    got_mid = flip(pair_mid, "ens", 1)
    to_before, to_after = call(ends_kernel, [own_end, got_end], [sds((variables, halo), F32)] * 2)
    from_next, from_prev = along(to_before, "dom", -1), along(to_after, "dom", 1)

    cols = 3 * width + variables + LANES
    quarter = width // 4
    parts = lax.axis_size("dom")
    if quarter % (16 * parts):
        parts = 1
    keep, send_far, send_near = call(
        functools.partial(backward_kernel, parts),
        [
            own_mid, got_mid, from_next, from_prev, to_next, to_prev, term, w_decode,
            vertex_refresh_matrix, nodes_t, picked_t, slope_t, slope_sum_t, agg_t, upd_slope_t, hidden_t,
        ],
        [sds((2 * quarter, cols), F32), sds((quarter, cols), BF16), sds((quarter, cols), BF16)],
        [pltpu.VMEM((width, cols), F32), pltpu.VMEM((width, count), F32), pltpu.VMEM((width, (degree + 1) * count), BF16)],
        flops=2 * (degree + 3) * width * width * count,
        room=16,
    )
    mine = reduced(keep, send_far, send_near, parts)
    across = [flip(x, "ens", 2) for x in mine]
    beside = [flip(x, "ens", 1) for x in mine]
    corner = [flip(x, "ens", 1) for x in across]
    g_send, g_recv, g_update, g_decode, loss = pl.pallas_call(
        functools.partial(finish_kernel, 1.0 / line_span, parts),
        out_shape=[sds((width, width), F32)] * 3 + [sds((width, variables), F32), sds((1, 1), F32)],
        in_specs=vmem(8),
        out_specs=vmem(4) + [SCALAR],
        compiler_params=params(14),
        cost_estimate=cost(0, 6 * width * cols),
    )(*mine, *beside, *across, *corner)
    return g_send, g_recv, g_update, g_decode, loss[0, 0]


def solution(mesh):
    return jax.shard_map(
        per_device,
        mesh=mesh,
        in_specs=(
            P("ens", "dom", None), P(None, "dom"), P("dom"), P("dom"), P(None, "dom"), P(None, "dom"),
            P("dom", None), P("dom", None), P(), P(), P(), P(),
        ),
        out_specs=(P(), P(), P(), P(), P()),
        check_vma=False,
    )
```

```python
import functools

import jax
import jax.numpy as jnp
from jax import lax
from jax.experimental import pallas as pl
from jax.experimental.pallas import tpu as pltpu
from jax.sharding import PartitionSpec as P

EPS = 0.04
F32 = jnp.float32
BF16 = jnp.bfloat16
MIB = 1024 * 1024


def dot(a, b, ca=1, cb=0):
    return lax.dot_general(a, b, (((ca,), (cb,)), ((), ())), preferred_element_type=F32)


def dot_nt(a, b):
    return dot(a, b, 1, 1)


def one_hot(rows, index_row):
    shape = (rows, index_row.shape[1])
    hit = lax.broadcasted_iota(jnp.int32, shape, 0) == index_row
    return jnp.where(hit, 1.0, 0.0).astype(BF16)


def params(mib):
    return pltpu.CompilerParams(vmem_limit_bytes=int(mib * MIB))


def vmem(n):
    return [pl.BlockSpec(memory_space=pltpu.VMEM)] * n


def cost(flops, size):
    return pl.CostEstimate(flops=int(flops), bytes_accessed=int(size), transcendentals=0)


def sds(shape, dtype):
    return jax.ShapeDtypeStruct(shape, dtype)


HBM = pl.BlockSpec(memory_space=pltpu.HBM)


def fetched(sources, targets, sems):
    copies = [pltpu.make_async_copy(a, b, sems.at[i]) for i, (a, b) in enumerate(zip(sources, targets))]
    for copy in copies:
        copy.start()
    return copies


def lend_kernel(nodes, to_next, to_prev, nodes_t, next_t, prev_t, held, rows_next, rows_prev, sems):
    for copy in fetched((nodes, to_next, to_prev), (held, rows_next, rows_prev), sems):
        copy.wait()
    table = held[...].T
    nodes_t[...] = table
    count = table.shape[1]
    next_t[...] = dot(table, one_hot(count, rows_next[...])).astype(BF16)
    prev_t[...] = dot(table, one_hot(count, rows_prev[...])).astype(BF16)


def decoder_kernel(core, vertices, weights, base, truth, after, mat, base_t, truth_t, base_rows, truth_rows, sems):
    del after
    span = base_rows.shape[0]
    half = pl.ds(pl.multiple_of(core[0] * span, span), span)
    copies = [
        pltpu.make_async_copy(base.at[half, :], base_rows, sems.at[0]),
        pltpu.make_async_copy(truth.at[half, :], truth_rows, sems.at[1]),
    ]

    @pl.when(pl.program_id(0) == 0)
    def _():
        for copy in copies:
            copy.start()

    rows, tile = mat.shape[0] // 2, 16
    shape = (tile, mat.shape[1])
    spread = lambda ref, k: jnp.broadcast_to(ref[k : k + 1, :], shape)
    vertex = [spread(vertices, k) for k in range(vertices.shape[0])]
    weight = [spread(weights, k) for k in range(vertices.shape[0])]
    row = lax.broadcasted_iota(jnp.int32, shape, 0)

    for start in range(0, rows, tile):
        here = row + start
        total = jnp.where(here == vertex[0], weight[0], 0.0)
        for k in range(1, len(vertex)):
            total += jnp.where(here == vertex[k], weight[k], 0.0)
        hi, lo = split(total)
        mat[start : start + tile, :] = hi
        mat[rows + start : rows + start + tile, :] = lo

    @pl.when(pl.program_id(0) == pl.num_programs(0) - 1)
    def _():
        for copy in copies:
            copy.wait()
        base_t[...] = base_rows[...].T
        truth_t[...] = truth_rows[...].T


TILE = 16


def bent(half):
    t = jnp.tanh(half)
    u = half * t
    return half + u, (1.0 + t) * (1.0 + half - u)


def forward_kernel(
    nodes_t, from_prev, from_next, senders_in, to_next_in, to_prev_in, w_send_in, w_recv_in, vertex_in, w_decode_in,
    picked_t, field_t, next_t, prev_t, slope_out, slope_sum_out, agg_out, upd_slope_out, hidden_out,
    pre, senders, to_next, to_prev, w_send, w_recv, vertex, w_decode, recv_t,
    slope_t, slope_sum_t, agg_t, upd_slope_t, hidden_t, in_sems, out_sems,
):
    fetch = fetched(
        (senders_in, to_next_in, to_prev_in, w_send_in, w_recv_in, vertex_in, w_decode_in),
        (senders, to_next, to_prev, w_send, w_recv, vertex, w_decode),
        in_sems,
    )
    stored = []

    def store(source, target):
        copy = pltpu.make_async_copy(source, target, out_sems.at[len(stored)])
        copy.start()
        stored.append(copy)

    degree, count = senders.shape
    halo = from_prev.shape[1]
    width = nodes_t.shape[0]
    ext = jnp.concatenate([nodes_t[...], from_prev[...], from_next[...]], axis=1)
    for copy in fetch:
        copy.wait()
    w_send_t = w_send[...].T * 0.5
    recv_t[...] = dot(w_recv[...].T, nodes_t[...]) * 0.5
    for k in range(degree):
        here = slice(k * count, (k + 1) * count)
        picked_t[:, here] = dot(ext, one_hot(count + 2 * halo, senders[k : k + 1, :])).astype(BF16)
        pre[:, here] = dot(w_send_t, picked_t[:, here])
    for start in range(0, width, TILE):
        rows = slice(start, start + TILE)
        recv = recv_t[rows, :]
        total = slopes = None
        for k in range(degree):
            here = slice(k * count, (k + 1) * count)
            value, slope = bent(pre[rows, here] + recv)
            slope_t[rows, here] = slope.astype(BF16)
            total = value if k == 0 else total + value
            slopes = slope if k == 0 else slopes + slope
        slope_sum_t[rows, :] = slopes
        agg_t[rows, :] = (total * (1.0 / degree)).astype(BF16)
        if (start + TILE) % 128 == 0:
            group = slice(start + TILE - 128, start + TILE)
            store(slope_t.at[group, :], slope_out.at[group, :])
    store(slope_sum_t, slope_sum_out)
    store(agg_t, agg_out)
    pre[:, :count] = dot(vertex[...].T * 0.5, agg_t[...])
    for start in range(0, width, TILE):
        rows = slice(start, start + TILE)
        value, slope = bent(pre[rows, :count])
        upd_slope_t[rows, :] = slope * 0.5
        hidden_t[rows, :] = (nodes_t[rows, :].astype(F32) + value).astype(BF16)
    store(upd_slope_t, upd_slope_out)
    store(hidden_t, hidden_out)
    field = dot(w_decode[...].T, hidden_t[...]).astype(BF16)
    field_t[...] = field
    next_t[...] = dot(field, one_hot(count, to_next[...])).astype(BF16)
    prev_t[...] = dot(field, one_hot(count, to_prev[...])).astype(BF16)
    for copy in stored:
        copy.wait()


def readout_kernel(line_span, *refs):
    mids, ends = refs[0:4], refs[4:8]
    mat, base_t, truth_t = refs[8:11]
    own_mid, own_end, pair_mid, pair_end, loss = refs[11:16]
    table, grad, states, slopes = refs[16:20]
    step = pl.program_id(0)
    members = len(mids)
    variables, count = own_mid.shape
    ext_rows = grad.shape[1]

    @pl.when(step == 0)
    def _():
        grad[...] = jnp.zeros_like(grad)
        loss[...] = jnp.zeros_like(loss)
        for m in range(members):
            for base in (0, ext_rows):
                table[m * variables : (m + 1) * variables, base : base + count] = mids[m][...]
                table[m * variables : (m + 1) * variables, base + count : base + ext_rows] = ends[m][...]

    states[...] = dot(table[...], mat[...])

    def bend(diff):
        square = diff * diff + EPS
        inverse = lax.rsqrt(square)
        return square * inverse, diff * inverse

    alone = EPS**0.5
    across = states.shape[1]
    wide = min(256, across)
    for left in range(0, across, wide):
        cols = slice(left, left + wide)
        summed = jnp.zeros((8, wide), F32)
        for start in range(0, variables, TILE):
            rows = slice(start, start + TILE)
            ready = base_t[rows, cols].astype(F32)
            truth = truth_t[rows, cols].astype(F32)
            x = [
                (states[m * variables + start : m * variables + start + TILE, cols] + ready).astype(BF16).astype(F32)
                for m in range(members)
            ]
            apart = [alone, alone]
            pull = [0.0, 0.0]
            for i in range(2):
                for j in range(i + 1, members):
                    size, slope = bend(x[i] - x[j])
                    apart[i] = apart[i] + size
                    pull[i] = pull[i] + slope
                    if j < 2:
                        apart[j] = apart[j] + size
                        pull[j] = pull[j] - slope
            near = 0.0
            for i in range(2):
                size, push = bend(x[i] - truth)
                near = near + size
                slope = push * (1.0 / members / line_span) - pull[i] * (1.0 / (members * (members - 1.0)) / line_span)
                slopes[i * variables + start : i * variables + start + TILE, cols] = slope.astype(BF16)
            term = near * (1.0 / members) - (apart[0] + apart[1]) * (1.0 / (2.0 * members * (members - 1)))
            summed += term[:8] + term[8:]
        loss[:, cols] += summed
    grad[...] += dot_nt(slopes[...], mat[:ext_rows, :])

    @pl.when(step == pl.num_programs(0) - 1)
    def _():
        for i, (mid, end) in enumerate(((own_mid, own_end), (pair_mid, pair_end))):
            rows = slice(i * variables, (i + 1) * variables)
            mid[...] = grad[rows, :count]
            end[...] = grad[rows, count:]


def ends_kernel(mine, got, after, before):
    halo = after.shape[1]
    total = mine[...] + got[...]
    after[...] = total[:, :halo]
    before[...] = total[:, halo:]


def split(value):
    hi = value.astype(BF16)
    return hi, (value - hi.astype(F32)).astype(BF16)


LANES = 128


def encoded(total):
    tile = total[:, -LANES:]
    value = tile + pltpu.roll(tile, LANES // 2, 1)
    hi = value.astype(BF16).astype(F32)
    lane = lax.broadcasted_iota(jnp.int32, tile.shape, 1)
    tile = jnp.where(lane < LANES // 2, hi, value - hi)
    return jnp.concatenate([total[:, :-LANES].astype(BF16), tile.astype(BF16)], axis=1)


def backward_kernel(
    own_mid, pair_mid, from_next, from_prev, to_next, to_prev, term, w_decode, vertex, nodes_t,
    picked_t, slope_t, slope_sum_t, agg_t, upd_slope_t, hidden_t,
    *refs,
):
    whole, back, grad_pre = refs[-3:]
    count = nodes_t.shape[1]
    width = nodes_t.shape[0]
    grad_z = own_mid[...] + pair_mid[...]
    for got, rows in ((from_next[...], to_next), (from_prev[...], to_prev)):
        place = one_hot(count, rows[...])
        hi, lo = split(got)
        grad_z += dot_nt(hi, place) + dot_nt(lo, place)
    grad_z = grad_z.astype(BF16)
    main = whole.shape[1] - LANES
    whole[:, 3 * width : main] = dot_nt(hidden_t[...], grad_z)
    grad_upd = (dot(w_decode[...], grad_z) * upd_slope_t[...]).astype(BF16)
    whole[:, 2 * width : 3 * width] = dot_nt(agg_t[...], grad_upd)
    degree = slope_t.shape[1] // count
    back[...] = dot(vertex[...], grad_upd)
    for start in range(0, width, TILE):
        rows = slice(start, start + TILE)
        grad_agg = back[rows, :] * (0.5 / degree)
        grad_pre[rows, degree * count :] = (grad_agg * slope_sum_t[rows, :]).astype(BF16)
        for k in range(degree):
            here = slice(k * count, (k + 1) * count)
            grad_pre[rows, here] = (grad_agg * slope_t[rows, here].astype(F32)).astype(BF16)
    whole[:, width : 2 * width] = dot_nt(nodes_t[...], grad_pre[:, degree * count :])
    whole[:, :width] = dot_nt(picked_t[...], grad_pre[:, : degree * count])
    whole[:, main:] = jnp.zeros((width, LANES), F32)
    spot = (lax.broadcasted_iota(jnp.int32, (8, LANES), 0) == 0) & (lax.broadcasted_iota(jnp.int32, (8, LANES), 1) == 0)
    whole[0:8, main:] = jnp.where(spot, jnp.sum(term[...]), 0.0)
    if len(refs) == 3:
        return
    keep, send_first, send_rest = refs[:3]
    core, x, z, y = position()
    share = width // 32

    def block(c, xr, yr, k):
        quarter = 2 * c + lax.bitwise_xor(x, xr)
        start = (8 * quarter + 2 * lax.rem(z + k, 4) + lax.bitwise_xor(y, yr)) * share
        return whole[pl.ds(pl.multiple_of(start, share), share), :]

    at = 0
    for xr, yr in ((1, 1), (1, 0), (0, 1), (0, 0)):
        for k in (1, 2, 3, 0):
            keep[at : at + share, :] = block(core, xr, yr, k)
            value = encoded(block(1 - core, xr, yr, k))
            if at < 4 * share:
                send_first[at : at + share, :] = value
            else:
                send_rest[at - 4 * share : at - 3 * share, :] = value
            at += share


def corner_kernel(keep, first, by_x, by_y):
    block = 2 * by_x.shape[0]
    total = encoded(keep[:block, :] + first[...].astype(F32))
    by_x[...] = total[: block // 2]
    by_y[...] = total[block // 2 :]


def sides_kernel(keep, rest, from_x, from_y, to_x, to_y):
    block = to_x.shape[0]
    half = block // 2
    for rows, source, target in ((slice(half, block), from_y, to_x), (slice(0, half), from_x, to_y)):
        base = 0 if target is to_x else block
        total = keep[block + base : 2 * block + base, :] + rest[base : base + block, :].astype(F32)
        extra = source[...].astype(F32)
        zeros = jnp.zeros_like(extra)
        extra = jnp.concatenate([zeros, extra] if rows.start else [extra, zeros], axis=0)
        target[...] = encoded(total + extra)


def shares_kernel(keep, rest, from_x, from_y, *outs):
    rows = outs[0].shape[0]
    block = from_x.shape[0]
    total = keep[3 * block :, :] + rest[2 * block :, :].astype(F32) + from_x[...].astype(F32) + from_y[...].astype(F32)
    for k, out in enumerate(outs):
        value = total[k * rows : (k + 1) * rows]
        out[...] = encoded(value) if out.dtype == BF16 else value


def sum_kernel(*refs):
    total = refs[0][...]
    for ref in refs[1:-1]:
        total += ref[...].astype(F32)
    refs[-1][...] = encoded(total)


def join_kernel(*refs):
    rows = refs[0].shape[0]
    for k, ref in enumerate(refs[:-1]):
        refs[-1][k * rows : (k + 1) * rows, :] = ref[...]


def half_kernel(at, source, target):
    rows = target.shape[0]
    target[...] = source[at * rows : (at + 1) * rows, :]


def finish_kernel(scale, *refs):
    g_send, g_recv, g_update, g_decode, loss = refs[-5:]
    pieces = refs[:-5]
    width = g_send.shape[1]
    share = width // 32
    core, x, z, y = position()
    total = jnp.zeros((share, LANES), F32)
    layout = ((0, 0, 0), (1, 0, 0), (0, 1, 0), (1, 1, 0), (1, 1, 2))
    for i, piece in enumerate(pieces):
        xr, yr, first = layout[i % 5]
        quarter = 2 * (core if i < 5 else 1 - core) + lax.bitwise_xor(x, xr)
        for j in range(piece.shape[0] // share):
            start = (8 * quarter + 2 * lax.rem(z + 4 - first - j, 4) + lax.bitwise_xor(y, yr)) * share
            place = pl.ds(pl.multiple_of(start, share), share)
            value = piece[j * share : (j + 1) * share, :].astype(F32)
            g_send[place, :] = value[:, :width]
            g_recv[place, :] = value[:, width : 2 * width]
            g_update[place, :] = value[:, 2 * width : 3 * width]
            g_decode[place, :] = value[:, 3 * width : -LANES]
            total += value[:, -LANES:]
    loss[0, 0] = jnp.sum(total) * scale


def position():
    ens, dom = lax.axis_index("ens"), lax.axis_index("dom")
    return lax.rem(ens, 2), lax.div(ens, 2), lax.div(dom, 2), lax.rem(dom, 2)


SCALAR = pl.BlockSpec(memory_space=pltpu.SMEM)


def along(value, axis, steps):
    size = lax.axis_size(axis)
    return lax.ppermute(value, axis, [(i, (i + steps) % size) for i in range(size)])


def flip(value, axis, bit):
    size = lax.axis_size(axis)
    return lax.ppermute(value, axis, [(i, i ^ bit) for i in range(size)])


def nbytes(arrays):
    return sum(x.size * x.dtype.itemsize for x in arrays)


def call(kernel, ins, outs, scratch=(), flops=0, room=4, in_hbm=0, out_hbm=0):
    size = nbytes(list(ins) + list(outs))
    return pl.pallas_call(
        kernel,
        out_shape=outs,
        in_specs=vmem(len(ins) - in_hbm) + [HBM] * in_hbm,
        out_specs=vmem(len(outs) - out_hbm) + [HBM] * out_hbm,
        scratch_shapes=list(scratch),
        compiler_params=params(1.1 * size / MIB + room),
        cost_estimate=cost(flops, size),
    )(*ins)


def scalar(value):
    return jnp.reshape(value, (1,)).astype(jnp.int32)


def summed(keep, send_first, send_rest):
    block, cols = send_first.shape
    half, share = block // 2, block // 4
    core = lambda v: flip(v, "ens", 1)
    over_x = lambda v: flip(v, "ens", 2)
    over_y = lambda v: flip(v, "dom", 1)
    piece = lambda rows: sds((rows, cols), BF16)
    first, rest = core(send_first), core(send_rest)
    by_x, by_y = call(corner_kernel, [keep, first], [piece(half)] * 2)
    by_x, by_y = over_x(by_x), over_y(by_y)
    to_x, to_y = call(sides_kernel, [keep, rest, by_x, by_y], [piece(block)] * 2)
    to_x, to_y = over_x(to_x), over_y(to_y)
    shares = call(shares_kernel, [keep, rest, to_x, to_y], [piece(share)] * 3 + [sds((share, cols), F32)])
    terms = [shares[3]] + [along(shares[k - 1], "dom", 2 * k) for k in (1, 2, 3)]
    (own,) = call(sum_kernel, terms, [piece(share)])
    (mine,) = call(join_kernel, [own] + [along(own, "dom", 2 * k) for k in (1, 2, 3)], [piece(block)])
    x, y = over_x(mine), over_y(mine)
    (low,) = call(functools.partial(half_kernel, 0), [y], [piece(half)])
    (high,) = call(functools.partial(half_kernel, 1), [x], [piece(half)])
    here = [mine, x, y, over_x(low), over_y(high)]
    return here + [core(v) for v in here]


def per_device(
    nodes, senders, send_next, send_prev, readout_vertex_list, dec_weights, base, observed_analysis,
    w_send, w_recv, vertex_refresh_matrix, w_decode,
):
    latent = nodes[0]
    count, width = latent.shape
    halo = send_next.shape[0]
    line_span, variables = base.shape
    degree = senders.shape[0]
    fan = readout_vertex_list.shape[0]
    ext_rows = count + 2 * halo
    members = lax.axis_size("ens")
    ens, dom = lax.axis_index("ens"), lax.axis_index("dom")
    to_next, to_prev = send_next.reshape(1, halo), send_prev.reshape(1, halo)

    held = lambda shape, dtype=BF16: pltpu.VMEM(shape, dtype)
    indices = lambda: [held((1, halo), jnp.int32)] * 2
    nodes_t, next_t, prev_t = call(
        lend_kernel,
        [latent, to_next, to_prev],
        [sds((width, count), BF16), sds((width, halo), BF16), sds((width, halo), BF16)],
        [held((count, width))] + indices() + [pltpu.SemaphoreType.DMA((3,))],
        flops=4 * width * count * halo,
        in_hbm=3,
    )
    lat_prev = along(next_t, "dom", 1)
    lat_next = along(prev_t, "dom", -1)

    core = scalar(lax.rem(ens, 2))
    picked_t, field_t, next_t, prev_t, slope_t, slope_sum_t, agg_t, upd_slope_t, hidden_t = call(
        forward_kernel,
        [nodes_t, lat_prev, lat_next, senders, to_next, to_prev, w_send, w_recv, vertex_refresh_matrix, w_decode],
        [
            sds((width, degree * count), BF16), sds((variables, count), BF16), sds((variables, halo), BF16),
            sds((variables, halo), BF16), sds((width, degree * count), BF16), sds((width, count), F32),
            sds((width, count), BF16), sds((width, count), F32), sds((width, count), BF16),
        ],
        [held((width, degree * count), F32), held((degree, count), jnp.int32)] + indices() + [
            held((width, width)), held((width, width)), held((width, width)), held((width, variables)),
            held((width, count), F32), held((width, degree * count)), held((width, count), F32),
            held((width, count)), held((width, count), F32), held((width, count)),
            pltpu.SemaphoreType.DMA((7,)), pltpu.SemaphoreType.DMA((width // 128 + 4,)),
        ],
        flops=2 * degree * width * count * (ext_rows + width),
        room=14,
        in_hbm=7,
        out_hbm=5,
    )
    lent = (along(next_t, "dom", 1), along(prev_t, "dom", -1))
    mids = [field_t] + [flip(field_t, "ens", m) for m in range(1, members)]

    block = 512
    steps = line_span // 2 // block
    fixed = lambda shape: pl.BlockSpec(shape, lambda i, *at: (0,) * len(shape))
    tall = lambda rows: pl.BlockSpec((rows, block), lambda i, *at: (0, i))
    tall_half = lambda rows: pl.BlockSpec((rows, block), lambda i, at: (0, i + at[0] * steps))
    half_span = line_span // 2
    mat, base_t, truth_t = pl.pallas_call(
        decoder_kernel,
        grid_spec=pltpu.PrefetchScalarGridSpec(
            num_scalar_prefetch=1,
            grid=(steps,),
            in_specs=[tall_half(fan), tall_half(fan), HBM, HBM, pl.BlockSpec(memory_space=pl.ANY)],
            out_specs=[tall(2 * ext_rows), fixed((variables, half_span)), fixed((variables, half_span))],
            scratch_shapes=[held((half_span, variables)), held((half_span, variables)), pltpu.SemaphoreType.DMA((2,))],
        ),
        out_shape=[sds((2 * ext_rows, half_span), BF16)] + [sds((variables, half_span), BF16)] * 2,
        compiler_params=params(12),
        cost_estimate=cost(10 * ext_rows * half_span, 16e6),
    )(core, readout_vertex_list, dec_weights, base, observed_analysis, field_t)

    end = jnp.concatenate(lent, axis=1)
    ends = [end] + [flip(end, "ens", m) for m in range(1, members)]

    grads = pl.pallas_call(
        functools.partial(readout_kernel, line_span),
        grid=(steps,),
        out_shape=[sds((variables, count), F32), sds((variables, 2 * halo), F32)] * 2 + [sds((8, block), F32)],
        in_specs=[fixed((variables, count))] * members + [fixed((variables, 2 * halo))] * members + [
            tall(2 * ext_rows), tall(variables), tall(variables),
        ],
        out_specs=[fixed((variables, count)), fixed((variables, 2 * halo))] * 2 + [fixed((8, block))],
        scratch_shapes=[
            pltpu.VMEM((members * variables, 2 * ext_rows), BF16), pltpu.VMEM((2 * variables, ext_rows), F32),
            pltpu.VMEM((members * variables, block), F32), pltpu.VMEM((2 * variables, block), BF16),
        ],
        compiler_params=params(20),
        cost_estimate=cost(4 * members * variables * ext_rows * half_span, 14e6),
    )(*mids, *ends, mat, base_t, truth_t)
    own_mid, own_end, pair_mid, pair_end, term = grads
    got_end = flip(pair_end, "ens", 1)
    got_mid = flip(pair_mid, "ens", 1)
    to_before, to_after = call(ends_kernel, [own_end, got_end], [sds((variables, halo), F32)] * 2)
    from_next, from_prev = along(to_before, "dom", -1), along(to_after, "dom", 1)

    cols = 3 * width + variables + LANES
    operands = [
        own_mid, got_mid, from_next, from_prev, to_next, to_prev, term, w_decode,
        vertex_refresh_matrix, nodes_t, picked_t, slope_t, slope_sum_t, agg_t, upd_slope_t, hidden_t,
    ]
    whole = sds((width, cols), F32)
    scratch = [held((width, count), F32), held((width, (degree + 1) * count))]
    flops = 2 * (degree + 3) * width * width * count
    scale = 1.0 / line_span
    if lax.axis_size("dom") != 8 or members != 4 or width % 512:
        (total,) = call(backward_kernel, operands, [whole], scratch, flops, room=16)
        total = lax.psum(total, ("ens", "dom"))
        cuts = [total[:, i * width : (i + 1) * width] for i in range(3)]
        return *cuts, total[:, 3 * width : -LANES], jnp.sum(total[:, -LANES:]) * scale
    block = width // 8
    parts = call(
        backward_kernel,
        operands,
        [sds((4 * block, cols), F32), sds((block, cols), BF16), sds((3 * block, cols), BF16)],
        [held(whole.shape, F32)] + scratch,
        flops,
        room=16,
    )
    pieces = summed(*parts)
    g_send, g_recv, g_update, g_decode, loss = pl.pallas_call(
        functools.partial(finish_kernel, scale),
        out_shape=[sds((width, width), F32)] * 3 + [sds((width, variables), F32), sds((1, 1), F32)],
        in_specs=vmem(len(pieces)),
        out_specs=vmem(4) + [SCALAR],
        compiler_params=params(14),
        cost_estimate=cost(0, 6 * width * cols),
    )(*pieces)
    return g_send, g_recv, g_update, g_decode, loss[0, 0]


def solution(mesh):
    return jax.shard_map(
        per_device,
        mesh=mesh,
        in_specs=(
            P("ens", "dom", None), P(None, "dom"), P("dom"), P("dom"), P(None, "dom"), P(None, "dom"),
            P("dom", None), P("dom", None), P(), P(), P(), P(),
        ),
        out_specs=(P(), P(), P(), P(), P()),
        check_vma=False,
    )
```

```python
import functools

import jax
import jax.numpy as jnp
from jax import lax
from jax.experimental import pallas as pl
from jax.experimental.pallas import tpu as pltpu
from jax.sharding import PartitionSpec as P

EPS = 0.04
F32 = jnp.float32
BF16 = jnp.bfloat16
MIB = 1024 * 1024


def dot(a, b, ca=1, cb=0):
    return lax.dot_general(a, b, (((ca,), (cb,)), ((), ())), preferred_element_type=F32)


def dot_nt(a, b):
    return dot(a, b, 1, 1)


def one_hot(rows, index_row):
    shape = (rows, index_row.shape[1])
    hit = lax.broadcasted_iota(jnp.int32, shape, 0) == index_row
    return jnp.where(hit, 1.0, 0.0).astype(BF16)


def params(mib):
    return pltpu.CompilerParams(vmem_limit_bytes=int(mib * MIB))


def vmem(n):
    return [pl.BlockSpec(memory_space=pltpu.VMEM)] * n


def cost(flops, size):
    return pl.CostEstimate(flops=int(flops), bytes_accessed=int(size), transcendentals=0)


def sds(shape, dtype):
    return jax.ShapeDtypeStruct(shape, dtype)


HBM = pl.BlockSpec(memory_space=pltpu.HBM)


def fetched(sources, targets, sems):
    copies = [pltpu.make_async_copy(a, b, sems.at[i]) for i, (a, b) in enumerate(zip(sources, targets))]
    for copy in copies:
        copy.start()
    return copies


def sides(next_side, prev_side):
    even = lax.rem(lax.axis_index("dom"), 2) == 0
    return jnp.where(even, next_side, prev_side), jnp.where(even, prev_side, next_side)


def lend_kernel(nodes, to_next, to_prev, nodes_t, first_t, second_t, held, rows_next, rows_prev, sems):
    for copy in fetched((nodes, to_next, to_prev), (held, rows_next, rows_prev), sems):
        copy.wait()
    table = held[...].T
    nodes_t[...] = table
    count = table.shape[1]
    first, second = sides(rows_next[...], rows_prev[...])
    first_t[...] = dot(table, one_hot(count, first)).astype(BF16)
    second_t[...] = dot(table, one_hot(count, second)).astype(BF16)


def decoder_kernel(core, vertices, weights, base, truth, after, mat, base_t, truth_t, base_rows, truth_rows, sems):
    del after
    span = base_rows.shape[0]
    half = pl.ds(pl.multiple_of(core[0] * span, span), span)
    copies = [
        pltpu.make_async_copy(base.at[half, :], base_rows, sems.at[0]),
        pltpu.make_async_copy(truth.at[half, :], truth_rows, sems.at[1]),
    ]

    @pl.when(pl.program_id(0) == 0)
    def _():
        for copy in copies:
            copy.start()

    rows, tile = mat.shape[0] // 2, 16
    shape = (tile, mat.shape[1])
    spread = lambda ref, k: jnp.broadcast_to(ref[k : k + 1, :], shape)
    vertex = [spread(vertices, k) for k in range(vertices.shape[0])]
    weight = [spread(weights, k) for k in range(vertices.shape[0])]
    row = lax.broadcasted_iota(jnp.int32, shape, 0)

    for start in range(0, rows, tile):
        here = row + start
        total = jnp.where(here == vertex[0], weight[0], 0.0)
        for k in range(1, len(vertex)):
            total += jnp.where(here == vertex[k], weight[k], 0.0)
        hi, lo = split(total)
        mat[start : start + tile, :] = hi
        mat[rows + start : rows + start + tile, :] = lo

    @pl.when(pl.program_id(0) == pl.num_programs(0) - 1)
    def _():
        for copy in copies:
            copy.wait()
        base_t[...] = base_rows[...].T
        truth_t[...] = truth_rows[...].T


TILE = 16


def bent(half):
    t = jnp.tanh(half)
    u = half * t
    return half + u, (1.0 + t) * (1.0 + half - u)


def forward_kernel(
    nodes_t, from_first, from_second, senders_in, to_next_in, to_prev_in, w_send_in, w_recv_in, vertex_in, w_decode_in,
    picked_t, field_t, first_t, second_t, slope_out, slope_sum_out, agg_out, upd_slope_out, hidden_out,
    pre, senders, to_next, to_prev, w_send, w_recv, vertex, w_decode, recv_t,
    slope_t, slope_sum_t, agg_t, upd_slope_t, hidden_t, in_sems, out_sems,
):
    fetch = fetched(
        (senders_in, to_next_in, to_prev_in, w_send_in, w_recv_in, vertex_in, w_decode_in),
        (senders, to_next, to_prev, w_send, w_recv, vertex, w_decode),
        in_sems,
    )
    stored = []

    def store(source, target):
        copy = pltpu.make_async_copy(source, target, out_sems.at[len(stored)])
        copy.start()
        stored.append(copy)

    degree, count = senders.shape
    halo = from_first.shape[1]
    width = nodes_t.shape[0]
    from_next, from_prev = sides(from_first[...], from_second[...])
    ext = jnp.concatenate([nodes_t[...], from_prev, from_next], axis=1)
    for copy in fetch[:5]:
        copy.wait()
    w_send_t = w_send[...].T * 0.5
    recv_t[...] = dot(w_recv[...].T, nodes_t[...]) * 0.5
    for k in range(degree):
        here = slice(k * count, (k + 1) * count)
        picked_t[:, here] = dot(ext, one_hot(count + 2 * halo, senders[k : k + 1, :])).astype(BF16)
        pre[:, here] = dot(w_send_t, picked_t[:, here])
    for start in range(0, width, TILE):
        rows = slice(start, start + TILE)
        recv = recv_t[rows, :]
        total = slopes = None
        for k in range(degree):
            here = slice(k * count, (k + 1) * count)
            value, slope = bent(pre[rows, here] + recv)
            slope_t[rows, here] = slope.astype(BF16)
            total = value if k == 0 else total + value
            slopes = slope if k == 0 else slopes + slope
        slope_sum_t[rows, :] = slopes
        agg_t[rows, :] = (total * (1.0 / degree)).astype(BF16)
        if (start + TILE) % 128 == 0:
            group = slice(start + TILE - 128, start + TILE)
            store(slope_t.at[group, :], slope_out.at[group, :])
    store(slope_sum_t, slope_sum_out)
    store(agg_t, agg_out)
    for copy in fetch[5:]:
        copy.wait()
    pre[:, :count] = dot(vertex[...].T * 0.5, agg_t[...])
    for start in range(0, width, TILE):
        rows = slice(start, start + TILE)
        value, slope = bent(pre[rows, :count])
        upd_slope_t[rows, :] = slope * 0.5
        hidden_t[rows, :] = (nodes_t[rows, :].astype(F32) + value).astype(BF16)
    store(upd_slope_t, upd_slope_out)
    store(hidden_t, hidden_out)
    field = dot(w_decode[...].T, hidden_t[...]).astype(BF16)
    field_t[...] = field
    first, second = sides(to_next[...], to_prev[...])
    first_t[...] = dot(field, one_hot(count, first)).astype(BF16)
    second_t[...] = dot(field, one_hot(count, second)).astype(BF16)
    for copy in stored:
        copy.wait()


def readout_kernel(line_span, *refs):
    mids, ends = refs[0:4], refs[4:8]
    mat, base_t, truth_t = refs[8:11]
    own_mid, own_end, pair_mid, pair_end, loss = refs[11:16]
    table, grad, states, slopes = refs[16:20]
    step = pl.program_id(0)
    members = len(mids)
    variables, count = own_mid.shape
    ext_rows = grad.shape[1]

    @pl.when(step == 0)
    def _():
        grad[...] = jnp.zeros_like(grad)
        loss[...] = jnp.zeros_like(loss)
        for m in range(members):
            for base in (0, ext_rows):
                table[m * variables : (m + 1) * variables, base : base + count] = mids[m][...]
                table[m * variables : (m + 1) * variables, base + count : base + ext_rows] = ends[m][...]

    states[...] = dot(table[...], mat[...])

    def bend(diff):
        square = diff * diff + EPS
        inverse = lax.rsqrt(square)
        return square * inverse, diff * inverse

    alone = EPS**0.5
    across = states.shape[1]
    wide = min(256, across)
    for left in range(0, across, wide):
        cols = slice(left, left + wide)
        summed = jnp.zeros((8, wide), F32)
        for start in range(0, variables, TILE):
            rows = slice(start, start + TILE)
            ready = base_t[rows, cols].astype(F32)
            truth = truth_t[rows, cols].astype(F32)
            x = [
                (states[m * variables + start : m * variables + start + TILE, cols] + ready).astype(BF16).astype(F32)
                for m in range(members)
            ]
            apart = [alone, alone]
            pull = [0.0, 0.0]
            for i in range(2):
                for j in range(i + 1, members):
                    size, slope = bend(x[i] - x[j])
                    apart[i] = apart[i] + size
                    pull[i] = pull[i] + slope
                    if j < 2:
                        apart[j] = apart[j] + size
                        pull[j] = pull[j] - slope
            near = 0.0
            for i in range(2):
                size, push = bend(x[i] - truth)
                near = near + size
                slope = push * (1.0 / members / line_span) - pull[i] * (1.0 / (members * (members - 1.0)) / line_span)
                slopes[i * variables + start : i * variables + start + TILE, cols] = slope.astype(BF16)
            term = near * (1.0 / members) - (apart[0] + apart[1]) * (1.0 / (2.0 * members * (members - 1)))
            summed += term[:8] + term[8:]
        loss[:, cols] += summed
    grad[...] += dot_nt(slopes[...], mat[:ext_rows, :])

    @pl.when(step == pl.num_programs(0) - 1)
    def _():
        for i, (mid, end) in enumerate(((own_mid, own_end), (pair_mid, pair_end))):
            rows = slice(i * variables, (i + 1) * variables)
            mid[...] = grad[rows, :count]
            end[...] = grad[rows, count:]


def borrowed_kernel(first, second, end):
    halo = first.shape[1]
    from_next, from_prev = sides(first[...], second[...])
    end[:, :halo] = from_prev
    end[:, halo:] = from_next


def ends_kernel(mine, got, first, second):
    halo = first.shape[1]
    total = mine[...] + got[...]
    to_first, to_second = sides(total[:, halo:], total[:, :halo])
    first[...] = to_first.astype(BF16)
    second[...] = to_second.astype(BF16)


def split(value):
    hi = value.astype(BF16)
    return hi, (value - hi.astype(F32)).astype(BF16)


LANES = 128


def encoded(total):
    tile = total[:, -LANES:]
    value = tile + pltpu.roll(tile, LANES // 2, 1)
    hi = value.astype(BF16).astype(F32)
    lane = lax.broadcasted_iota(jnp.int32, tile.shape, 1)
    tile = jnp.where(lane < LANES // 2, hi, value - hi)
    return jnp.concatenate([total[:, :-LANES].astype(BF16), tile.astype(BF16)], axis=1)


def backward_kernel(
    own_mid, pair_mid, from_first, from_second, to_next, to_prev, term, w_decode, vertex, nodes_t,
    picked_t, slope_t, slope_sum_t, agg_t, upd_slope_t, hidden_t,
    *refs,
):
    whole, back, grad_pre = refs[-3:]
    count = nodes_t.shape[1]
    width = nodes_t.shape[0]
    grad_z = own_mid[...] + pair_mid[...]
    for got, rows in zip((from_first, from_second), sides(to_next[...], to_prev[...])):
        grad_z += dot_nt(got[...], one_hot(count, rows))
    grad_z = grad_z.astype(BF16)
    main = whole.shape[1] - LANES
    whole[:, 3 * width : main] = dot_nt(hidden_t[...], grad_z)
    grad_upd = (dot(w_decode[...], grad_z) * upd_slope_t[...]).astype(BF16)
    whole[:, 2 * width : 3 * width] = dot_nt(agg_t[...], grad_upd)
    degree = slope_t.shape[1] // count
    back[...] = dot(vertex[...], grad_upd)
    for start in range(0, width, TILE):
        rows = slice(start, start + TILE)
        grad_agg = back[rows, :] * (0.5 / degree)
        grad_pre[rows, degree * count :] = (grad_agg * slope_sum_t[rows, :]).astype(BF16)
        for k in range(degree):
            here = slice(k * count, (k + 1) * count)
            grad_pre[rows, here] = (grad_agg * slope_t[rows, here].astype(F32)).astype(BF16)
    whole[:, width : 2 * width] = dot_nt(nodes_t[...], grad_pre[:, degree * count :])
    whole[:, :width] = dot_nt(picked_t[...], grad_pre[:, : degree * count])
    whole[:, main:] = jnp.zeros((width, LANES), F32)
    spot = (lax.broadcasted_iota(jnp.int32, (8, LANES), 0) == 0) & (lax.broadcasted_iota(jnp.int32, (8, LANES), 1) == 0)
    whole[0:8, main:] = jnp.where(spot, jnp.sum(term[...]), 0.0)
    if len(refs) == 3:
        return
    keep, send_first, send_rest = refs[:3]
    core, x, z, y = position()
    share = width // 32

    def block(c, xr, yr, k):
        quarter = 2 * c + lax.bitwise_xor(x, xr)
        start = (8 * quarter + 2 * lax.bitwise_xor(z, k) + lax.bitwise_xor(y, yr)) * share
        return whole[pl.ds(pl.multiple_of(start, share), share), :]

    at = 0
    for xr, yr in ((1, 1), (1, 0), (0, 1), (0, 0)):
        for k in (1, 2, 3, 0):
            keep[at : at + share, :] = block(core, xr, yr, k)
            value = encoded(block(1 - core, xr, yr, k))
            if at < 4 * share:
                send_first[at : at + share, :] = value
            else:
                send_rest[at - 4 * share : at - 3 * share, :] = value
            at += share


def corner_kernel(keep, first, by_x, by_y):
    block = 2 * by_x.shape[0]
    total = encoded(keep[:block, :] + first[...].astype(F32))
    by_x[...] = total[: block // 2]
    by_y[...] = total[block // 2 :]


def sides_kernel(keep, rest, from_x, from_y, to_x, to_y):
    block = to_x.shape[0]
    half = block // 2
    for rows, source, target in ((slice(half, block), from_y, to_x), (slice(0, half), from_x, to_y)):
        base = 0 if target is to_x else block
        total = keep[block + base : 2 * block + base, :] + rest[base : base + block, :].astype(F32)
        extra = source[...].astype(F32)
        zeros = jnp.zeros_like(extra)
        extra = jnp.concatenate([zeros, extra] if rows.start else [extra, zeros], axis=0)
        target[...] = encoded(total + extra)


def shares_kernel(keep, rest, from_x, from_y, *outs):
    rows = outs[0].shape[0]
    block = from_x.shape[0]
    total = keep[3 * block :, :] + rest[2 * block :, :].astype(F32) + from_x[...].astype(F32) + from_y[...].astype(F32)
    for k, out in enumerate(outs):
        value = total[k * rows : (k + 1) * rows]
        out[...] = encoded(value) if out.dtype == BF16 else value


def sum_kernel(*refs):
    total = refs[0][...]
    for ref in refs[1:-1]:
        total += ref[...].astype(F32)
    refs[-1][...] = encoded(total)


def join_kernel(*refs):
    rows = refs[0].shape[0]
    for k, ref in enumerate(refs[:-1]):
        refs[-1][k * rows : (k + 1) * rows, :] = ref[...]


def finish_kernel(scale, *refs):
    g_send, g_recv, g_update, g_decode, loss = refs[-5:]
    pieces = refs[:-5]
    width = g_send.shape[1]
    share = width // 32
    core, x, z, y = position()
    total = jnp.zeros((share, LANES), F32)
    for i, piece in enumerate(pieces):
        quarter = 2 * (core if i < 4 else 1 - core) + (x if i % 4 < 2 else 1 - x)
        for j in range(piece.shape[0] // share):
            start = (8 * quarter + lax.bitwise_xor(2 * z + y, 4 * (i % 2) + j)) * share
            place = pl.ds(pl.multiple_of(start, share), share)
            value = piece[j * share : (j + 1) * share, :].astype(F32)
            g_send[place, :] = value[:, :width]
            g_recv[place, :] = value[:, width : 2 * width]
            g_update[place, :] = value[:, 2 * width : 3 * width]
            g_decode[place, :] = value[:, 3 * width : -LANES]
            total += value[:, -LANES:]
    loss[0, 0] = jnp.sum(total) * scale


def position():
    ens, dom = lax.axis_index("ens"), lax.axis_index("dom")
    return lax.rem(ens, 2), lax.div(ens, 2), lax.div(dom, 2), lax.rem(dom, 2)


SCALAR = pl.BlockSpec(memory_space=pltpu.SMEM)


def meet(first, second):
    size = lax.axis_size("dom")
    second = lax.ppermute(second, "dom", [(i, (i + (1 if i % 2 else size - 1)) % size) for i in range(size)])
    return flip(first, "dom", 1), second


def flip(value, axis, bit):
    size = lax.axis_size(axis)
    return lax.ppermute(value, axis, [(i, i ^ bit) for i in range(size)])


def nbytes(arrays):
    return sum(x.size * x.dtype.itemsize for x in arrays)


def call(kernel, ins, outs, scratch=(), flops=0, room=4, in_hbm=0, out_hbm=0, limit=0):
    size = nbytes(list(ins) + list(outs))
    return pl.pallas_call(
        kernel,
        out_shape=outs,
        in_specs=vmem(len(ins) - in_hbm) + [HBM] * in_hbm,
        out_specs=vmem(len(outs) - out_hbm) + [HBM] * out_hbm,
        scratch_shapes=list(scratch),
        compiler_params=params(limit or 1.1 * size / MIB + room),
        cost_estimate=cost(flops, size),
    )(*ins)


def scalar(value):
    return jnp.reshape(value, (1,)).astype(jnp.int32)


def gathered(value):
    found = [value]
    bit = lax.axis_size("ens") // 2
    while bit:
        found = [x for v in found for x in (v, flip(v, "ens", bit))]
        bit //= 2
    return found


def summed(keep, send_first, send_rest):
    block, cols = send_first.shape
    half, share = block // 2, block // 4
    core = lambda v: flip(v, "ens", 1)
    over_x = lambda v: flip(v, "ens", 2)
    over_y = lambda v: flip(v, "dom", 1)
    piece = lambda rows: sds((rows, cols), BF16)
    first, rest = core(send_first), core(send_rest)
    by_x, by_y = call(corner_kernel, [keep, first], [piece(half)] * 2)
    by_x, by_y = over_x(by_x), over_y(by_y)
    to_x, to_y = call(sides_kernel, [keep, rest, by_x, by_y], [piece(block)] * 2)
    to_x, to_y = over_x(to_x), over_y(to_y)
    shares = call(shares_kernel, [keep, rest, to_x, to_y], [piece(share)] * 3 + [sds((share, cols), F32)])
    terms = [shares[3]] + [flip(shares[k - 1], "dom", 2 * k) for k in (1, 2, 3)]
    (own,) = call(sum_kernel, terms, [piece(share)])
    pieces = [own] + [flip(own, "dom", k) for k in range(1, 8)]
    here = [call(join_kernel, pieces[i : i + 4], [piece(block)])[0] for i in (0, 4)]
    here += [over_x(v) for v in here]
    return here + [core(v) for v in here]


def per_device(
    nodes, senders, send_next, send_prev, readout_vertex_list, dec_weights, base, observed_analysis,
    w_send, w_recv, vertex_refresh_matrix, w_decode,
):
    latent = nodes[0]
    count, width = latent.shape
    halo = send_next.shape[0]
    line_span, variables = base.shape
    degree = senders.shape[0]
    fan = readout_vertex_list.shape[0]
    ext_rows = count + 2 * halo
    members = lax.axis_size("ens")
    ens, dom = lax.axis_index("ens"), lax.axis_index("dom")
    to_next, to_prev = send_next.reshape(1, halo), send_prev.reshape(1, halo)

    held = lambda shape, dtype=BF16: pltpu.VMEM(shape, dtype)
    indices = lambda: [held((1, halo), jnp.int32)] * 2
    nodes_t, first_t, second_t = call(
        lend_kernel,
        [latent, to_next, to_prev],
        [sds((width, count), BF16), sds((width, halo), BF16), sds((width, halo), BF16)],
        [held((count, width))] + indices() + [pltpu.SemaphoreType.DMA((3,))],
        flops=4 * width * count * halo,
        in_hbm=3,
        limit=56,
    )
    from_first, from_second = meet(first_t, second_t)

    core = scalar(lax.rem(ens, 2))
    picked_t, field_t, first_t, second_t, slope_t, slope_sum_t, agg_t, upd_slope_t, hidden_t = call(
        forward_kernel,
        [nodes_t, from_first, from_second, senders, to_next, to_prev, w_send, w_recv, vertex_refresh_matrix, w_decode],
        [
            sds((width, degree * count), BF16), sds((variables, count), BF16), sds((variables, halo), BF16),
            sds((variables, halo), BF16), sds((width, degree * count), BF16), sds((width, count), F32),
            sds((width, count), BF16), sds((width, count), F32), sds((width, count), BF16),
        ],
        [held((width, degree * count), F32), held((degree, count), jnp.int32)] + indices() + [
            held((width, width)), held((width, width)), held((width, width)), held((width, variables)),
            held((width, count), F32), held((width, degree * count)), held((width, count), F32),
            held((width, count)), held((width, count), F32), held((width, count)),
            pltpu.SemaphoreType.DMA((7,)), pltpu.SemaphoreType.DMA((width // 128 + 4,)),
        ],
        flops=2 * degree * width * count * (ext_rows + width),
        in_hbm=7,
        out_hbm=5,
        limit=56,
    )
    lent = meet(first_t, second_t)
    mids = gathered(field_t)

    block = 512
    steps = line_span // 2 // block
    fixed = lambda shape: pl.BlockSpec(shape, lambda i, *at: (0,) * len(shape))
    tall = lambda rows: pl.BlockSpec((rows, block), lambda i, *at: (0, i))
    tall_half = lambda rows: pl.BlockSpec((rows, block), lambda i, at: (0, i + at[0] * steps))
    half_span = line_span // 2
    mat, base_t, truth_t = pl.pallas_call(
        decoder_kernel,
        grid_spec=pltpu.PrefetchScalarGridSpec(
            num_scalar_prefetch=1,
            grid=(steps,),
            in_specs=[tall_half(fan), tall_half(fan), HBM, HBM, pl.BlockSpec(memory_space=pl.ANY)],
            out_specs=[tall(2 * ext_rows), fixed((variables, half_span)), fixed((variables, half_span))],
            scratch_shapes=[held((half_span, variables)), held((half_span, variables)), pltpu.SemaphoreType.DMA((2,))],
        ),
        out_shape=[sds((2 * ext_rows, half_span), BF16)] + [sds((variables, half_span), BF16)] * 2,
        compiler_params=params(12),
        cost_estimate=cost(10 * ext_rows * half_span, 16e6),
    )(core, readout_vertex_list, dec_weights, base, observed_analysis, nodes_t)

    (end,) = call(borrowed_kernel, list(lent), [sds((variables, 2 * halo), BF16)])
    ends = gathered(end)

    grads = pl.pallas_call(
        functools.partial(readout_kernel, line_span),
        grid=(steps,),
        out_shape=[sds((variables, count), F32), sds((variables, 2 * halo), F32)] * 2 + [sds((8, block), F32)],
        in_specs=[fixed((variables, count))] * members + [fixed((variables, 2 * halo))] * members + [
            tall(2 * ext_rows), tall(variables), tall(variables),
        ],
        out_specs=[fixed((variables, count)), fixed((variables, 2 * halo))] * 2 + [fixed((8, block))],
        scratch_shapes=[
            pltpu.VMEM((members * variables, 2 * ext_rows), BF16), pltpu.VMEM((2 * variables, ext_rows), F32),
            pltpu.VMEM((members * variables, block), F32), pltpu.VMEM((2 * variables, block), BF16),
        ],
        compiler_params=params(20),
        cost_estimate=cost(4 * members * variables * ext_rows * half_span, 14e6),
    )(*mids, *ends, mat, base_t, truth_t)
    own_mid, own_end, pair_mid, pair_end, term = grads
    got_end = flip(pair_end, "ens", 1)
    got_mid = flip(pair_mid, "ens", 1)
    to_first, to_second = call(ends_kernel, [own_end, got_end], [sds((variables, halo), BF16)] * 2)
    from_first, from_second = meet(to_first, to_second)

    cols = 3 * width + variables + LANES
    operands = [
        own_mid, got_mid, from_first, from_second, to_next, to_prev, term, w_decode,
        vertex_refresh_matrix, nodes_t, picked_t, slope_t, slope_sum_t, agg_t, upd_slope_t, hidden_t,
    ]
    whole = sds((width, cols), F32)
    scratch = [held((width, count), F32), held((width, (degree + 1) * count))]
    flops = 2 * (degree + 3) * width * width * count
    scale = 1.0 / line_span
    if lax.axis_size("dom") != 8 or members != 4 or width % 512:
        (total,) = call(backward_kernel, operands, [whole], scratch, flops, room=16)
        total = lax.psum(total, ("ens", "dom"))
        cuts = [total[:, i * width : (i + 1) * width] for i in range(3)]
        return *cuts, total[:, 3 * width : -LANES], jnp.sum(total[:, -LANES:]) * scale
    block = width // 8
    parts = call(
        backward_kernel,
        operands,
        [sds((4 * block, cols), F32), sds((block, cols), BF16), sds((3 * block, cols), BF16)],
        [held(whole.shape, F32)] + scratch,
        flops,
        room=16,
    )
    pieces = summed(*parts)
    g_send, g_recv, g_update, g_decode, loss = pl.pallas_call(
        functools.partial(finish_kernel, scale),
        out_shape=[sds((width, width), F32)] * 3 + [sds((width, variables), F32), sds((1, 1), F32)],
        in_specs=vmem(len(pieces)),
        out_specs=vmem(4) + [SCALAR],
        compiler_params=params(14),
        cost_estimate=cost(0, 6 * width * cols),
    )(*pieces)
    return g_send, g_recv, g_update, g_decode, loss[0, 0]


def solution(mesh):
    return jax.shard_map(
        per_device,
        mesh=mesh,
        in_specs=(
            P("ens", "dom", None), P(None, "dom"), P("dom"), P("dom"), P(None, "dom"), P(None, "dom"),
            P("dom", None), P("dom", None), P(), P(), P(), P(),
        ),
        out_specs=(P(), P(), P(), P(), P()),
        check_vma=False,
    )
```

```python
import functools

import jax
import jax.numpy as jnp
from jax import lax
from jax.experimental import pallas as pl
from jax.experimental.pallas import tpu as pltpu
from jax.sharding import PartitionSpec as P

EPS = 0.04
F32 = jnp.float32
BF16 = jnp.bfloat16
MIB = 1024 * 1024


def dot(a, b, ca=1, cb=0):
    return lax.dot_general(a, b, (((ca,), (cb,)), ((), ())), preferred_element_type=F32)


def dot_nt(a, b):
    return dot(a, b, 1, 1)


def one_hot(rows, index_row):
    shape = (rows, index_row.shape[1])
    hit = lax.broadcasted_iota(jnp.int32, shape, 0) == index_row
    return jnp.where(hit, 1.0, 0.0).astype(BF16)


def params(mib):
    return pltpu.CompilerParams(vmem_limit_bytes=int(mib * MIB))


def vmem(n):
    return [pl.BlockSpec(memory_space=pltpu.VMEM)] * n


def cost(flops, size):
    return pl.CostEstimate(flops=int(flops), bytes_accessed=int(size), transcendentals=0)


def sds(shape, dtype):
    return jax.ShapeDtypeStruct(shape, dtype)


HBM = pl.BlockSpec(memory_space=pltpu.HBM)


def fetched(sources, targets, sems):
    copies = [pltpu.make_async_copy(a, b, sems.at[i]) for i, (a, b) in enumerate(zip(sources, targets))]
    for copy in copies:
        copy.start()
    return copies


def sides(next_side, prev_side):
    even = lax.rem(lax.axis_index("dom"), 2) == 0
    return jnp.where(even, next_side, prev_side), jnp.where(even, prev_side, next_side)


def lend_kernel(nodes, to_next, to_prev, nodes_t, first_t, second_t, held, rows_next, rows_prev, sems):
    for copy in fetched((nodes, to_next, to_prev), (held, rows_next, rows_prev), sems):
        copy.wait()
    table = held[...].T
    nodes_t[...] = table
    count = table.shape[1]
    first, second = sides(rows_next[...], rows_prev[...])
    first_t[...] = dot(table, one_hot(count, first)).astype(BF16)
    second_t[...] = dot(table, one_hot(count, second)).astype(BF16)


def decoder_kernel(core, vertices, weights, base, truth, after, mat, base_t, truth_t, done, base_rows, truth_rows, sems):
    del after
    done[...] = jnp.zeros_like(done)
    span = base_rows.shape[0]
    half = pl.ds(pl.multiple_of(core[0] * span, span), span)
    copies = [
        pltpu.make_async_copy(base.at[half, :], base_rows, sems.at[0]),
        pltpu.make_async_copy(truth.at[half, :], truth_rows, sems.at[1]),
    ]

    @pl.when(pl.program_id(0) == 0)
    def _():
        for copy in copies:
            copy.start()

    rows, tile = mat.shape[0] // 2, 16
    shape = (tile, mat.shape[1])
    spread = lambda ref, k: jnp.broadcast_to(ref[k : k + 1, :], shape)
    vertex = [spread(vertices, k) for k in range(vertices.shape[0])]
    weight = [spread(weights, k) for k in range(vertices.shape[0])]
    row = lax.broadcasted_iota(jnp.int32, shape, 0)

    for start in range(0, rows, tile):
        here = row + start
        total = jnp.where(here == vertex[0], weight[0], 0.0)
        for k in range(1, len(vertex)):
            total += jnp.where(here == vertex[k], weight[k], 0.0)
        hi, lo = split(total)
        mat[start : start + tile, :] = hi
        mat[rows + start : rows + start + tile, :] = lo

    @pl.when(pl.program_id(0) == pl.num_programs(0) - 1)
    def _():
        for copy in copies:
            copy.wait()
        base_t[...] = base_rows[...].T
        truth_t[...] = truth_rows[...].T


TILE = 16


def bent(half):
    t = jnp.tanh(half)
    u = half * t
    return half + u, (1.0 + t) * (1.0 + half - u)


def forward_kernel(
    nodes_in, from_first, from_second, senders_in, w_send_in, w_recv_in, to_next_in, to_prev_in, vertex_in, w_decode_in, after,
    field_t, first_t, second_t, picked_out, slope_out, slope_sum_out, agg_out, upd_slope_out, hidden_out,
    ext, senders, w_send, w_recv, to_next, to_prev, vertex, w_decode, picked_t, recv_t,
    slope_t, slope_sum_t, agg_t, upd_slope_t, hidden_t, pre, in_sems, out_sems,
):
    del after
    degree, count = senders.shape
    width, ext_rows = ext.shape
    halo = from_first.shape[1]
    swap = lax.rem(lax.axis_index("dom"), 2) * halo
    column = lambda start: ext.at[:, pl.ds(pl.multiple_of(start, 128), halo)]
    fetch = fetched(
        (nodes_in, from_first, from_second, senders_in, w_recv_in, w_send_in, vertex_in, to_next_in, to_prev_in, w_decode_in),
        (
            ext.at[:, :count], column(count + halo - swap), column(count + swap),
            senders, w_recv, w_send, vertex, to_next, to_prev, w_decode,
        ),
        in_sems,
    )
    stored = []

    def store(source, target):
        copy = pltpu.make_async_copy(source, target, out_sems.at[len(stored)])
        copy.start()
        stored.append(copy)

    for copy in fetch[:6]:
        copy.wait()
    recv_t[...] = dot(w_recv[...].T, ext[:, :count]) * 0.5
    w_send_t = w_send[...].T * 0.5
    for k in range(degree):
        here = slice(k * count, (k + 1) * count)
        picked_t[:, here] = dot(ext[...], one_hot(ext_rows, senders[k : k + 1, :])).astype(BF16)
        pre[:, here] = dot(w_send_t, picked_t[:, here])
    store(picked_t, picked_out)
    for copy in fetch[6:]:
        copy.wait()
    for start in range(0, width, TILE):
        rows = slice(start, start + TILE)
        recv = recv_t[rows, :]
        total = slopes = None
        for k in range(degree):
            here = slice(k * count, (k + 1) * count)
            value, slope = bent(pre[rows, here] + recv)
            slope_t[rows, here] = slope.astype(BF16)
            total = value if k == 0 else total + value
            slopes = slope if k == 0 else slopes + slope
        slope_sum_t[rows, :] = slopes
        agg_t[rows, :] = (total * (1.0 / degree)).astype(BF16)
        if (start + TILE) % 128 == 0:
            group = slice(start + TILE - 128, start + TILE)
            store(slope_t.at[group, :], slope_out.at[group, :])
    store(slope_sum_t, slope_sum_out)
    store(agg_t, agg_out)
    pre[:, :count] = dot(vertex[...].T * 0.5, agg_t[...])
    for start in range(0, width, TILE):
        rows = slice(start, start + TILE)
        value, slope = bent(pre[rows, :count])
        upd_slope_t[rows, :] = slope * 0.5
        hidden_t[rows, :] = (ext[rows, :count].astype(F32) + value).astype(BF16)
    store(upd_slope_t, upd_slope_out)
    store(hidden_t, hidden_out)
    field = dot(w_decode[...].T, hidden_t[...]).astype(BF16)
    field_t[...] = field
    first, second = sides(to_next[...], to_prev[...])
    first_t[...] = dot(field, one_hot(count, first)).astype(BF16)
    second_t[...] = dot(field, one_hot(count, second)).astype(BF16)
    for copy in stored:
        copy.wait()


def readout_kernel(line_span, *refs):
    mids, ends = refs[0:4], refs[4:8]
    mat, base_t, truth_t = refs[8:11]
    own_mid, own_end, pair_mid, pair_end, loss = refs[11:16]
    table, grad = refs[16:18]
    states, slopes = refs[18:20], refs[20:22]
    step = pl.program_id(0)
    members = len(mids)
    variables, count = own_mid.shape
    ext_rows = grad.shape[1]

    @pl.when(step == 0)
    def _():
        grad[...] = jnp.zeros_like(grad)
        loss[...] = jnp.zeros_like(loss)
        for m in range(members):
            for base in (0, ext_rows):
                table[m * variables : (m + 1) * variables, base : base + count] = mids[m][...]
                table[m * variables : (m + 1) * variables, base + count : base + ext_rows] = ends[m][...]

    wide = states[0].shape[1]
    for i, state in enumerate(states):
        state[...] = dot(table[...], mat[:, i * wide : (i + 1) * wide])

    def bend(diff):
        square = diff * diff + EPS
        inverse = lax.rsqrt(square)
        return square * inverse, diff * inverse

    alone = EPS**0.5
    for i, (state, slope_out) in enumerate(zip(states, slopes)):
        cols = slice(i * wide, (i + 1) * wide)
        summed = jnp.zeros((8, wide), F32)
        for start in range(0, variables, TILE):
            rows = slice(start, start + TILE)
            ready = base_t[rows, cols].astype(F32)
            truth = truth_t[rows, cols].astype(F32)
            x = [
                (state[m * variables + start : m * variables + start + TILE, :] + ready).astype(BF16).astype(F32)
                for m in range(members)
            ]
            apart = [alone, alone]
            pull = [0.0, 0.0]
            for m in range(2):
                for j in range(m + 1, members):
                    size, slope = bend(x[m] - x[j])
                    apart[m] = apart[m] + size
                    pull[m] = pull[m] + slope
                    if j < 2:
                        apart[j] = apart[j] + size
                        pull[j] = pull[j] - slope
            near = 0.0
            for m in range(2):
                size, push = bend(x[m] - truth)
                near = near + size
                slope = push * (1.0 / members / line_span) - pull[m] * (1.0 / (members * (members - 1.0)) / line_span)
                slope_out[m * variables + start : m * variables + start + TILE, :] = slope.astype(BF16)
            term = near * (1.0 / members) - (apart[0] + apart[1]) * (1.0 / (2.0 * members * (members - 1)))
            summed += term[:8] + term[8:]
        loss[:, cols] += summed
        grad[...] += dot_nt(slope_out[...], mat[:ext_rows, cols])

    @pl.when(step == pl.num_programs(0) - 1)
    def _():
        for i, (mid, end) in enumerate(((own_mid, own_end), (pair_mid, pair_end))):
            rows = slice(i * variables, (i + 1) * variables)
            mid[...] = grad[rows, :count]
            end[...] = grad[rows, count:]


def borrowed_kernel(first, second, end):
    halo = first.shape[1]
    from_next, from_prev = sides(first[...], second[...])
    end[:, :halo] = from_prev
    end[:, halo:] = from_next


def ends_kernel(mine, got, first, second):
    halo = first.shape[1]
    total = mine[...] + got[...]
    to_first, to_second = sides(total[:, halo:], total[:, :halo])
    first[...] = to_first.astype(BF16)
    second[...] = to_second.astype(BF16)


def split(value):
    hi = value.astype(BF16)
    return hi, (value - hi.astype(F32)).astype(BF16)


LANES = 128


def encoded(total):
    tile = total[:, -LANES:]
    value = tile + pltpu.roll(tile, LANES // 2, 1)
    hi = value.astype(BF16).astype(F32)
    lane = lax.broadcasted_iota(jnp.int32, tile.shape, 1)
    tile = jnp.where(lane < LANES // 2, hi, value - hi)
    return jnp.concatenate([total[:, :-LANES].astype(BF16), tile.astype(BF16)], axis=1)


def backward_kernel(
    own_mid, pair_mid, from_first, from_second, to_next, to_prev, term, w_decode, vertex, nodes_t,
    picked_t, slope_t, slope_sum_t, agg_t, upd_slope_t, hidden_t,
    *refs,
):
    whole, back, grad_pre = refs[-3:]
    count = nodes_t.shape[1]
    width = nodes_t.shape[0]
    grad_z = own_mid[...] + pair_mid[...]
    for got, rows in zip((from_first, from_second), sides(to_next[...], to_prev[...])):
        grad_z += dot_nt(got[...], one_hot(count, rows))
    grad_z = grad_z.astype(BF16)
    main = whole.shape[1] - LANES
    whole[:, 3 * width : main] = dot_nt(hidden_t[...], grad_z)
    grad_upd = (dot(w_decode[...], grad_z) * upd_slope_t[...]).astype(BF16)
    whole[:, 2 * width : 3 * width] = dot_nt(agg_t[...], grad_upd)
    degree = slope_t.shape[1] // count
    back[...] = dot(vertex[...], grad_upd)
    for start in range(0, width, TILE):
        rows = slice(start, start + TILE)
        grad_agg = back[rows, :] * (0.5 / degree)
        grad_pre[rows, degree * count :] = (grad_agg * slope_sum_t[rows, :]).astype(BF16)
        for k in range(degree):
            here = slice(k * count, (k + 1) * count)
            grad_pre[rows, here] = (grad_agg * slope_t[rows, here].astype(F32)).astype(BF16)
    whole[:, width : 2 * width] = dot_nt(nodes_t[...], grad_pre[:, degree * count :])
    whole[:, :width] = dot_nt(picked_t[...], grad_pre[:, : degree * count])
    whole[:, main:] = jnp.zeros((width, LANES), F32)
    spot = (lax.broadcasted_iota(jnp.int32, (8, LANES), 0) == 0) & (lax.broadcasted_iota(jnp.int32, (8, LANES), 1) == 0)
    whole[0:8, main:] = jnp.where(spot, jnp.sum(term[...]), 0.0)
    if len(refs) == 3:
        return
    keep, send_first, send_rest = refs[:3]
    core, x, dom = position()
    share = width // 32

    def block(c, other, k):
        quarter = 2 * c + (1 - x if other else x)
        start = (8 * quarter + lax.bitwise_xor(dom, k)) * share
        return whole[pl.ds(pl.multiple_of(start, share), share), :]

    order = [(1, k) for k in (4, 5, 6, 7)]
    order += [(other, k) for k in (1, 2, 3) for other in (1, 0)]
    order += [(0, k) for k in (4, 5, 6, 7)] + [(1, 0), (0, 0)]
    for i, (other, k) in enumerate(order):
        keep[i * share : (i + 1) * share, :] = block(core, other, k)
        value = encoded(block(1 - core, other, k))
        if i < 4:
            send_first[i * share : (i + 1) * share, :] = value
        else:
            send_rest[(i - 4) * share : (i - 3) * share, :] = value


def far_kernel(keep, first, out):
    out[...] = encoded(keep[: out.shape[0], :] + first[...].astype(F32))


def pairs_kernel(keep, rest, *outs):
    rows = outs[0].shape[0]
    for k, out in enumerate(outs):
        out[...] = encoded(keep[(k + 2) * rows : (k + 3) * rows, :] + rest[k * rows : (k + 1) * rows, :].astype(F32))


def quads_kernel(keep, rest, far, *outs):
    rows = outs[0].shape[0]
    for k, out in enumerate(outs):
        total = keep[(k + 10) * rows : (k + 11) * rows, :] + rest[(k + 6) * rows : (k + 7) * rows, :].astype(F32)
        out[...] = encoded(total + far[k * rows : (k + 1) * rows, :].astype(F32))


def across_kernel(keep, rest, *refs):
    out = refs[-1]
    rows = out.shape[0]
    total = keep[14 * rows : 15 * rows, :] + rest[10 * rows : 11 * rows, :].astype(F32)
    for ref in refs[:-1]:
        total += ref[:rows, :].astype(F32)
    out[...] = encoded(total)


def own_kernel(keep, rest, *refs):
    out = refs[-1]
    rows = out.shape[0]
    total = keep[15 * rows :, :] + rest[11 * rows :, :].astype(F32)
    for ref in refs[:-1]:
        total += ref[ref.shape[0] - rows :, :].astype(F32)
    out[...] = encoded(total)


def join_kernel(*refs):
    start = 0
    for ref in refs[:-1]:
        refs[-1][start : start + ref.shape[0], :] = ref[...]
        start += ref.shape[0]


def pair_kernel(mine, other, after, out):
    del after
    rows = mine.shape[0]
    out[:rows, :] = mine[...]
    out[rows:, :] = other[...]


def finish_kernel(scale, *refs):
    g_send, g_recv, g_update, g_decode, loss = refs[-5:]
    pieces = refs[:-5]
    width = g_send.shape[1]
    share = width // 32
    core, x, dom = position()
    total = jnp.zeros((share, LANES), F32)
    for i, piece in enumerate(pieces):
        for j in range(piece.shape[0] // share):
            if i % 3 == 0:
                other, k = j % 2, j // 2
            else:
                other, k = i % 3 - 1, 4 + j
            quarter = 2 * (core if i < 3 else 1 - core) + (1 - x if other else x)
            start = (8 * quarter + lax.bitwise_xor(dom, k)) * share
            place = pl.ds(pl.multiple_of(start, share), share)
            value = piece[j * share : (j + 1) * share, :].astype(F32)
            g_send[place, :] = value[:, :width]
            g_recv[place, :] = value[:, width : 2 * width]
            g_update[place, :] = value[:, 2 * width : 3 * width]
            g_decode[place, :] = value[:, 3 * width : -LANES]
            total += value[:, -LANES:]
    loss[0, 0] = jnp.sum(total) * scale


def position():
    ens = lax.axis_index("ens")
    return lax.rem(ens, 2), lax.div(ens, 2), lax.axis_index("dom")


SCALAR = pl.BlockSpec(memory_space=pltpu.SMEM)


def meet(first, second):
    size = lax.axis_size("dom")
    second = lax.ppermute(second, "dom", [(i, (i + (1 if i % 2 else size - 1)) % size) for i in range(size)])
    return flip(first, "dom", 1), second


def flip(value, axis, bit):
    size = lax.axis_size(axis)
    return lax.ppermute(value, axis, [(i, i ^ bit) for i in range(size)])


def nbytes(arrays):
    return sum(x.size * x.dtype.itemsize for x in arrays)


def call(kernel, ins, outs, scratch=(), flops=0, room=4, in_hbm=0, out_hbm=0, limit=0):
    size = nbytes(list(ins) + list(outs))
    return pl.pallas_call(
        kernel,
        out_shape=outs,
        in_specs=vmem(len(ins) - in_hbm) + [HBM] * in_hbm,
        out_specs=vmem(len(outs) - out_hbm) + [HBM] * out_hbm,
        scratch_shapes=list(scratch),
        compiler_params=params(limit or 1.1 * size / MIB + room),
        cost_estimate=cost(flops, size),
    )(*ins)


def scalar(value):
    return jnp.reshape(value, (1,)).astype(jnp.int32)


def gathered(value):
    found = [value]
    bit = lax.axis_size("ens") // 2
    while bit:
        found = [x for v in found for x in (v, flip(v, "ens", bit))]
        bit //= 2
    return found


def summed(keep, send_first, send_rest):
    cols = keep.shape[1]
    share = keep.shape[0] // 16
    core = lambda v: flip(v, "ens", 1)
    over_x = lambda v: flip(v, "ens", 2)
    piece = lambda shares: sds((shares * share, cols), BF16)
    near, far = (1, 2, 3), (4, 5, 6, 7)
    first, rest = core(send_first), core(send_rest)
    (out,) = call(far_kernel, [keep, first], [piece(4)])
    from_x = over_x(out)
    outs = call(pairs_kernel, [keep, rest], [piece(2)] * 3)
    pairs = [flip(v, "dom", k) for k, v in zip(near, outs)]
    outs = call(quads_kernel, [keep, rest, from_x], [piece(1)] * 4)
    quads = [flip(v, "dom", k) for k, v in zip(far, outs)]
    (out,) = call(across_kernel, [keep, rest] + pairs, [piece(1)])
    got = over_x(out)
    (own,) = call(own_kernel, [keep, rest] + pairs + quads + [got], [piece(1)])

    (far_own,) = call(join_kernel, [flip(own, "dom", k) for k in far], [piece(4)])
    (pair,) = call(pair_kernel, [own, over_x(own), far_own], [piece(2)])
    (close,) = call(join_kernel, [pair] + [flip(pair, "dom", k) for k in near], [piece(8)])
    here = [close, far_own, over_x(far_own)]
    return here + [core(v) for v in here]


def per_device(
    nodes, senders, send_next, send_prev, readout_vertex_list, dec_weights, base, observed_analysis,
    w_send, w_recv, vertex_refresh_matrix, w_decode,
):
    latent = nodes[0]
    count, width = latent.shape
    halo = send_next.shape[0]
    line_span, variables = base.shape
    degree = senders.shape[0]
    fan = readout_vertex_list.shape[0]
    ext_rows = count + 2 * halo
    members = lax.axis_size("ens")
    ens, dom = lax.axis_index("ens"), lax.axis_index("dom")
    to_next, to_prev = send_next.reshape(1, halo), send_prev.reshape(1, halo)

    held = lambda shape, dtype=BF16: pltpu.VMEM(shape, dtype)
    indices = lambda: [held((1, halo), jnp.int32)] * 2
    nodes_t, first_t, second_t = call(
        lend_kernel,
        [latent, to_next, to_prev],
        [sds((width, count), BF16), sds((width, halo), BF16), sds((width, halo), BF16)],
        [held((count, width))] + indices() + [pltpu.SemaphoreType.DMA((3,))],
        flops=4 * width * count * halo,
        in_hbm=3,
        limit=56,
    )
    from_first, from_second = meet(first_t, second_t)

    core = scalar(lax.rem(ens, 2))
    block = 512
    steps = line_span // 2 // block
    fixed = lambda shape: pl.BlockSpec(shape, lambda i, *at: (0,) * len(shape))
    tall = lambda rows: pl.BlockSpec((rows, block), lambda i, *at: (0, i))
    tall_half = lambda rows: pl.BlockSpec((rows, block), lambda i, at: (0, i + at[0] * steps))
    half_span = line_span // 2
    mat, base_t, truth_t, done = pl.pallas_call(
        decoder_kernel,
        grid_spec=pltpu.PrefetchScalarGridSpec(
            num_scalar_prefetch=1,
            grid=(steps,),
            in_specs=[tall_half(fan), tall_half(fan), HBM, HBM, pl.BlockSpec(memory_space=pl.ANY)],
            out_specs=[tall(2 * ext_rows), fixed((variables, half_span)), fixed((variables, half_span)), fixed((8, 128))],
            scratch_shapes=[held((half_span, variables)), held((half_span, variables)), pltpu.SemaphoreType.DMA((2,))],
        ),
        out_shape=[sds((2 * ext_rows, half_span), BF16)] + [sds((variables, half_span), BF16)] * 2 + [sds((8, 128), F32)],
        compiler_params=params(56),
        cost_estimate=cost(10 * ext_rows * half_span, 16e6),
    )(core, readout_vertex_list, dec_weights, base, observed_analysis, nodes_t)

    field_t, first_t, second_t, picked_t, slope_t, slope_sum_t, agg_t, upd_slope_t, hidden_t = call(
        forward_kernel,
        [nodes_t, from_first, from_second, senders, w_send, w_recv, to_next, to_prev, vertex_refresh_matrix, w_decode, done],
        [
            sds((variables, count), BF16), sds((variables, halo), BF16), sds((variables, halo), BF16),
            sds((width, degree * count), BF16), sds((width, degree * count), BF16), sds((width, count), F32),
            sds((width, count), BF16), sds((width, count), F32), sds((width, count), BF16),
        ],
        [held((width, ext_rows)), held((degree, count), jnp.int32), held((width, width)), held((width, width))] + indices() + [
            held((width, width)), held((width, variables)), held((width, degree * count)), held((width, count), F32),
            held((width, degree * count)), held((width, count), F32), held((width, count)), held((width, count), F32),
            held((width, count)), held((width, degree * count), F32),
            pltpu.SemaphoreType.DMA((10,)), pltpu.SemaphoreType.DMA((width // 128 + 5,)),
        ],
        flops=2 * degree * width * count * (ext_rows + width),
        in_hbm=11,
        out_hbm=6,
        limit=56,
    )
    lent = meet(first_t, second_t)
    mids = gathered(field_t)

    (end,) = call(borrowed_kernel, list(lent), [sds((variables, 2 * halo), BF16)])
    ends = gathered(end)

    grads = pl.pallas_call(
        functools.partial(readout_kernel, line_span),
        grid=(steps,),
        out_shape=[sds((variables, count), F32), sds((variables, 2 * halo), F32)] * 2 + [sds((8, block), F32)],
        in_specs=[fixed((variables, count))] * members + [fixed((variables, 2 * halo))] * members + [
            tall(2 * ext_rows), tall(variables), tall(variables),
        ],
        out_specs=[fixed((variables, count)), fixed((variables, 2 * halo))] * 2 + [fixed((8, block))],
        scratch_shapes=[
            pltpu.VMEM((members * variables, 2 * ext_rows), BF16), pltpu.VMEM((2 * variables, ext_rows), F32),
            *[pltpu.VMEM((members * variables, 256), F32)] * (block // 256),
            *[pltpu.VMEM((2 * variables, 256), BF16)] * (block // 256),
        ],
        compiler_params=params(20),
        cost_estimate=cost(4 * members * variables * ext_rows * half_span, 14e6),
    )(*mids, *ends, mat, base_t, truth_t)
    own_mid, own_end, pair_mid, pair_end, term = grads
    got_end = flip(pair_end, "ens", 1)
    got_mid = flip(pair_mid, "ens", 1)
    to_first, to_second = call(ends_kernel, [own_end, got_end], [sds((variables, halo), BF16)] * 2)
    from_first, from_second = meet(to_first, to_second)

    cols = 3 * width + variables + LANES
    operands = [
        own_mid, got_mid, from_first, from_second, to_next, to_prev, term, w_decode,
        vertex_refresh_matrix, nodes_t, picked_t, slope_t, slope_sum_t, agg_t, upd_slope_t, hidden_t,
    ]
    whole = sds((width, cols), F32)
    scratch = [held((width, count), F32), held((width, (degree + 1) * count))]
    flops = 2 * (degree + 3) * width * width * count
    scale = 1.0 / line_span
    if lax.axis_size("dom") != 8 or members != 4 or width % 512:
        (total,) = call(backward_kernel, operands, [whole], scratch, flops, room=16)
        total = lax.psum(total, ("ens", "dom"))
        cuts = [total[:, i * width : (i + 1) * width] for i in range(3)]
        return *cuts, total[:, 3 * width : -LANES], jnp.sum(total[:, -LANES:]) * scale
    block = width // 8
    parts = call(
        backward_kernel,
        operands,
        [sds((4 * block, cols), F32), sds((block, cols), BF16), sds((3 * block, cols), BF16)],
        [held(whole.shape, F32)] + scratch,
        flops,
        room=16,
    )
    pieces = summed(*parts)
    g_send, g_recv, g_update, g_decode, loss = pl.pallas_call(
        functools.partial(finish_kernel, scale),
        out_shape=[sds((width, width), F32)] * 3 + [sds((width, variables), F32), sds((1, 1), F32)],
        in_specs=vmem(len(pieces)),
        out_specs=vmem(4) + [SCALAR],
        compiler_params=params(14),
        cost_estimate=cost(0, 6 * width * cols),
    )(*pieces)
    return g_send, g_recv, g_update, g_decode, loss[0, 0]


def solution(mesh):
    return jax.shard_map(
        per_device,
        mesh=mesh,
        in_specs=(
            P("ens", "dom", None), P(None, "dom"), P("dom"), P("dom"), P(None, "dom"), P(None, "dom"),
            P("dom", None), P("dom", None), P(), P(), P(), P(),
        ),
        out_specs=(P(), P(), P(), P(), P()),
        check_vma=False,
    )
```

```python
import functools

import jax
import jax.numpy as jnp
from jax import lax
from jax.experimental import pallas as pl
from jax.experimental.pallas import tpu as pltpu
from jax.sharding import PartitionSpec as P

EPS = 0.04
F32 = jnp.float32
BF16 = jnp.bfloat16
MIB = 1024 * 1024


def dot(a, b, ca=1, cb=0):
    return lax.dot_general(a, b, (((ca,), (cb,)), ((), ())), preferred_element_type=F32)


def dot_nt(a, b):
    return dot(a, b, 1, 1)


def one_hot(rows, index_row):
    shape = (rows, index_row.shape[1])
    hit = lax.broadcasted_iota(jnp.int32, shape, 0) == index_row
    return jnp.where(hit, 1.0, 0.0).astype(BF16)


def params(mib):
    return pltpu.CompilerParams(vmem_limit_bytes=int(mib * MIB))


def vmem(n):
    return [pl.BlockSpec(memory_space=pltpu.VMEM)] * n


def cost(flops, size):
    return pl.CostEstimate(flops=int(flops), bytes_accessed=int(size), transcendentals=0)


def sds(shape, dtype):
    return jax.ShapeDtypeStruct(shape, dtype)


HBM = pl.BlockSpec(memory_space=pltpu.HBM)


def fetched(sources, targets, sems):
    copies = [pltpu.make_async_copy(a, b, sems.at[i]) for i, (a, b) in enumerate(zip(sources, targets))]
    for copy in copies:
        copy.start()
    return copies


def sides(next_side, prev_side):
    even = lax.rem(lax.axis_index("dom"), 2) == 0
    return jnp.where(even, next_side, prev_side), jnp.where(even, prev_side, next_side)


def lend_kernel(nodes, to_next, to_prev, nodes_t, first_t, second_t, held, rows_next, rows_prev, sems):
    for copy in fetched((nodes, to_next, to_prev), (held, rows_next, rows_prev), sems):
        copy.wait()
    table = held[...].T
    nodes_t[...] = table
    count = table.shape[1]
    first, second = sides(rows_next[...], rows_prev[...])
    first_t[...] = dot(table, one_hot(count, first)).astype(BF16)
    second_t[...] = dot(table, one_hot(count, second)).astype(BF16)


def decoder_kernel(core, vertices, weights, base, truth, after, mat, base_t, truth_t, done, base_rows, truth_rows, sems):
    del after
    done[...] = jnp.zeros_like(done)
    span = base_rows.shape[0]
    half = pl.ds(pl.multiple_of(core[0] * span, span), span)
    copies = [
        pltpu.make_async_copy(base.at[half, :], base_rows, sems.at[0]),
        pltpu.make_async_copy(truth.at[half, :], truth_rows, sems.at[1]),
    ]

    @pl.when(pl.program_id(0) == 0)
    def _():
        for copy in copies:
            copy.start()

    rows, lanes = mat.shape[0] // 2, 256
    row = lax.broadcasted_iota(jnp.int32, (8, lanes), 0)
    for left in range(0, mat.shape[1], lanes):
        cols = slice(left, left + lanes)
        spread = lambda ref, k: jnp.broadcast_to(ref[k : k + 1, cols], (8, lanes))
        ahead = [spread(vertices, k) - row for k in range(vertices.shape[0])]
        weight = [spread(weights, k) for k in range(vertices.shape[0])]

        def weighted(start):
            total = jnp.where(ahead[0] == start, weight[0], 0.0)
            for k in range(1, len(ahead)):
                total += jnp.where(ahead[k] == start, weight[k], 0.0)
            return total

        for start in range(0, rows, 16):
            hi, lo = split(jnp.concatenate([weighted(start), weighted(start + 8)], axis=0))
            mat[start : start + 16, cols] = hi
            mat[rows + start : rows + start + 16, cols] = lo

    step, block = pl.program_id(0), mat.shape[1]

    @pl.when(step == 0)
    def _():
        for copy in copies:
            copy.wait()

    some = pl.ds(pl.multiple_of(step * block, block), block)
    base_t[...] = base_rows[some, :].T
    truth_t[...] = truth_rows[some, :].T


TILE = 16


def bent(half):
    t = jnp.tanh(half)
    u = half * t
    return half + u, (1.0 + t) * (1.0 + half - u)


def forward_kernel(
    nodes_in, from_first, from_second, senders_in, w_send_in, w_recv_in, to_next_in, to_prev_in, vertex_in, w_decode_in, after,
    field_out, first_out, second_out, picked_out, slope_out, slope_sum_out, agg_out, upd_slope_out, hidden_out,
    ext, senders, w_send, w_recv, to_next, to_prev, vertex, w_decode, picked_t, recv_t,
    slope_t, slope_sum_t, agg_t, upd_slope_t, hidden_t, pre, field_t, first_t, second_t, in_sems, out_sems,
):
    del after
    degree, count = senders.shape
    width, ext_rows = ext.shape
    halo = from_first.shape[1]
    swap = lax.rem(lax.axis_index("dom"), 2) * halo
    column = lambda start: ext.at[:, pl.ds(pl.multiple_of(start, 128), halo)]
    fetch = fetched(
        (nodes_in, from_first, from_second, senders_in, w_recv_in, w_send_in, vertex_in, to_next_in, to_prev_in, w_decode_in),
        (
            ext.at[:, :count], column(count + halo - swap), column(count + swap),
            senders, w_recv, w_send, vertex, to_next, to_prev, w_decode,
        ),
        in_sems,
    )
    stored = []

    def store(source, target):
        copy = pltpu.make_async_copy(source, target, out_sems.at[len(stored)])
        copy.start()
        stored.append(copy)

    for copy in fetch[:4]:
        copy.wait()
    for k in range(degree):
        here = slice(k * count, (k + 1) * count)
        picked_t[:, here] = dot(ext[...], one_hot(ext_rows, senders[k : k + 1, :])).astype(BF16)
        store(picked_t.at[:, here], picked_out.at[:, here])
        if k == 0:
            for copy in fetch[4:]:
                copy.wait()
            w_send_t = w_send[...].T * 0.5
        pre[:, here] = dot(w_send_t, picked_t[:, here])
    recv_t[...] = dot(w_recv[...].T, ext[:, :count]) * 0.5
    for start in range(0, width, TILE):
        rows = slice(start, start + TILE)
        recv = recv_t[rows, :]
        total = slopes = None
        for k in range(degree):
            here = slice(k * count, (k + 1) * count)
            value, slope = bent(pre[rows, here] + recv)
            slope_t[rows, here] = slope.astype(BF16)
            total = value if k == 0 else total + value
            slopes = slope if k == 0 else slopes + slope
        slope_sum_t[rows, :] = slopes
        agg_t[rows, :] = (total * (1.0 / degree)).astype(BF16)
        if (start + TILE) % 128 == 0:
            group = slice(start + TILE - 128, start + TILE)
            store(slope_t.at[group, :], slope_out.at[group, :])
    store(slope_sum_t, slope_sum_out)
    store(agg_t, agg_out)
    pre[:, :count] = dot(vertex[...].T * 0.5, agg_t[...])
    for start in range(0, width, TILE):
        rows = slice(start, start + TILE)
        value, slope = bent(pre[rows, :count])
        upd_slope_t[rows, :] = slope * 0.5
        hidden_t[rows, :] = (ext[rows, :count].astype(F32) + value).astype(BF16)
    store(hidden_t, hidden_out)
    store(upd_slope_t, upd_slope_out)
    field = dot(w_decode[...].T, hidden_t[...]).astype(BF16)
    field_t[...] = field
    first, second = sides(to_next[...], to_prev[...])
    first_t[...] = dot(field, one_hot(count, first)).astype(BF16)
    second_t[...] = dot(field, one_hot(count, second)).astype(BF16)
    store(field_t, field_out)
    store(first_t, first_out)
    store(second_t, second_out)
    for copy in stored:
        copy.wait()


def readout_kernel(line_span, *refs):
    mids, ends = refs[0:4], refs[4:8]
    mat, base_t, truth_t = refs[8:11]
    own_mid, own_end, pair_mid, pair_end, loss = refs[11:16]
    table, grad = refs[16:18]
    subs = (len(refs) - 18) // 2
    states, slopes = refs[18 : 18 + subs], refs[18 + subs :]
    step = pl.program_id(0)
    members = len(mids)
    variables, count = own_mid.shape
    ext_rows = grad.shape[1]

    @pl.when(step == 0)
    def _():
        grad[...] = jnp.zeros_like(grad)
        loss[...] = jnp.zeros_like(loss)
        for m in range(members):
            for base in (0, ext_rows):
                table[m * variables : (m + 1) * variables, base : base + count] = mids[m][...]
                table[m * variables : (m + 1) * variables, base + count : base + ext_rows] = ends[m][...]

    wide = states[0].shape[1]
    for i, state in enumerate(states):
        state[...] = dot(table[...], mat[:, i * wide : (i + 1) * wide])

    def bend(diff):
        square = diff * diff + EPS
        inverse = lax.rsqrt(square)
        return square * inverse, diff * inverse

    alone = EPS**0.5
    for i, (state, slope_out) in enumerate(zip(states, slopes)):
        cols = slice(i * wide, (i + 1) * wide)
        summed = jnp.zeros((8, wide), F32)
        for start in range(0, variables, TILE):
            rows = slice(start, start + TILE)
            ready = base_t[rows, cols].astype(F32)
            truth = truth_t[rows, cols].astype(F32)
            x = [
                (state[m * variables + start : m * variables + start + TILE, :] + ready).astype(BF16).astype(F32)
                for m in range(members)
            ]
            apart = [alone, alone]
            pull = [0.0, 0.0]
            for m in range(2):
                for j in range(m + 1, members):
                    size, slope = bend(x[m] - x[j])
                    apart[m] = apart[m] + size
                    pull[m] = pull[m] + slope
                    if j < 2:
                        apart[j] = apart[j] + size
                        pull[j] = pull[j] - slope
            near = 0.0
            for m in range(2):
                size, push = bend(x[m] - truth)
                near = near + size
                slope = push * (1.0 / members / line_span) - pull[m] * (1.0 / (members * (members - 1.0)) / line_span)
                slope_out[m * variables + start : m * variables + start + TILE, :] = slope.astype(BF16)
            term = near * (1.0 / members) - (apart[0] + apart[1]) * (1.0 / (2.0 * members * (members - 1)))
            summed += term[:8] + term[8:]
        loss[:, cols] += summed
        grad[...] += dot_nt(slope_out[...], mat[:ext_rows, cols])

    @pl.when(step == pl.num_programs(0) - 1)
    def _():
        for i, (mid, end) in enumerate(((own_mid, own_end), (pair_mid, pair_end))):
            rows = slice(i * variables, (i + 1) * variables)
            mid[...] = grad[rows, :count]
            end[...] = grad[rows, count:]


def borrowed_kernel(first, second, end):
    halo = first.shape[1]
    from_next, from_prev = sides(first[...], second[...])
    end[:, :halo] = from_prev
    end[:, halo:] = from_next


def ends_kernel(mine, got, first, second):
    halo = first.shape[1]
    total = mine[...] + got[...]
    to_first, to_second = sides(total[:, halo:], total[:, :halo])
    first[...] = to_first.astype(BF16)
    second[...] = to_second.astype(BF16)


def split(value):
    hi = value.astype(BF16)
    return hi, (value - hi.astype(F32)).astype(BF16)


LANES = 128


def encoded(total):
    tile = total[:, -LANES:]
    value = tile + pltpu.roll(tile, LANES // 2, 1)
    hi = value.astype(BF16).astype(F32)
    lane = lax.broadcasted_iota(jnp.int32, tile.shape, 1)
    tile = jnp.where(lane < LANES // 2, hi, value - hi)
    return jnp.concatenate([total[:, :-LANES].astype(BF16), tile.astype(BF16)], axis=1)


def backward_kernel(
    own_mid, pair_mid, from_first, from_second, to_next, to_prev, term, w_decode, vertex, nodes_t,
    picked_t, slope_t, slope_sum_t, agg_t, upd_slope_t, hidden_t,
    *refs,
):
    whole, back, grad_pre = refs[-3:]
    count = nodes_t.shape[1]
    width = nodes_t.shape[0]
    grad_z = own_mid[...] + pair_mid[...]
    for got, rows in zip((from_first, from_second), sides(to_next[...], to_prev[...])):
        grad_z += dot_nt(got[...], one_hot(count, rows))
    grad_z = grad_z.astype(BF16)
    main = whole.shape[1] - LANES
    whole[:, 3 * width : main] = dot_nt(hidden_t[...], grad_z)
    grad_upd = (dot(w_decode[...], grad_z) * upd_slope_t[...]).astype(BF16)
    whole[:, 2 * width : 3 * width] = dot_nt(agg_t[...], grad_upd)
    degree = slope_t.shape[1] // count
    back[...] = dot(vertex[...], grad_upd)
    for start in range(0, width, TILE):
        rows = slice(start, start + TILE)
        grad_agg = back[rows, :] * (0.5 / degree)
        grad_pre[rows, degree * count :] = (grad_agg * slope_sum_t[rows, :]).astype(BF16)
        for k in range(degree):
            here = slice(k * count, (k + 1) * count)
            grad_pre[rows, here] = (grad_agg * slope_t[rows, here].astype(F32)).astype(BF16)
    whole[:, width : 2 * width] = dot_nt(nodes_t[...], grad_pre[:, degree * count :])
    whole[:, :width] = dot_nt(picked_t[...], grad_pre[:, : degree * count])
    whole[:, main:] = jnp.zeros((width, LANES), F32)
    spot = (lax.broadcasted_iota(jnp.int32, (8, LANES), 0) == 0) & (lax.broadcasted_iota(jnp.int32, (8, LANES), 1) == 0)
    whole[0:8, main:] = jnp.where(spot, jnp.sum(term[...]), 0.0)
    if len(refs) == 3:
        return
    keep, send_first, send_rest = refs[:3]
    core, x, dom = position()
    share = width // 32

    def block(c, other, k):
        quarter = 2 * c + (1 - x if other else x)
        start = (8 * quarter + lax.bitwise_xor(dom, k)) * share
        return whole[pl.ds(pl.multiple_of(start, share), share), :]

    order = [(1, k) for k in (4, 5, 6, 7)]
    order += [(other, k) for k in (1, 2, 3) for other in (1, 0)]
    order += [(0, k) for k in (4, 5, 6, 7)] + [(1, 0), (0, 0)]
    for i, (other, k) in enumerate(order):
        keep[i * share : (i + 1) * share, :] = block(core, other, k)
        value = encoded(block(1 - core, other, k))
        if i < 4:
            send_first[i * share : (i + 1) * share, :] = value
        else:
            send_rest[(i - 4) * share : (i - 3) * share, :] = value


def far_kernel(keep, first, out):
    out[...] = encoded(keep[: out.shape[0], :] + first[...].astype(F32))


def pairs_kernel(keep, rest, *outs):
    rows = outs[0].shape[0]
    for k, out in enumerate(outs):
        out[...] = encoded(keep[(k + 2) * rows : (k + 3) * rows, :] + rest[k * rows : (k + 1) * rows, :].astype(F32))


def quads_kernel(keep, rest, far, *outs):
    rows = outs[0].shape[0]
    for k, out in enumerate(outs):
        total = keep[(k + 10) * rows : (k + 11) * rows, :] + rest[(k + 6) * rows : (k + 7) * rows, :].astype(F32)
        out[...] = encoded(total + far[k * rows : (k + 1) * rows, :].astype(F32))


def across_kernel(keep, rest, *refs):
    out = refs[-1]
    rows = out.shape[0]
    total = keep[14 * rows : 15 * rows, :] + rest[10 * rows : 11 * rows, :].astype(F32)
    for ref in refs[:-1]:
        total += ref[:rows, :].astype(F32)
    out[...] = encoded(total)


def own_kernel(keep, rest, *refs):
    out = refs[-1]
    rows = out.shape[0]
    total = keep[15 * rows :, :] + rest[11 * rows :, :].astype(F32)
    for ref in refs[:-1]:
        total += ref[ref.shape[0] - rows :, :].astype(F32)
    out[...] = encoded(total)


def join_kernel(*refs):
    start = 0
    for ref in refs[:-1]:
        refs[-1][start : start + ref.shape[0], :] = ref[...]
        start += ref.shape[0]


def pair_kernel(mine, other, after, out):
    del after
    rows = mine.shape[0]
    out[:rows, :] = mine[...]
    out[rows:, :] = other[...]


def finish_kernel(scale, *refs):
    g_send, g_recv, g_update, g_decode, loss = refs[-5:]
    pieces = refs[:-5]
    width = g_send.shape[1]
    share = width // 32
    core, x, dom = position()
    total = jnp.zeros((share, LANES), F32)
    for i, piece in enumerate(pieces):
        for j in range(piece.shape[0] // share):
            if i % 3 == 0:
                other, k = j % 2, j // 2
            else:
                other, k = i % 3 - 1, 4 + j
            quarter = 2 * (core if i < 3 else 1 - core) + (1 - x if other else x)
            start = (8 * quarter + lax.bitwise_xor(dom, k)) * share
            place = pl.ds(pl.multiple_of(start, share), share)
            value = piece[j * share : (j + 1) * share, :].astype(F32)
            g_send[place, :] = value[:, :width]
            g_recv[place, :] = value[:, width : 2 * width]
            g_update[place, :] = value[:, 2 * width : 3 * width]
            g_decode[place, :] = value[:, 3 * width : -LANES]
            total += value[:, -LANES:]
    loss[0, 0] = jnp.sum(total) * scale


def position():
    ens = lax.axis_index("ens")
    return lax.rem(ens, 2), lax.div(ens, 2), lax.axis_index("dom")


SCALAR = pl.BlockSpec(memory_space=pltpu.SMEM)


def meet(first, second):
    size = lax.axis_size("dom")
    second = lax.ppermute(second, "dom", [(i, (i + (1 if i % 2 else size - 1)) % size) for i in range(size)])
    return flip(first, "dom", 1), second


def flip(value, axis, bit):
    size = lax.axis_size(axis)
    return lax.ppermute(value, axis, [(i, i ^ bit) for i in range(size)])


def nbytes(arrays):
    return sum(x.size * x.dtype.itemsize for x in arrays)


def call(kernel, ins, outs, scratch=(), flops=0, room=4, in_hbm=0, out_hbm=0, limit=0):
    size = nbytes(list(ins) + list(outs))
    return pl.pallas_call(
        kernel,
        out_shape=outs,
        in_specs=vmem(len(ins) - in_hbm) + [HBM] * in_hbm,
        out_specs=vmem(len(outs) - out_hbm) + [HBM] * out_hbm,
        scratch_shapes=list(scratch),
        compiler_params=params(limit or 1.1 * size / MIB + room),
        cost_estimate=cost(flops, size),
    )(*ins)


def scalar(value):
    return jnp.reshape(value, (1,)).astype(jnp.int32)


def gathered(value):
    found = [value]
    bit = lax.axis_size("ens") // 2
    while bit:
        found = [x for v in found for x in (v, flip(v, "ens", bit))]
        bit //= 2
    return found


def summed(keep, send_first, send_rest):
    cols = keep.shape[1]
    share = keep.shape[0] // 16
    core = lambda v: flip(v, "ens", 1)
    over_x = lambda v: flip(v, "ens", 2)
    piece = lambda shares: sds((shares * share, cols), BF16)
    near, far = (1, 2, 3), (4, 5, 6, 7)
    first, rest = core(send_first), core(send_rest)
    (out,) = call(far_kernel, [keep, first], [piece(4)])
    from_x = over_x(out)
    outs = call(pairs_kernel, [keep, rest], [piece(2)] * 3)
    pairs = [flip(v, "dom", k) for k, v in zip(near, outs)]
    outs = call(quads_kernel, [keep, rest, from_x], [piece(1)] * 4)
    quads = [flip(v, "dom", k) for k, v in zip(far, outs)]
    (out,) = call(across_kernel, [keep, rest] + pairs, [piece(1)])
    got = over_x(out)
    (own,) = call(own_kernel, [keep, rest] + pairs + quads + [got], [piece(1)])

    (far_own,) = call(join_kernel, [flip(own, "dom", k) for k in far], [piece(4)])
    (pair,) = call(pair_kernel, [own, over_x(own), far_own], [piece(2)])
    (close,) = call(join_kernel, [pair] + [flip(pair, "dom", k) for k in near], [piece(8)])
    here = [close, far_own, over_x(far_own)]
    return here + [core(v) for v in here]


def per_device(
    nodes, senders, send_next, send_prev, readout_vertex_list, dec_weights, base, observed_analysis,
    w_send, w_recv, vertex_refresh_matrix, w_decode,
):
    latent = nodes[0]
    count, width = latent.shape
    halo = send_next.shape[0]
    line_span, variables = base.shape
    degree = senders.shape[0]
    fan = readout_vertex_list.shape[0]
    ext_rows = count + 2 * halo
    members = lax.axis_size("ens")
    ens, dom = lax.axis_index("ens"), lax.axis_index("dom")
    to_next, to_prev = send_next.reshape(1, halo), send_prev.reshape(1, halo)

    held = lambda shape, dtype=BF16: pltpu.VMEM(shape, dtype)
    indices = lambda: [held((1, halo), jnp.int32)] * 2
    nodes_t, first_t, second_t = call(
        lend_kernel,
        [latent, to_next, to_prev],
        [sds((width, count), BF16), sds((width, halo), BF16), sds((width, halo), BF16)],
        [held((count, width))] + indices() + [pltpu.SemaphoreType.DMA((3,))],
        flops=4 * width * count * halo,
        in_hbm=3,
        limit=56,
    )
    from_first, from_second = meet(first_t, second_t)

    core = scalar(lax.rem(ens, 2))
    block = 1024
    steps = line_span // 2 // block
    fixed = lambda shape: pl.BlockSpec(shape, lambda i, *at: (0,) * len(shape))
    tall = lambda rows: pl.BlockSpec((rows, block), lambda i, *at: (0, i))
    tall_half = lambda rows: pl.BlockSpec((rows, block), lambda i, at: (0, i + at[0] * steps))
    half_span = line_span // 2
    mat, base_t, truth_t, done = pl.pallas_call(
        decoder_kernel,
        grid_spec=pltpu.PrefetchScalarGridSpec(
            num_scalar_prefetch=1,
            grid=(steps,),
            in_specs=[tall_half(fan), tall_half(fan), HBM, HBM, pl.BlockSpec(memory_space=pl.ANY)],
            out_specs=[tall(2 * ext_rows), tall(variables), tall(variables), fixed((8, 128))],
            scratch_shapes=[held((half_span, variables)), held((half_span, variables)), pltpu.SemaphoreType.DMA((2,))],
        ),
        out_shape=[sds((2 * ext_rows, half_span), BF16)] + [sds((variables, half_span), BF16)] * 2 + [sds((8, 128), F32)],
        compiler_params=params(56),
        cost_estimate=cost(10 * ext_rows * half_span, 16e6),
    )(core, readout_vertex_list, dec_weights, base, observed_analysis, nodes_t)

    field_t, first_t, second_t, picked_t, slope_t, slope_sum_t, agg_t, upd_slope_t, hidden_t = call(
        forward_kernel,
        [nodes_t, from_first, from_second, senders, w_send, w_recv, to_next, to_prev, vertex_refresh_matrix, w_decode, done],
        [
            sds((variables, count), BF16), sds((variables, halo), BF16), sds((variables, halo), BF16),
            sds((width, degree * count), BF16), sds((width, degree * count), BF16), sds((width, count), F32),
            sds((width, count), BF16), sds((width, count), F32), sds((width, count), BF16),
        ],
        [held((width, ext_rows)), held((degree, count), jnp.int32), held((width, width)), held((width, width))] + indices() + [
            held((width, width)), held((width, variables)), held((width, degree * count)), held((width, count), F32),
            held((width, degree * count)), held((width, count), F32), held((width, count)), held((width, count), F32),
            held((width, count)), held((width, degree * count), F32),
            held((variables, count)), held((variables, halo)), held((variables, halo)),
            pltpu.SemaphoreType.DMA((10,)), pltpu.SemaphoreType.DMA((width // 128 + 7 + degree,)),
        ],
        flops=2 * degree * width * count * (ext_rows + width),
        in_hbm=11,
        out_hbm=9,
        limit=56,
    )
    lent = meet(first_t, second_t)
    mids = gathered(field_t)

    (end,) = call(borrowed_kernel, list(lent), [sds((variables, 2 * halo), BF16)])
    ends = gathered(end)

    wide = lambda rows: pl.BlockSpec((rows, 2 * block), lambda i, *at: (0, i))
    grads = pl.pallas_call(
        functools.partial(readout_kernel, line_span),
        grid=(steps,),
        out_shape=[sds((variables, count), F32), sds((variables, 2 * halo), F32)] * 2 + [sds((8, block), F32)],
        in_specs=[fixed((variables, count))] * members + [fixed((variables, 2 * halo))] * members + [
            tall(2 * ext_rows), tall(variables), tall(variables),
        ],
        out_specs=[fixed((variables, count)), fixed((variables, 2 * halo))] * 2 + [fixed((8, block))],
        scratch_shapes=[
            pltpu.VMEM((members * variables, 2 * ext_rows), BF16), pltpu.VMEM((2 * variables, ext_rows), F32),
            *[pltpu.VMEM((members * variables, 256), F32)] * (block // 256),
            *[pltpu.VMEM((2 * variables, 256), BF16)] * (block // 256),
        ],
        compiler_params=params(20),
        cost_estimate=cost(4 * members * variables * ext_rows * half_span, 14e6),
    )(*mids, *ends, mat, base_t, truth_t)
    own_mid, own_end, pair_mid, pair_end, term = grads
    got_end = flip(pair_end, "ens", 1)
    got_mid = flip(pair_mid, "ens", 1)
    to_first, to_second = call(ends_kernel, [own_end, got_end], [sds((variables, halo), BF16)] * 2)
    from_first, from_second = meet(to_first, to_second)

    cols = 3 * width + variables + LANES
    operands = [
        own_mid, got_mid, from_first, from_second, to_next, to_prev, term, w_decode,
        vertex_refresh_matrix, nodes_t, picked_t, slope_t, slope_sum_t, agg_t, upd_slope_t, hidden_t,
    ]
    whole = sds((width, cols), F32)
    scratch = [held((width, count), F32), held((width, (degree + 1) * count))]
    flops = 2 * (degree + 3) * width * width * count
    scale = 1.0 / line_span
    if lax.axis_size("dom") != 8 or members != 4 or width % 512:
        (total,) = call(backward_kernel, operands, [whole], scratch, flops, room=16)
        total = lax.psum(total, ("ens", "dom"))
        cuts = [total[:, i * width : (i + 1) * width] for i in range(3)]
        return *cuts, total[:, 3 * width : -LANES], jnp.sum(total[:, -LANES:]) * scale
    block = width // 8
    parts = call(
        backward_kernel,
        operands,
        [sds((4 * block, cols), F32), sds((block, cols), BF16), sds((3 * block, cols), BF16)],
        [held(whole.shape, F32)] + scratch,
        flops,
        room=16,
    )
    pieces = summed(*parts)
    g_send, g_recv, g_update, g_decode, loss = pl.pallas_call(
        functools.partial(finish_kernel, scale),
        out_shape=[sds((width, width), F32)] * 3 + [sds((width, variables), F32), sds((1, 1), F32)],
        in_specs=vmem(len(pieces)),
        out_specs=vmem(4) + [SCALAR],
        compiler_params=params(14),
        cost_estimate=cost(0, 6 * width * cols),
    )(*pieces)
    return g_send, g_recv, g_update, g_decode, loss[0, 0]


def solution(mesh):
    return jax.shard_map(
        per_device,
        mesh=mesh,
        in_specs=(
            P("ens", "dom", None), P(None, "dom"), P("dom"), P("dom"), P(None, "dom"), P(None, "dom"),
            P("dom", None), P("dom", None), P(), P(), P(), P(),
        ),
        out_specs=(P(), P(), P(), P(), P()),
        check_vma=False,
    )
```

```python
import functools

import jax
import jax.numpy as jnp
from jax import lax
from jax.experimental import pallas as pl
from jax.experimental.pallas import tpu as pltpu
from jax.sharding import PartitionSpec as P

EPS = 0.04
F32 = jnp.float32
BF16 = jnp.bfloat16
MIB = 1024 * 1024


def dot(a, b, ca=1, cb=0):
    return lax.dot_general(a, b, (((ca,), (cb,)), ((), ())), preferred_element_type=F32)


def dot_nt(a, b):
    return dot(a, b, 1, 1)


def one_hot(rows, index_row):
    shape = (rows, index_row.shape[1])
    hit = lax.broadcasted_iota(jnp.int32, shape, 0) == index_row
    return jnp.where(hit, 1.0, 0.0).astype(BF16)


def params(mib):
    return pltpu.CompilerParams(vmem_limit_bytes=int(mib * MIB))


def vmem(n):
    return [pl.BlockSpec(memory_space=pltpu.VMEM)] * n


def cost(flops, size):
    return pl.CostEstimate(flops=int(flops), bytes_accessed=int(size), transcendentals=0)


def sds(shape, dtype):
    return jax.ShapeDtypeStruct(shape, dtype)


HBM = pl.BlockSpec(memory_space=pltpu.HBM)


def fetched(sources, targets, sems):
    copies = [pltpu.make_async_copy(a, b, sems.at[i]) for i, (a, b) in enumerate(zip(sources, targets))]
    for copy in copies:
        copy.start()
    return copies


def sides(next_side, prev_side):
    even = lax.rem(lax.axis_index("dom"), 2) == 0
    return jnp.where(even, next_side, prev_side), jnp.where(even, prev_side, next_side)


def lend_kernel(nodes, to_next, to_prev, nodes_t, first_t, second_t, held, rows_next, rows_prev, sems):
    for copy in fetched((nodes, to_next, to_prev), (held, rows_next, rows_prev), sems):
        copy.wait()
    table = held[...].T
    nodes_t[...] = table
    count = table.shape[1]
    first, second = sides(rows_next[...], rows_prev[...])
    first_t[...] = dot(table, one_hot(count, first)).astype(BF16)
    second_t[...] = dot(table, one_hot(count, second)).astype(BF16)


def decoder_kernel(core, vertices, weights, base, truth, after, mat, base_t, truth_t, done, base_rows, truth_rows, sems):
    del after
    done[...] = jnp.zeros_like(done)
    span = base_rows.shape[0]
    half = pl.ds(pl.multiple_of(core[0] * span, span), span)
    copies = [
        pltpu.make_async_copy(base.at[half, :], base_rows, sems.at[0]),
        pltpu.make_async_copy(truth.at[half, :], truth_rows, sems.at[1]),
    ]

    @pl.when(pl.program_id(0) == 0)
    def _():
        for copy in copies:
            copy.start()

    rows, lanes = mat.shape[0] // 2, 256
    row = lax.broadcasted_iota(jnp.int32, (8, lanes), 0)
    for left in range(0, mat.shape[1], lanes):
        cols = slice(left, left + lanes)
        spread = lambda ref, k: jnp.broadcast_to(ref[k : k + 1, cols], (8, lanes))
        ahead = [spread(vertices, k) - row for k in range(vertices.shape[0])]
        weight = [spread(weights, k) for k in range(vertices.shape[0])]

        def weighted(start):
            total = jnp.where(ahead[0] == start, weight[0], 0.0)
            for k in range(1, len(ahead)):
                total += jnp.where(ahead[k] == start, weight[k], 0.0)
            return total

        for start in range(0, rows, 16):
            hi, lo = split(jnp.concatenate([weighted(start), weighted(start + 8)], axis=0))
            mat[start : start + 16, cols] = hi
            mat[rows + start : rows + start + 16, cols] = lo

    step, block = pl.program_id(0), mat.shape[1]

    @pl.when(step == 0)
    def _():
        for copy in copies:
            copy.wait()

    some = pl.ds(pl.multiple_of(step * block, block), block)
    base_t[...] = base_rows[some, :].T
    truth_t[...] = truth_rows[some, :].T


TILE = 16


def bent(half):
    t = jnp.tanh(half)
    u = half * t
    return half + u, (1.0 + t) * (1.0 + half - u)


def forward_kernel(
    nodes_in, from_first, from_second, senders_in, w_send_in, w_recv_in, to_next_in, to_prev_in, vertex_in, w_decode_in, after,
    field_out, first_out, second_out, picked_out, slope_out, slope_sum_out, agg_out, upd_slope_out, hidden_out,
    ext, senders, w_send, w_recv, to_next, to_prev, vertex, w_decode, picked_t, recv_t,
    slope_t, slope_sum_t, agg_t, upd_slope_t, hidden_t, pre, field_t, first_t, second_t, in_sems, out_sems,
):
    del after
    degree, count = senders.shape
    width, ext_rows = ext.shape
    halo = from_first.shape[1]
    swap = lax.rem(lax.axis_index("dom"), 2) * halo
    column = lambda start: ext.at[:, pl.ds(pl.multiple_of(start, 128), halo)]
    fetch = fetched(
        (nodes_in, from_first, from_second, senders_in, w_recv_in, w_send_in, vertex_in, to_next_in, to_prev_in, w_decode_in),
        (
            ext.at[:, :count], column(count + halo - swap), column(count + swap),
            senders, w_recv, w_send, vertex, to_next, to_prev, w_decode,
        ),
        in_sems,
    )
    stored = []

    def store(source, target):
        copy = pltpu.make_async_copy(source, target, out_sems.at[len(stored)])
        copy.start()
        stored.append(copy)

    for copy in fetch[:4]:
        copy.wait()
    for k in range(degree):
        here = slice(k * count, (k + 1) * count)
        picked_t[:, here] = dot(ext[...], one_hot(ext_rows, senders[k : k + 1, :])).astype(BF16)
        store(picked_t.at[:, here], picked_out.at[:, here])
        if k == 0:
            for copy in fetch[4:]:
                copy.wait()
            w_send_t = w_send[...].T * 0.5
        pre[:, here] = dot(w_send_t, picked_t[:, here])
    recv_t[...] = dot(w_recv[...].T, ext[:, :count]) * 0.5
    for start in range(0, width, TILE):
        rows = slice(start, start + TILE)
        recv = recv_t[rows, :]
        total = slopes = None
        for k in range(degree):
            here = slice(k * count, (k + 1) * count)
            value, slope = bent(pre[rows, here] + recv)
            slope_t[rows, here] = slope.astype(BF16)
            total = value if k == 0 else total + value
            slopes = slope if k == 0 else slopes + slope
        slope_sum_t[rows, :] = slopes
        agg_t[rows, :] = (total * (1.0 / degree)).astype(BF16)
        if (start + TILE) % 128 == 0:
            group = slice(start + TILE - 128, start + TILE)
            store(slope_t.at[group, :], slope_out.at[group, :])
    store(slope_sum_t, slope_sum_out)
    store(agg_t, agg_out)
    pre[:, :count] = dot(vertex[...].T * 0.5, agg_t[...])
    for start in range(0, width, TILE):
        rows = slice(start, start + TILE)
        value, slope = bent(pre[rows, :count])
        upd_slope_t[rows, :] = slope * 0.5
        hidden_t[rows, :] = (ext[rows, :count].astype(F32) + value).astype(BF16)
    store(hidden_t, hidden_out)
    store(upd_slope_t, upd_slope_out)
    field = dot(w_decode[...].T, hidden_t[...]).astype(BF16)
    field_t[...] = field
    first, second = sides(to_next[...], to_prev[...])
    first_t[...] = dot(field, one_hot(count, first)).astype(BF16)
    second_t[...] = dot(field, one_hot(count, second)).astype(BF16)
    store(field_t, field_out)
    store(first_t, first_out)
    store(second_t, second_out)
    for copy in stored:
        copy.wait()


def readout_kernel(line_span, *refs):
    mids, ends = refs[0:4], refs[4:8]
    mat, base_t, truth_t = refs[8:11]
    own_mid, own_end, pair_mid, pair_end, loss = refs[11:16]
    table, grad = refs[16:18]
    subs = (len(refs) - 18) // 2
    states, slopes = refs[18 : 18 + subs], refs[18 + subs :]
    step = pl.program_id(0)
    members = len(mids)
    variables, count = own_mid.shape
    ext_rows = grad.shape[1]

    @pl.when(step == 0)
    def _():
        grad[...] = jnp.zeros_like(grad)
        loss[...] = jnp.zeros_like(loss)
        for m in range(members):
            for base in (0, ext_rows):
                table[m * variables : (m + 1) * variables, base : base + count] = mids[m][...]
                table[m * variables : (m + 1) * variables, base + count : base + ext_rows] = ends[m][...]

    wide = states[0].shape[1]
    for i, state in enumerate(states):
        state[...] = dot(table[...], mat[:, i * wide : (i + 1) * wide])

    def bend(diff):
        square = diff * diff + EPS
        inverse = lax.rsqrt(square)
        return square * inverse, diff * inverse

    alone = EPS**0.5
    for i, (state, slope_out) in enumerate(zip(states, slopes)):
        cols = slice(i * wide, (i + 1) * wide)
        summed = jnp.zeros((8, wide), F32)
        for start in range(0, variables, TILE):
            rows = slice(start, start + TILE)
            ready = base_t[rows, cols].astype(F32)
            truth = truth_t[rows, cols].astype(F32)
            x = [
                (state[m * variables + start : m * variables + start + TILE, :] + ready).astype(BF16).astype(F32)
                for m in range(members)
            ]
            apart = [alone, alone]
            pull = [0.0, 0.0]
            for m in range(2):
                for j in range(m + 1, members):
                    size, slope = bend(x[m] - x[j])
                    apart[m] = apart[m] + size
                    pull[m] = pull[m] + slope
                    if j < 2:
                        apart[j] = apart[j] + size
                        pull[j] = pull[j] - slope
            near = 0.0
            for m in range(2):
                size, push = bend(x[m] - truth)
                near = near + size
                slope = push * (1.0 / members / line_span) - pull[m] * (1.0 / (members * (members - 1.0)) / line_span)
                slope_out[m * variables + start : m * variables + start + TILE, :] = slope.astype(BF16)
            term = near * (1.0 / members) - (apart[0] + apart[1]) * (1.0 / (2.0 * members * (members - 1)))
            summed += term[:8] + term[8:]
        loss[:, cols] += summed
        grad[...] += dot_nt(slope_out[...], mat[:ext_rows, cols])

    @pl.when(step == pl.num_programs(0) - 1)
    def _():
        for i, (mid, end) in enumerate(((own_mid, own_end), (pair_mid, pair_end))):
            rows = slice(i * variables, (i + 1) * variables)
            mid[...] = grad[rows, :count]
            end[...] = grad[rows, count:]


def borrowed_kernel(first, second, end):
    halo = first.shape[1]
    from_next, from_prev = sides(first[...], second[...])
    end[:, :halo] = from_prev
    end[:, halo:] = from_next


def ends_kernel(mine, got, first, second):
    halo = first.shape[1]
    total = mine[...] + got[...]
    to_first, to_second = sides(total[:, halo:], total[:, :halo])
    first[...] = to_first.astype(BF16)
    second[...] = to_second.astype(BF16)


def split(value):
    hi = value.astype(BF16)
    return hi, (value - hi.astype(F32)).astype(BF16)


LANES = 128


def encoded(total):
    tile = total[:, -LANES:]
    value = tile + pltpu.roll(tile, LANES // 2, 1)
    hi = value.astype(BF16).astype(F32)
    lane = lax.broadcasted_iota(jnp.int32, tile.shape, 1)
    tile = jnp.where(lane < LANES // 2, hi, value - hi)
    return jnp.concatenate([total[:, :-LANES].astype(BF16), tile.astype(BF16)], axis=1)


def backward_kernel(
    own_mid, pair_mid, from_first, from_second, to_next, to_prev, term, w_decode, vertex, nodes_t,
    picked_t, slope_t, slope_sum_t, agg_t, upd_slope_t, hidden_t,
    *refs,
):
    whole, back, grad_pre = refs[-3:]
    count = nodes_t.shape[1]
    width = nodes_t.shape[0]
    grad_z = own_mid[...] + pair_mid[...]
    for got, rows in zip((from_first, from_second), sides(to_next[...], to_prev[...])):
        grad_z += dot_nt(got[...], one_hot(count, rows))
    grad_z = grad_z.astype(BF16)
    main = whole.shape[1] - LANES
    whole[:, 3 * width : main] = dot_nt(hidden_t[...], grad_z)
    grad_upd = (dot(w_decode[...], grad_z) * upd_slope_t[...]).astype(BF16)
    whole[:, 2 * width : 3 * width] = dot_nt(agg_t[...], grad_upd)
    degree = slope_t.shape[1] // count
    back[...] = dot(vertex[...], grad_upd)
    for start in range(0, width, TILE):
        rows = slice(start, start + TILE)
        grad_agg = back[rows, :] * (0.5 / degree)
        grad_pre[rows, degree * count :] = (grad_agg * slope_sum_t[rows, :]).astype(BF16)
        for k in range(degree):
            here = slice(k * count, (k + 1) * count)
            grad_pre[rows, here] = (grad_agg * slope_t[rows, here].astype(F32)).astype(BF16)
    whole[:, width : 2 * width] = dot_nt(nodes_t[...], grad_pre[:, degree * count :])
    whole[:, :width] = dot_nt(picked_t[...], grad_pre[:, : degree * count])
    whole[:, main:] = jnp.zeros((width, LANES), F32)
    spot = (lax.broadcasted_iota(jnp.int32, (8, LANES), 0) == 0) & (lax.broadcasted_iota(jnp.int32, (8, LANES), 1) == 0)
    whole[0:8, main:] = jnp.where(spot, jnp.sum(term[...]), 0.0)
    if len(refs) == 3:
        return
    keep, send_first, send_rest = refs[:3]
    core, x, dom = position()
    share = width // 32

    def block(c, other, k):
        quarter = 2 * c + (1 - x if other else x)
        start = (8 * quarter + lax.bitwise_xor(dom, k)) * share
        return whole[pl.ds(pl.multiple_of(start, share), share), :]

    order = [(1, k) for k in (4, 5, 6, 7)]
    order += [(other, k) for k in (1, 2, 3) for other in (1, 0)]
    order += [(0, k) for k in (4, 5, 6, 7)] + [(1, 0), (0, 0)]
    for i, (other, k) in enumerate(order):
        keep[i * share : (i + 1) * share, :] = block(core, other, k)
        value = encoded(block(1 - core, other, k))
        if i < 4:
            send_first[i * share : (i + 1) * share, :] = value
        else:
            send_rest[(i - 4) * share : (i - 3) * share, :] = value


def far_kernel(keep, first, out):
    out[...] = encoded(keep[: out.shape[0], :] + first[...].astype(F32))


def pairs_kernel(keep, rest, *outs):
    rows = outs[0].shape[0]
    for k, out in enumerate(outs):
        out[...] = encoded(keep[(k + 2) * rows : (k + 3) * rows, :] + rest[k * rows : (k + 1) * rows, :].astype(F32))


def quads_kernel(keep, rest, far, *outs):
    rows = outs[0].shape[0]
    for k, out in enumerate(outs):
        total = keep[(k + 10) * rows : (k + 11) * rows, :] + rest[(k + 6) * rows : (k + 7) * rows, :].astype(F32)
        out[...] = encoded(total + far[k * rows : (k + 1) * rows, :].astype(F32))


def across_kernel(keep, rest, *refs):
    out = refs[-1]
    rows = out.shape[0]
    total = keep[14 * rows : 15 * rows, :] + rest[10 * rows : 11 * rows, :].astype(F32)
    for ref in refs[:-1]:
        total += ref[:rows, :].astype(F32)
    out[...] = encoded(total)


def own_kernel(keep, rest, *refs):
    out = refs[-1]
    rows = out.shape[0]
    total = keep[15 * rows :, :] + rest[11 * rows :, :].astype(F32)
    for ref in refs[:-1]:
        total += ref[ref.shape[0] - rows :, :].astype(F32)
    out[...] = encoded(total)


def join_kernel(*refs):
    start = 0
    for ref in refs[:-1]:
        refs[-1][start : start + ref.shape[0], :] = ref[...]
        start += ref.shape[0]


def pair_kernel(mine, other, after, out):
    del after
    rows = mine.shape[0]
    out[:rows, :] = mine[...]
    out[rows:, :] = other[...]


def finish_kernel(scale, *refs):
    g_send, g_recv, g_update, g_decode, loss = refs[-5:]
    pieces = refs[:-5]
    width = g_send.shape[1]
    share = width // 32
    core, x, dom = position()
    total = jnp.zeros((share, LANES), F32)
    for i, piece in enumerate(pieces):
        for j in range(piece.shape[0] // share):
            if i % 3 == 0:
                other, k = j % 2, j // 2
            else:
                other, k = i % 3 - 1, 4 + j
            quarter = 2 * (core if i < 3 else 1 - core) + (1 - x if other else x)
            start = (8 * quarter + lax.bitwise_xor(dom, k)) * share
            place = pl.ds(pl.multiple_of(start, share), share)
            value = piece[j * share : (j + 1) * share, :].astype(F32)
            g_send[place, :] = value[:, :width]
            g_recv[place, :] = value[:, width : 2 * width]
            g_update[place, :] = value[:, 2 * width : 3 * width]
            g_decode[place, :] = value[:, 3 * width : -LANES]
            total += value[:, -LANES:]
    loss[0, 0] = jnp.sum(total) * scale


def position():
    ens = lax.axis_index("ens")
    return lax.rem(ens, 2), lax.div(ens, 2), lax.axis_index("dom")


SCALAR = pl.BlockSpec(memory_space=pltpu.SMEM)


def meet(first, second):
    size = lax.axis_size("dom")
    second = lax.ppermute(second, "dom", [(i, (i + (1 if i % 2 else size - 1)) % size) for i in range(size)])
    return flip(first, "dom", 1), second


def flip(value, axis, bit):
    size = lax.axis_size(axis)
    return lax.ppermute(value, axis, [(i, i ^ bit) for i in range(size)])


def nbytes(arrays):
    return sum(x.size * x.dtype.itemsize for x in arrays)


def freed(specs, places):
    return [pl.BlockSpec(memory_space=pl.ANY) if i in places else x for i, x in enumerate(specs)]


def call(kernel, ins, outs, scratch=(), flops=0, room=4, in_hbm=0, out_hbm=0, limit=0, free_ins=(), free_outs=()):
    size = nbytes(list(ins) + list(outs))
    return pl.pallas_call(
        kernel,
        out_shape=outs,
        in_specs=freed(vmem(len(ins) - in_hbm) + [HBM] * in_hbm, free_ins),
        out_specs=freed(vmem(len(outs) - out_hbm) + [HBM] * out_hbm, free_outs),
        scratch_shapes=list(scratch),
        compiler_params=params(limit or 1.1 * size / MIB + room),
        cost_estimate=cost(flops, size),
    )(*ins)


def scalar(value):
    return jnp.reshape(value, (1,)).astype(jnp.int32)


def gathered(value):
    found = [value]
    bit = lax.axis_size("ens") // 2
    while bit:
        found = [x for v in found for x in (v, flip(v, "ens", bit))]
        bit //= 2
    return found


def summed(keep, send_first, send_rest):
    cols = keep.shape[1]
    share = keep.shape[0] // 16
    core = lambda v: flip(v, "ens", 1)
    over_x = lambda v: flip(v, "ens", 2)
    piece = lambda shares: sds((shares * share, cols), BF16)
    near, far = (1, 2, 3), (4, 5, 6, 7)
    first, rest = core(send_first), core(send_rest)
    (out,) = call(far_kernel, [keep, first], [piece(4)])
    from_x = over_x(out)
    outs = call(pairs_kernel, [keep, rest], [piece(2)] * 3)
    pairs = [flip(v, "dom", k) for k, v in zip(near, outs)]
    outs = call(quads_kernel, [keep, rest, from_x], [piece(1)] * 4)
    quads = [flip(v, "dom", k) for k, v in zip(far, outs)]
    (out,) = call(across_kernel, [keep, rest] + pairs, [piece(1)])
    got = over_x(out)
    (own,) = call(own_kernel, [keep, rest] + pairs + quads + [got], [piece(1)])

    (far_own,) = call(join_kernel, [flip(own, "dom", k) for k in far], [piece(4)])
    (pair,) = call(pair_kernel, [own, over_x(own), far_own], [piece(2)])
    (close,) = call(join_kernel, [pair] + [flip(pair, "dom", k) for k in near], [piece(8)])
    here = [close, far_own, over_x(far_own)]
    return here + [core(v) for v in here]


def per_device(
    nodes, senders, send_next, send_prev, readout_vertex_list, dec_weights, base, observed_analysis,
    w_send, w_recv, vertex_refresh_matrix, w_decode,
):
    latent = nodes[0]
    count, width = latent.shape
    halo = send_next.shape[0]
    line_span, variables = base.shape
    degree = senders.shape[0]
    fan = readout_vertex_list.shape[0]
    ext_rows = count + 2 * halo
    members = lax.axis_size("ens")
    ens, dom = lax.axis_index("ens"), lax.axis_index("dom")
    to_next, to_prev = send_next.reshape(1, halo), send_prev.reshape(1, halo)

    held = lambda shape, dtype=BF16: pltpu.VMEM(shape, dtype)
    indices = lambda: [held((1, halo), jnp.int32)] * 2
    nodes_t, first_t, second_t = call(
        lend_kernel,
        [latent, to_next, to_prev],
        [sds((width, count), BF16), sds((width, halo), BF16), sds((width, halo), BF16)],
        [held((count, width))] + indices() + [pltpu.SemaphoreType.DMA((3,))],
        flops=4 * width * count * halo,
        in_hbm=3,
        limit=56,
    )
    from_first, from_second = meet(first_t, second_t)

    core = scalar(lax.rem(ens, 2))
    block = 1024
    steps = line_span // 2 // block
    fixed = lambda shape: pl.BlockSpec(shape, lambda i, *at: (0,) * len(shape))
    tall = lambda rows: pl.BlockSpec((rows, block), lambda i, *at: (0, i))
    tall_half = lambda rows: pl.BlockSpec((rows, block), lambda i, at: (0, i + at[0] * steps))
    half_span = line_span // 2
    mat, base_t, truth_t, done = pl.pallas_call(
        decoder_kernel,
        grid_spec=pltpu.PrefetchScalarGridSpec(
            num_scalar_prefetch=1,
            grid=(steps,),
            in_specs=[tall_half(fan), tall_half(fan), HBM, HBM, pl.BlockSpec(memory_space=pl.ANY)],
            out_specs=[tall(2 * ext_rows), tall(variables), tall(variables), fixed((8, 128))],
            scratch_shapes=[held((half_span, variables)), held((half_span, variables)), pltpu.SemaphoreType.DMA((2,))],
        ),
        out_shape=[sds((2 * ext_rows, half_span), BF16)] + [sds((variables, half_span), BF16)] * 2 + [sds((8, 128), F32)],
        compiler_params=params(56),
        cost_estimate=cost(10 * ext_rows * half_span, 16e6),
    )(core, readout_vertex_list, dec_weights, base, observed_analysis, nodes_t)

    field_t, first_t, second_t, picked_t, slope_t, slope_sum_t, agg_t, upd_slope_t, hidden_t = call(
        forward_kernel,
        [nodes_t, from_first, from_second, senders, w_send, w_recv, to_next, to_prev, vertex_refresh_matrix, w_decode, done],
        [
            sds((variables, count), BF16), sds((variables, halo), BF16), sds((variables, halo), BF16),
            sds((width, degree * count), BF16), sds((width, degree * count), BF16), sds((width, count), F32),
            sds((width, count), BF16), sds((width, count), F32), sds((width, count), BF16),
        ],
        [held((width, ext_rows)), held((degree, count), jnp.int32), held((width, width)), held((width, width))] + indices() + [
            held((width, width)), held((width, variables)), held((width, degree * count)), held((width, count), F32),
            held((width, degree * count)), held((width, count), F32), held((width, count)), held((width, count), F32),
            held((width, count)), held((width, degree * count), F32),
            held((variables, count)), held((variables, halo)), held((variables, halo)),
            pltpu.SemaphoreType.DMA((10,)), pltpu.SemaphoreType.DMA((width // 128 + 7 + degree,)),
        ],
        flops=2 * degree * width * count * (ext_rows + width),
        in_hbm=11,
        out_hbm=9,
        free_ins=(1, 2),
        free_outs=(0, 1, 2),
        limit=52,
    )
    lent = meet(first_t, second_t)
    mids = gathered(field_t)

    (end,) = call(borrowed_kernel, list(lent), [sds((variables, 2 * halo), BF16)])
    ends = gathered(end)

    wide = lambda rows: pl.BlockSpec((rows, 2 * block), lambda i, *at: (0, i))
    grads = pl.pallas_call(
        functools.partial(readout_kernel, line_span),
        grid=(steps,),
        out_shape=[sds((variables, count), F32), sds((variables, 2 * halo), F32)] * 2 + [sds((8, block), F32)],
        in_specs=[fixed((variables, count))] * members + [fixed((variables, 2 * halo))] * members + [
            tall(2 * ext_rows), tall(variables), tall(variables),
        ],
        out_specs=[fixed((variables, count)), fixed((variables, 2 * halo))] * 2 + [fixed((8, block))],
        scratch_shapes=[
            pltpu.VMEM((members * variables, 2 * ext_rows), BF16), pltpu.VMEM((2 * variables, ext_rows), F32),
            *[pltpu.VMEM((members * variables, 256), F32)] * (block // 256),
            *[pltpu.VMEM((2 * variables, 256), BF16)] * (block // 256),
        ],
        compiler_params=params(20),
        cost_estimate=cost(4 * members * variables * ext_rows * half_span, 14e6),
    )(*mids, *ends, mat, base_t, truth_t)
    own_mid, own_end, pair_mid, pair_end, term = grads
    got_end = flip(pair_end, "ens", 1)
    got_mid = flip(pair_mid, "ens", 1)
    to_first, to_second = call(ends_kernel, [own_end, got_end], [sds((variables, halo), BF16)] * 2)
    from_first, from_second = meet(to_first, to_second)

    cols = 3 * width + variables + LANES
    operands = [
        own_mid, got_mid, from_first, from_second, to_next, to_prev, term, w_decode,
        vertex_refresh_matrix, nodes_t, picked_t, slope_t, slope_sum_t, agg_t, upd_slope_t, hidden_t,
    ]
    whole = sds((width, cols), F32)
    scratch = [held((width, count), F32), held((width, (degree + 1) * count))]
    flops = 2 * (degree + 3) * width * width * count
    scale = 1.0 / line_span
    if lax.axis_size("dom") != 8 or members != 4 or width % 512:
        (total,) = call(backward_kernel, operands, [whole], scratch, flops, room=16)
        total = lax.psum(total, ("ens", "dom"))
        cuts = [total[:, i * width : (i + 1) * width] for i in range(3)]
        return *cuts, total[:, 3 * width : -LANES], jnp.sum(total[:, -LANES:]) * scale
    block = width // 8
    parts = call(
        backward_kernel,
        operands,
        [sds((4 * block, cols), F32), sds((block, cols), BF16), sds((3 * block, cols), BF16)],
        [held(whole.shape, F32)] + scratch,
        flops,
        room=16,
    )
    pieces = summed(*parts)
    g_send, g_recv, g_update, g_decode, loss = pl.pallas_call(
        functools.partial(finish_kernel, scale),
        out_shape=[sds((width, width), F32)] * 3 + [sds((width, variables), F32), sds((1, 1), F32)],
        in_specs=vmem(len(pieces)),
        out_specs=vmem(4) + [SCALAR],
        compiler_params=params(14),
        cost_estimate=cost(0, 6 * width * cols),
    )(*pieces)
    return g_send, g_recv, g_update, g_decode, loss[0, 0]


def solution(mesh):
    return jax.shard_map(
        per_device,
        mesh=mesh,
        in_specs=(
            P("ens", "dom", None), P(None, "dom"), P("dom"), P("dom"), P(None, "dom"), P(None, "dom"),
            P("dom", None), P("dom", None), P(), P(), P(), P(),
        ),
        out_specs=(P(), P(), P(), P(), P()),
        check_vma=False,
    )
```

```python
import functools

import jax
import jax.numpy as jnp
from jax import lax
from jax.experimental import pallas as pl
from jax.experimental.pallas import tpu as pltpu
from jax.sharding import PartitionSpec as P

EPS = 0.04
F32 = jnp.float32
BF16 = jnp.bfloat16
MIB = 1024 * 1024


def dot(a, b, ca=1, cb=0):
    return lax.dot_general(a, b, (((ca,), (cb,)), ((), ())), preferred_element_type=F32)


def dot_nt(a, b):
    return dot(a, b, 1, 1)


def one_hot(rows, index_row):
    shape = (rows, index_row.shape[1])
    hit = lax.broadcasted_iota(jnp.int32, shape, 0) == index_row
    return jnp.where(hit, 1.0, 0.0).astype(BF16)


def params(mib):
    return pltpu.CompilerParams(vmem_limit_bytes=int(mib * MIB))


def vmem(n):
    return [pl.BlockSpec(memory_space=pltpu.VMEM)] * n


def cost(flops, size):
    return pl.CostEstimate(flops=int(flops), bytes_accessed=int(size), transcendentals=0)


def sds(shape, dtype):
    return jax.ShapeDtypeStruct(shape, dtype)


HBM = pl.BlockSpec(memory_space=pltpu.HBM)


def fetched(sources, targets, sems):
    copies = [pltpu.make_async_copy(a, b, sems.at[i]) for i, (a, b) in enumerate(zip(sources, targets))]
    for copy in copies:
        copy.start()
    return copies


def sides(next_side, prev_side):
    even = lax.rem(lax.axis_index("dom"), 2) == 0
    return jnp.where(even, next_side, prev_side), jnp.where(even, prev_side, next_side)


def lend_kernel(nodes, to_next, to_prev, nodes_t, first_t, second_t, held, rows_next, rows_prev, sems):
    for copy in fetched((nodes, to_next, to_prev), (held, rows_next, rows_prev), sems):
        copy.wait()
    table = held[...].T
    nodes_t[...] = table
    count = table.shape[1]
    first, second = sides(rows_next[...], rows_prev[...])
    first_t[...] = dot(table, one_hot(count, first)).astype(BF16)
    second_t[...] = dot(table, one_hot(count, second)).astype(BF16)


def decoder_kernel(core, vertices, weights, base, truth, after, mat, base_t, truth_t, done, base_rows, truth_rows, sems):
    del after
    done[...] = jnp.zeros_like(done)
    span = base_rows.shape[0]
    half = pl.ds(pl.multiple_of(core[0] * span, span), span)
    copies = [
        pltpu.make_async_copy(base.at[half, :], base_rows, sems.at[0]),
        pltpu.make_async_copy(truth.at[half, :], truth_rows, sems.at[1]),
    ]

    @pl.when(pl.program_id(0) == 0)
    def _():
        for copy in copies:
            copy.start()

    rows, lanes = mat.shape[0] // 2, 256
    row = lax.broadcasted_iota(jnp.int32, (8, lanes), 0)
    for left in range(0, mat.shape[1], lanes):
        cols = slice(left, left + lanes)
        spread = lambda ref, k: jnp.broadcast_to(ref[k : k + 1, cols], (8, lanes))
        ahead = [spread(vertices, k) - row for k in range(vertices.shape[0])]
        weight = [spread(weights, k) for k in range(vertices.shape[0])]

        def weighted(start):
            total = jnp.where(ahead[0] == start, weight[0], 0.0)
            for k in range(1, len(ahead)):
                total += jnp.where(ahead[k] == start, weight[k], 0.0)
            return total

        for start in range(0, rows, 16):
            hi, lo = split(jnp.concatenate([weighted(start), weighted(start + 8)], axis=0))
            mat[start : start + 16, cols] = hi
            mat[rows + start : rows + start + 16, cols] = lo

    step, block = pl.program_id(0), mat.shape[1]

    @pl.when(step == 0)
    def _():
        for copy in copies:
            copy.wait()

    some = pl.ds(pl.multiple_of(step * block, block), block)
    base_t[...] = base_rows[some, :].T
    truth_t[...] = truth_rows[some, :].T


TILE = 16


def bent(half):
    t = jnp.tanh(half)
    u = half * t
    return half + u, (1.0 + t) * (1.0 + half - u)


def forward_kernel(
    nodes_in, from_first, from_second, senders_in, w_send_in, w_recv_in, to_next_in, to_prev_in, vertex_in, w_decode_in, after,
    field_out, first_out, second_out, picked_out, slope_out, slope_sum_out, agg_out, upd_slope_out, hidden_out,
    ext, senders, w_send, w_recv, to_next, to_prev, vertex, w_decode, picked_t, recv_t,
    slope_t, slope_sum_t, agg_t, upd_slope_t, hidden_t, pre, field_t, first_t, second_t, in_sems, out_sems,
):
    del after
    degree, count = senders.shape
    width, ext_rows = ext.shape
    halo = from_first.shape[1]
    swap = lax.rem(lax.axis_index("dom"), 2) * halo
    column = lambda start: ext.at[:, pl.ds(pl.multiple_of(start, 128), halo)]
    fetch = fetched(
        (nodes_in, from_first, from_second, senders_in, w_recv_in, w_send_in, vertex_in, to_next_in, to_prev_in, w_decode_in),
        (
            ext.at[:, :count], column(count + halo - swap), column(count + swap),
            senders, w_recv, w_send, vertex, to_next, to_prev, w_decode,
        ),
        in_sems,
    )
    stored = []

    def store(source, target):
        copy = pltpu.make_async_copy(source, target, out_sems.at[len(stored)])
        copy.start()
        stored.append(copy)

    for copy in fetch[:4]:
        copy.wait()
    for k in range(degree):
        here = slice(k * count, (k + 1) * count)
        picked_t[:, here] = dot(ext[...], one_hot(ext_rows, senders[k : k + 1, :])).astype(BF16)
        store(picked_t.at[:, here], picked_out.at[:, here])
        if k == 0:
            for copy in fetch[4:]:
                copy.wait()
            w_send_t = w_send[...].T * 0.5
        pre[:, here] = dot(w_send_t, picked_t[:, here])
    recv_t[...] = dot(w_recv[...].T, ext[:, :count]) * 0.5
    for start in range(0, width, TILE):
        rows = slice(start, start + TILE)
        recv = recv_t[rows, :]
        total = slopes = None
        for k in range(degree):
            here = slice(k * count, (k + 1) * count)
            value, slope = bent(pre[rows, here] + recv)
            slope_t[rows, here] = slope.astype(BF16)
            total = value if k == 0 else total + value
            slopes = slope if k == 0 else slopes + slope
        slope_sum_t[rows, :] = slopes
        agg_t[rows, :] = (total * (1.0 / degree)).astype(BF16)
        if (start + TILE) % 128 == 0:
            group = slice(start + TILE - 128, start + TILE)
            store(slope_t.at[group, :], slope_out.at[group, :])
    store(slope_sum_t, slope_sum_out)
    store(agg_t, agg_out)
    pre[:, :count] = dot(vertex[...].T * 0.5, agg_t[...])
    for start in range(0, width, TILE):
        rows = slice(start, start + TILE)
        value, slope = bent(pre[rows, :count])
        upd_slope_t[rows, :] = slope * 0.5
        hidden_t[rows, :] = (ext[rows, :count].astype(F32) + value).astype(BF16)
    store(hidden_t, hidden_out)
    store(upd_slope_t, upd_slope_out)
    field = dot(w_decode[...].T, hidden_t[...]).astype(BF16)
    field_t[...] = field
    first, second = sides(to_next[...], to_prev[...])
    first_t[...] = dot(field, one_hot(count, first)).astype(BF16)
    second_t[...] = dot(field, one_hot(count, second)).astype(BF16)
    store(field_t, field_out)
    store(first_t, first_out)
    store(second_t, second_out)
    for copy in stored:
        copy.wait()


def readout_kernel(line_span, *refs):
    mids, ends = refs[0:4], refs[4:8]
    mat, base_t, truth_t = refs[8:11]
    own_mid, own_end, pair_mid, pair_end, loss = refs[11:16]
    table, grad = refs[16:18]
    subs = (len(refs) - 18) // 2
    states, slopes = refs[18 : 18 + subs], refs[18 + subs :]
    members = len(mids)
    variables, count = own_mid.shape
    ext_rows = grad.shape[1]

    grad[...] = jnp.zeros_like(grad)
    loss[...] = jnp.zeros_like(loss)
    for m in range(members):
        for start in (0, ext_rows):
            table[m * variables : (m + 1) * variables, start : start + count] = mids[m][...]
            table[m * variables : (m + 1) * variables, start + count : start + ext_rows] = ends[m][...]

    def bend(diff):
        square = diff * diff + EPS
        inverse = lax.rsqrt(square)
        return square * inverse, diff * inverse

    alone = EPS**0.5
    wide = states[0].shape[1]
    blocks = mat.shape[1] // wide

    def decode(i):
        states[i % 2][...] = dot(table[...], mat[:, i * wide : (i + 1) * wide])

    decode(0)
    for i in range(blocks):
        state, slope_out = states[i % 2], slopes[i % 2]
        cols = slice(i * wide, (i + 1) * wide)
        if i + 1 < blocks:
            decode(i + 1)
        summed = jnp.zeros((8, wide), F32)
        for start in range(0, variables, TILE):
            rows = slice(start, start + TILE)
            ready = base_t[rows, cols].astype(F32)
            truth = truth_t[rows, cols].astype(F32)
            x = [
                (state[m * variables + start : m * variables + start + TILE, :] + ready).astype(BF16).astype(F32)
                for m in range(members)
            ]
            apart = [alone, alone]
            pull = [0.0, 0.0]
            for m in range(2):
                for j in range(m + 1, members):
                    size, slope = bend(x[m] - x[j])
                    apart[m] = apart[m] + size
                    pull[m] = pull[m] + slope
                    if j < 2:
                        apart[j] = apart[j] + size
                        pull[j] = pull[j] - slope
            near = 0.0
            for m in range(2):
                size, push = bend(x[m] - truth)
                near = near + size
                slope = push * (1.0 / members / line_span) - pull[m] * (1.0 / (members * (members - 1.0)) / line_span)
                slope_out[m * variables + start : m * variables + start + TILE, :] = slope.astype(BF16)
            term = near * (1.0 / members) - (apart[0] + apart[1]) * (1.0 / (2.0 * members * (members - 1)))
            summed += term[:8] + term[8:]
        loss[...] += summed
        grad[...] += dot_nt(slope_out[...], mat[:ext_rows, cols])

    for i, (mid, end) in enumerate(((own_mid, own_end), (pair_mid, pair_end))):
        rows = slice(i * variables, (i + 1) * variables)
        mid[...] = grad[rows, :count]
        end[...] = grad[rows, count:]


def borrowed_kernel(first, second, end):
    halo = first.shape[1]
    from_next, from_prev = sides(first[...], second[...])
    end[:, :halo] = from_prev
    end[:, halo:] = from_next


def ends_kernel(mine, got, first, second):
    halo = first.shape[1]
    total = mine[...] + got[...]
    to_first, to_second = sides(total[:, halo:], total[:, :halo])
    first[...] = to_first.astype(BF16)
    second[...] = to_second.astype(BF16)


def split(value):
    hi = value.astype(BF16)
    return hi, (value - hi.astype(F32)).astype(BF16)


LANES = 128


def encoded(total):
    tile = total[:, -LANES:]
    value = tile + pltpu.roll(tile, LANES // 2, 1)
    hi = value.astype(BF16).astype(F32)
    lane = lax.broadcasted_iota(jnp.int32, tile.shape, 1)
    tile = jnp.where(lane < LANES // 2, hi, value - hi)
    return jnp.concatenate([total[:, :-LANES].astype(BF16), tile.astype(BF16)], axis=1)


def backward_kernel(
    own_mid, pair_mid, from_first, from_second, to_next, to_prev, term, w_decode, vertex, nodes_t,
    picked_t, slope_t, slope_sum_t, agg_t, upd_slope_t, hidden_t,
    *refs,
):
    whole, back, grad_pre = refs[-3:]
    count = nodes_t.shape[1]
    width = nodes_t.shape[0]
    grad_z = own_mid[...] + pair_mid[...]
    for got, rows in zip((from_first, from_second), sides(to_next[...], to_prev[...])):
        grad_z += dot_nt(got[...], one_hot(count, rows))
    grad_z = grad_z.astype(BF16)
    main = whole.shape[1] - LANES
    whole[:, 3 * width : main] = dot_nt(hidden_t[...], grad_z)
    grad_upd = (dot(w_decode[...], grad_z) * upd_slope_t[...]).astype(BF16)
    whole[:, 2 * width : 3 * width] = dot_nt(agg_t[...], grad_upd)
    degree = slope_t.shape[1] // count
    back[...] = dot(vertex[...], grad_upd)
    for start in range(0, width, TILE):
        rows = slice(start, start + TILE)
        grad_agg = back[rows, :] * (0.5 / degree)
        grad_pre[rows, degree * count :] = (grad_agg * slope_sum_t[rows, :]).astype(BF16)
        for k in range(degree):
            here = slice(k * count, (k + 1) * count)
            grad_pre[rows, here] = (grad_agg * slope_t[rows, here].astype(F32)).astype(BF16)
    whole[:, width : 2 * width] = dot_nt(nodes_t[...], grad_pre[:, degree * count :])
    whole[:, :width] = dot_nt(picked_t[...], grad_pre[:, : degree * count])
    whole[:, main:] = jnp.zeros((width, LANES), F32)
    spot = (lax.broadcasted_iota(jnp.int32, (8, LANES), 0) == 0) & (lax.broadcasted_iota(jnp.int32, (8, LANES), 1) == 0)
    whole[0:8, main:] = jnp.where(spot, jnp.sum(term[...]), 0.0)
    if len(refs) == 3:
        return
    keep, send_first, send_rest = refs[:3]
    core, x, dom = position()
    share = width // 32

    def block(c, other, k):
        quarter = 2 * c + (1 - x if other else x)
        start = (8 * quarter + lax.bitwise_xor(dom, k)) * share
        return whole[pl.ds(pl.multiple_of(start, share), share), :]

    order = [(1, k) for k in (4, 5, 6, 7)]
    order += [(other, k) for k in (1, 2, 3) for other in (1, 0)]
    order += [(0, k) for k in (4, 5, 6, 7)] + [(1, 0), (0, 0)]
    for i, (other, k) in enumerate(order):
        keep[i * share : (i + 1) * share, :] = block(core, other, k)
        value = encoded(block(1 - core, other, k))
        if i < 4:
            send_first[i * share : (i + 1) * share, :] = value
        else:
            send_rest[(i - 4) * share : (i - 3) * share, :] = value


def far_kernel(keep, first, out):
    out[...] = encoded(keep[: out.shape[0], :] + first[...].astype(F32))


def pairs_kernel(keep, rest, *outs):
    rows = outs[0].shape[0]
    for k, out in enumerate(outs):
        out[...] = encoded(keep[(k + 2) * rows : (k + 3) * rows, :] + rest[k * rows : (k + 1) * rows, :].astype(F32))


def quads_kernel(keep, rest, far, *outs):
    rows = outs[0].shape[0]
    for k, out in enumerate(outs):
        total = keep[(k + 10) * rows : (k + 11) * rows, :] + rest[(k + 6) * rows : (k + 7) * rows, :].astype(F32)
        out[...] = encoded(total + far[k * rows : (k + 1) * rows, :].astype(F32))


def across_kernel(keep, rest, *refs):
    out = refs[-1]
    rows = out.shape[0]
    total = keep[14 * rows : 15 * rows, :] + rest[10 * rows : 11 * rows, :].astype(F32)
    for ref in refs[:-1]:
        total += ref[:rows, :].astype(F32)
    out[...] = encoded(total)


def own_kernel(keep, rest, *refs):
    out = refs[-1]
    rows = out.shape[0]
    total = keep[15 * rows :, :] + rest[11 * rows :, :].astype(F32)
    for ref in refs[:-1]:
        total += ref[ref.shape[0] - rows :, :].astype(F32)
    out[...] = encoded(total)


def join_kernel(*refs):
    start = 0
    for ref in refs[:-1]:
        refs[-1][start : start + ref.shape[0], :] = ref[...]
        start += ref.shape[0]


def pair_kernel(mine, other, after, out):
    del after
    rows = mine.shape[0]
    out[:rows, :] = mine[...]
    out[rows:, :] = other[...]


def finish_kernel(scale, *refs):
    g_send, g_recv, g_update, g_decode, loss = refs[-5:]
    pieces = refs[:-5]
    width = g_send.shape[1]
    share = width // 32
    core, x, dom = position()
    total = jnp.zeros((share, LANES), F32)
    for i, piece in enumerate(pieces):
        for j in range(piece.shape[0] // share):
            if i % 3 == 0:
                other, k = j % 2, j // 2
            else:
                other, k = i % 3 - 1, 4 + j
            quarter = 2 * (core if i < 3 else 1 - core) + (1 - x if other else x)
            start = (8 * quarter + lax.bitwise_xor(dom, k)) * share
            place = pl.ds(pl.multiple_of(start, share), share)
            value = piece[j * share : (j + 1) * share, :].astype(F32)
            g_send[place, :] = value[:, :width]
            g_recv[place, :] = value[:, width : 2 * width]
            g_update[place, :] = value[:, 2 * width : 3 * width]
            g_decode[place, :] = value[:, 3 * width : -LANES]
            total += value[:, -LANES:]
    loss[0, 0] = jnp.sum(total) * scale


def position():
    ens = lax.axis_index("ens")
    return lax.rem(ens, 2), lax.div(ens, 2), lax.axis_index("dom")


SCALAR = pl.BlockSpec(memory_space=pltpu.SMEM)


def meet(first, second):
    size = lax.axis_size("dom")
    second = lax.ppermute(second, "dom", [(i, (i + (1 if i % 2 else size - 1)) % size) for i in range(size)])
    return flip(first, "dom", 1), second


def flip(value, axis, bit):
    size = lax.axis_size(axis)
    return lax.ppermute(value, axis, [(i, i ^ bit) for i in range(size)])


def nbytes(arrays):
    return sum(x.size * x.dtype.itemsize for x in arrays)


def freed(specs, places):
    return [pl.BlockSpec(memory_space=pl.ANY) if i in places else x for i, x in enumerate(specs)]


def call(kernel, ins, outs, scratch=(), flops=0, room=4, in_hbm=0, out_hbm=0, limit=0, free_ins=(), free_outs=()):
    size = nbytes(list(ins) + list(outs))
    return pl.pallas_call(
        kernel,
        out_shape=outs,
        in_specs=freed(vmem(len(ins) - in_hbm) + [HBM] * in_hbm, free_ins),
        out_specs=freed(vmem(len(outs) - out_hbm) + [HBM] * out_hbm, free_outs),
        scratch_shapes=list(scratch),
        compiler_params=params(limit or 1.1 * size / MIB + room),
        cost_estimate=cost(flops, size),
    )(*ins)


def scalar(value):
    return jnp.reshape(value, (1,)).astype(jnp.int32)


def gathered(value):
    found = [value]
    bit = lax.axis_size("ens") // 2
    while bit:
        found = [x for v in found for x in (v, flip(v, "ens", bit))]
        bit //= 2
    return found


def summed(keep, send_first, send_rest):
    cols = keep.shape[1]
    share = keep.shape[0] // 16
    core = lambda v: flip(v, "ens", 1)
    over_x = lambda v: flip(v, "ens", 2)
    piece = lambda shares: sds((shares * share, cols), BF16)
    near, far = (1, 2, 3), (4, 5, 6, 7)
    first, rest = core(send_first), core(send_rest)
    (out,) = call(far_kernel, [keep, first], [piece(4)])
    from_x = over_x(out)
    outs = call(pairs_kernel, [keep, rest], [piece(2)] * 3)
    pairs = [flip(v, "dom", k) for k, v in zip(near, outs)]
    outs = call(quads_kernel, [keep, rest, from_x], [piece(1)] * 4)
    quads = [flip(v, "dom", k) for k, v in zip(far, outs)]
    (out,) = call(across_kernel, [keep, rest] + pairs, [piece(1)])
    got = over_x(out)
    (own,) = call(own_kernel, [keep, rest] + pairs + quads + [got], [piece(1)])

    (far_own,) = call(join_kernel, [flip(own, "dom", k) for k in far], [piece(4)])
    (pair,) = call(pair_kernel, [own, over_x(own), far_own], [piece(2)])
    (close,) = call(join_kernel, [pair] + [flip(pair, "dom", k) for k in near], [piece(8)])
    here = [close, far_own, over_x(far_own)]
    return here + [core(v) for v in here]


def per_device(
    nodes, senders, send_next, send_prev, readout_vertex_list, dec_weights, base, observed_analysis,
    w_send, w_recv, vertex_refresh_matrix, w_decode,
):
    latent = nodes[0]
    count, width = latent.shape
    halo = send_next.shape[0]
    line_span, variables = base.shape
    degree = senders.shape[0]
    fan = readout_vertex_list.shape[0]
    ext_rows = count + 2 * halo
    members = lax.axis_size("ens")
    ens, dom = lax.axis_index("ens"), lax.axis_index("dom")
    to_next, to_prev = send_next.reshape(1, halo), send_prev.reshape(1, halo)

    held = lambda shape, dtype=BF16: pltpu.VMEM(shape, dtype)
    indices = lambda: [held((1, halo), jnp.int32)] * 2
    nodes_t, first_t, second_t = call(
        lend_kernel,
        [latent, to_next, to_prev],
        [sds((width, count), BF16), sds((width, halo), BF16), sds((width, halo), BF16)],
        [held((count, width))] + indices() + [pltpu.SemaphoreType.DMA((3,))],
        flops=4 * width * count * halo,
        in_hbm=3,
        limit=56,
    )
    from_first, from_second = meet(first_t, second_t)

    core = scalar(lax.rem(ens, 2))
    block = 1024
    steps = line_span // 2 // block
    fixed = lambda shape: pl.BlockSpec(shape, lambda i, *at: (0,) * len(shape))
    tall = lambda rows: pl.BlockSpec((rows, block), lambda i, *at: (0, i))
    tall_half = lambda rows: pl.BlockSpec((rows, block), lambda i, at: (0, i + at[0] * steps))
    half_span = line_span // 2
    mat, base_t, truth_t, done = pl.pallas_call(
        decoder_kernel,
        grid_spec=pltpu.PrefetchScalarGridSpec(
            num_scalar_prefetch=1,
            grid=(steps,),
            in_specs=[tall_half(fan), tall_half(fan), HBM, HBM, pl.BlockSpec(memory_space=pl.ANY)],
            out_specs=[tall(2 * ext_rows), tall(variables), tall(variables), fixed((8, 128))],
            scratch_shapes=[held((half_span, variables)), held((half_span, variables)), pltpu.SemaphoreType.DMA((2,))],
        ),
        out_shape=[sds((2 * ext_rows, half_span), BF16)] + [sds((variables, half_span), BF16)] * 2 + [sds((8, 128), F32)],
        compiler_params=params(56),
        cost_estimate=cost(10 * ext_rows * half_span, 16e6),
    )(core, readout_vertex_list, dec_weights, base, observed_analysis, nodes_t)

    field_t, first_t, second_t, picked_t, slope_t, slope_sum_t, agg_t, upd_slope_t, hidden_t = call(
        forward_kernel,
        [nodes_t, from_first, from_second, senders, w_send, w_recv, to_next, to_prev, vertex_refresh_matrix, w_decode, done],
        [
            sds((variables, count), BF16), sds((variables, halo), BF16), sds((variables, halo), BF16),
            sds((width, degree * count), BF16), sds((width, degree * count), BF16), sds((width, count), F32),
            sds((width, count), BF16), sds((width, count), F32), sds((width, count), BF16),
        ],
        [held((width, ext_rows)), held((degree, count), jnp.int32), held((width, width)), held((width, width))] + indices() + [
            held((width, width)), held((width, variables)), held((width, degree * count)), held((width, count), F32),
            held((width, degree * count)), held((width, count), F32), held((width, count)), held((width, count), F32),
            held((width, count)), held((width, degree * count), F32),
            held((variables, count)), held((variables, halo)), held((variables, halo)),
            pltpu.SemaphoreType.DMA((10,)), pltpu.SemaphoreType.DMA((width // 128 + 7 + degree,)),
        ],
        flops=2 * degree * width * count * (ext_rows + width),
        in_hbm=11,
        out_hbm=9,
        free_ins=(1, 2),
        free_outs=(0, 1, 2),
        limit=52,
    )
    lent = meet(first_t, second_t)
    mids = gathered(field_t)

    (end,) = call(borrowed_kernel, list(lent), [sds((variables, 2 * halo), BF16)])
    ends = gathered(end)

    grads = call(
        functools.partial(readout_kernel, line_span),
        mids + ends + [mat, base_t, truth_t],
        [sds((variables, count), F32), sds((variables, 2 * halo), F32)] * 2 + [sds((8, 256), F32)],
        [held((members * variables, 2 * ext_rows)), held((2 * variables, ext_rows), F32)]
        + [held((members * variables, 256), F32)] * 2 + [held((2 * variables, 256))] * 2,
        flops=4 * members * variables * ext_rows * half_span,
        limit=24,
    )
    own_mid, own_end, pair_mid, pair_end, term = grads
    got_end = flip(pair_end, "ens", 1)
    got_mid = flip(pair_mid, "ens", 1)
    to_first, to_second = call(ends_kernel, [own_end, got_end], [sds((variables, halo), BF16)] * 2)
    from_first, from_second = meet(to_first, to_second)

    cols = 3 * width + variables + LANES
    operands = [
        own_mid, got_mid, from_first, from_second, to_next, to_prev, term, w_decode,
        vertex_refresh_matrix, nodes_t, picked_t, slope_t, slope_sum_t, agg_t, upd_slope_t, hidden_t,
    ]
    whole = sds((width, cols), F32)
    scratch = [held((width, count), F32), held((width, (degree + 1) * count))]
    flops = 2 * (degree + 3) * width * width * count
    scale = 1.0 / line_span
    if lax.axis_size("dom") != 8 or members != 4 or width % 512:
        (total,) = call(backward_kernel, operands, [whole], scratch, flops, room=16)
        total = lax.psum(total, ("ens", "dom"))
        cuts = [total[:, i * width : (i + 1) * width] for i in range(3)]
        return *cuts, total[:, 3 * width : -LANES], jnp.sum(total[:, -LANES:]) * scale
    block = width // 8
    parts = call(
        backward_kernel,
        operands,
        [sds((4 * block, cols), F32), sds((block, cols), BF16), sds((3 * block, cols), BF16)],
        [held(whole.shape, F32)] + scratch,
        flops,
        room=16,
    )
    pieces = summed(*parts)
    g_send, g_recv, g_update, g_decode, loss = pl.pallas_call(
        functools.partial(finish_kernel, scale),
        out_shape=[sds((width, width), F32)] * 3 + [sds((width, variables), F32), sds((1, 1), F32)],
        in_specs=vmem(len(pieces)),
        out_specs=vmem(4) + [SCALAR],
        compiler_params=params(14),
        cost_estimate=cost(0, 6 * width * cols),
    )(*pieces)
    return g_send, g_recv, g_update, g_decode, loss[0, 0]


def solution(mesh):
    return jax.shard_map(
        per_device,
        mesh=mesh,
        in_specs=(
            P("ens", "dom", None), P(None, "dom"), P("dom"), P("dom"), P(None, "dom"), P(None, "dom"),
            P("dom", None), P("dom", None), P(), P(), P(), P(),
        ),
        out_specs=(P(), P(), P(), P(), P()),
        check_vma=False,
    )
```

```python
import functools

import jax
import jax.numpy as jnp
from jax import lax
from jax.experimental import pallas as pl
from jax.experimental.pallas import tpu as pltpu
from jax.sharding import PartitionSpec as P

EPS = 0.04
F32 = jnp.float32
BF16 = jnp.bfloat16
MIB = 1024 * 1024


def dot(a, b, ca=1, cb=0):
    return lax.dot_general(a, b, (((ca,), (cb,)), ((), ())), preferred_element_type=F32)


def dot_nt(a, b):
    return dot(a, b, 1, 1)


def one_hot(rows, index_row):
    shape = (rows, index_row.shape[1])
    hit = lax.broadcasted_iota(jnp.int32, shape, 0) == index_row
    return jnp.where(hit, 1.0, 0.0).astype(BF16)


def params(mib):
    return pltpu.CompilerParams(vmem_limit_bytes=int(mib * MIB))


def vmem(n):
    return [pl.BlockSpec(memory_space=pltpu.VMEM)] * n


def cost(flops, size):
    return pl.CostEstimate(flops=int(flops), bytes_accessed=int(size), transcendentals=0)


def sds(shape, dtype):
    return jax.ShapeDtypeStruct(shape, dtype)


HBM = pl.BlockSpec(memory_space=pltpu.HBM)


def fetched(sources, targets, sems):
    copies = [pltpu.make_async_copy(a, b, sems.at[i]) for i, (a, b) in enumerate(zip(sources, targets))]
    for copy in copies:
        copy.start()
    return copies


def sides(next_side, prev_side):
    even = lax.rem(lax.axis_index("dom"), 2) == 0
    return jnp.where(even, next_side, prev_side), jnp.where(even, prev_side, next_side)


def lend_kernel(nodes, to_next, to_prev, nodes_t, first_t, second_t, held, rows_next, rows_prev, sems):
    for copy in fetched((nodes, to_next, to_prev), (held, rows_next, rows_prev), sems):
        copy.wait()
    table = held[...].T
    nodes_t[...] = table
    count = table.shape[1]
    first, second = sides(rows_next[...], rows_prev[...])
    first_t[...] = dot(table, one_hot(count, first)).astype(BF16)
    second_t[...] = dot(table, one_hot(count, second)).astype(BF16)


def decoder_kernel(core, vertices, weights, base, truth, after, mat, base_t, truth_t, done, base_rows, truth_rows, sems):
    del after
    done[...] = jnp.zeros_like(done)
    span = base_rows.shape[0]
    half = pl.ds(pl.multiple_of(core[0] * span, span), span)
    copies = [
        pltpu.make_async_copy(base.at[half, :], base_rows, sems.at[0]),
        pltpu.make_async_copy(truth.at[half, :], truth_rows, sems.at[1]),
    ]

    @pl.when(pl.program_id(0) == 0)
    def _():
        for copy in copies:
            copy.start()

    rows, lanes = mat.shape[0] // 2, 256
    row = lax.broadcasted_iota(jnp.int32, (8, lanes), 0)
    for left in range(0, mat.shape[1], lanes):
        cols = slice(left, left + lanes)
        spread = lambda ref, k: jnp.broadcast_to(ref[k : k + 1, cols], (8, lanes))
        ahead = [spread(vertices, k) - row for k in range(vertices.shape[0])]
        weight = [spread(weights, k) for k in range(vertices.shape[0])]

        def weighted(start):
            total = jnp.where(ahead[0] == start, weight[0], 0.0)
            for k in range(1, len(ahead)):
                total += jnp.where(ahead[k] == start, weight[k], 0.0)
            return total

        for start in range(0, rows, 16):
            hi, lo = split(jnp.concatenate([weighted(start), weighted(start + 8)], axis=0))
            mat[start : start + 16, cols] = hi
            mat[rows + start : rows + start + 16, cols] = lo

    step, block = pl.program_id(0), mat.shape[1]

    @pl.when(step == 0)
    def _():
        for copy in copies:
            copy.wait()

    some = pl.ds(pl.multiple_of(step * block, block), block)
    base_t[...] = base_rows[some, :].T
    truth_t[...] = truth_rows[some, :].T


TILE = 16


def bent(half):
    t = jnp.tanh(half)
    u = half * t
    return half + u, (1.0 + t) * (1.0 + half - u)


def forward_kernel(
    nodes_in, from_first, from_second, senders_in, w_send_in, w_recv_in, to_next_in, to_prev_in, vertex_in, w_decode_in, after,
    field_out, first_out, second_out, picked_out, slope_out, slope_sum_out, agg_out, upd_slope_out, hidden_out,
    ext, senders, w_send, w_recv, to_next, to_prev, vertex, w_decode, picked_t, recv_t,
    slope_t, slope_sum_t, agg_t, upd_slope_t, hidden_t, pre, field_t, first_t, second_t, in_sems, out_sems,
):
    del after
    degree, count = senders.shape
    width, ext_rows = ext.shape
    halo = from_first.shape[1]
    swap = lax.rem(lax.axis_index("dom"), 2) * halo
    column = lambda start: ext.at[:, pl.ds(pl.multiple_of(start, 128), halo)]
    fetch = fetched(
        (nodes_in, from_first, from_second, senders_in, w_recv_in, w_send_in, vertex_in, to_next_in, to_prev_in, w_decode_in),
        (
            ext.at[:, :count], column(count + halo - swap), column(count + swap),
            senders, w_recv, w_send, vertex, to_next, to_prev, w_decode,
        ),
        in_sems,
    )
    stored = []

    def store(source, target):
        copy = pltpu.make_async_copy(source, target, out_sems.at[len(stored)])
        copy.start()
        stored.append(copy)

    for copy in fetch[:4]:
        copy.wait()
    for k in range(degree):
        here = slice(k * count, (k + 1) * count)
        picked_t[:, here] = dot(ext[...], one_hot(ext_rows, senders[k : k + 1, :])).astype(BF16)
        store(picked_t.at[:, here], picked_out.at[:, here])
        if k == 0:
            for copy in fetch[4:]:
                copy.wait()
            w_send_t = w_send[...].T * 0.5
        pre[:, here] = dot(w_send_t, picked_t[:, here])
    recv_t[...] = dot(w_recv[...].T, ext[:, :count]) * 0.5
    for start in range(0, width, TILE):
        rows = slice(start, start + TILE)
        recv = recv_t[rows, :]
        total = slopes = None
        for k in range(degree):
            here = slice(k * count, (k + 1) * count)
            value, slope = bent(pre[rows, here] + recv)
            slope_t[rows, here] = slope.astype(BF16)
            total = value if k == 0 else total + value
            slopes = slope if k == 0 else slopes + slope
        slope_sum_t[rows, :] = slopes
        agg_t[rows, :] = (total * (1.0 / degree)).astype(BF16)
        if (start + TILE) % 128 == 0:
            group = slice(start + TILE - 128, start + TILE)
            store(slope_t.at[group, :], slope_out.at[group, :])
    store(slope_sum_t, slope_sum_out)
    store(agg_t, agg_out)
    pre[:, :count] = dot(vertex[...].T * 0.5, agg_t[...])
    for start in range(0, width, TILE):
        rows = slice(start, start + TILE)
        value, slope = bent(pre[rows, :count])
        upd_slope_t[rows, :] = slope * 0.5
        hidden_t[rows, :] = (ext[rows, :count].astype(F32) + value).astype(BF16)
    store(hidden_t, hidden_out)
    store(upd_slope_t, upd_slope_out)
    field = dot(w_decode[...].T, hidden_t[...]).astype(BF16)
    field_t[...] = field
    first, second = sides(to_next[...], to_prev[...])
    first_t[...] = dot(field, one_hot(count, first)).astype(BF16)
    second_t[...] = dot(field, one_hot(count, second)).astype(BF16)
    store(field_t, field_out)
    store(first_t, first_out)
    store(second_t, second_out)
    for copy in stored:
        copy.wait()


def readout_kernel(line_span, *refs):
    mids, ends = refs[0:4], refs[4:8]
    mat, base_t, truth_t = refs[8:11]
    own_mid, own_end, pair_mid, pair_end, loss = refs[11:16]
    table, grad = refs[16:18]
    subs = (len(refs) - 18) // 2
    states, slopes = refs[18 : 18 + subs], refs[18 + subs :]
    members = len(mids)
    variables, count = own_mid.shape
    ext_rows = grad.shape[1]

    grad[...] = jnp.zeros_like(grad)
    loss[...] = jnp.zeros_like(loss)
    for m in range(members):
        for start in (0, ext_rows):
            table[m * variables : (m + 1) * variables, start : start + count] = mids[m][...]
            table[m * variables : (m + 1) * variables, start + count : start + ext_rows] = ends[m][...]

    def bend(diff):
        square = diff * diff + EPS
        inverse = lax.rsqrt(square)
        return square * inverse, diff * inverse

    alone = EPS**0.5
    wide = states[0].shape[1]
    blocks = mat.shape[1] // wide

    def decode(i):
        states[i % 2][...] = dot(table[...], mat[:, i * wide : (i + 1) * wide])

    decode(0)
    for i in range(blocks):
        state, slope_out = states[i % 2], slopes[i % 2]
        cols = slice(i * wide, (i + 1) * wide)
        if i + 1 < blocks:
            decode(i + 1)
        summed = jnp.zeros((8, wide), F32)
        for start in range(0, variables, TILE):
            rows = slice(start, start + TILE)
            ready = base_t[rows, cols].astype(F32)
            truth = truth_t[rows, cols].astype(F32)
            x = [
                (state[m * variables + start : m * variables + start + TILE, :] + ready).astype(BF16).astype(F32)
                for m in range(members)
            ]
            apart = [alone, alone]
            pull = [0.0, 0.0]
            for m in range(2):
                for j in range(m + 1, members):
                    size, slope = bend(x[m] - x[j])
                    apart[m] = apart[m] + size
                    pull[m] = pull[m] + slope
                    if j < 2:
                        apart[j] = apart[j] + size
                        pull[j] = pull[j] - slope
            near = 0.0
            for m in range(2):
                size, push = bend(x[m] - truth)
                near = near + size
                slope = push * (1.0 / members / line_span) - pull[m] * (1.0 / (members * (members - 1.0)) / line_span)
                slope_out[m * variables + start : m * variables + start + TILE, :] = slope.astype(BF16)
            term = near * (1.0 / members) - (apart[0] + apart[1]) * (1.0 / (2.0 * members * (members - 1)))
            summed += term[:8] + term[8:]
        loss[...] += summed
        grad[...] += dot_nt(slope_out[...], mat[:ext_rows, cols])

    for i, (mid, end) in enumerate(((own_mid, own_end), (pair_mid, pair_end))):
        rows = slice(i * variables, (i + 1) * variables)
        mid[...] = grad[rows, :count]
        end[...] = grad[rows, count:]


def borrowed_kernel(first, second, end):
    halo = first.shape[1]
    from_next, from_prev = sides(first[...], second[...])
    end[:, :halo] = from_prev
    end[:, halo:] = from_next


def ends_kernel(mine, got, first, second):
    halo = first.shape[1]
    total = mine[...] + got[...]
    to_first, to_second = sides(total[:, halo:], total[:, :halo])
    first[...] = to_first.astype(BF16)
    second[...] = to_second.astype(BF16)


def split(value):
    hi = value.astype(BF16)
    return hi, (value - hi.astype(F32)).astype(BF16)


LANES = 128


def encoded(total):
    tile = total[:, -LANES:]
    value = tile + pltpu.roll(tile, LANES // 2, 1)
    hi = value.astype(BF16).astype(F32)
    lane = lax.broadcasted_iota(jnp.int32, tile.shape, 1)
    tile = jnp.where(lane < LANES // 2, hi, value - hi)
    return jnp.concatenate([total[:, :-LANES].astype(BF16), tile.astype(BF16)], axis=1)


def backward_kernel(
    own_mid, pair_mid, from_first, from_second, to_next, to_prev, term, w_decode, vertex, nodes_t,
    picked_t, slope_t, slope_sum_t, agg_t, upd_slope_t, hidden_t,
    *refs,
):
    whole, back, grad_pre = refs[-3:]
    count = nodes_t.shape[1]
    width = nodes_t.shape[0]
    grad_z = own_mid[...] + pair_mid[...]
    for got, rows in zip((from_first, from_second), sides(to_next[...], to_prev[...])):
        grad_z += dot_nt(got[...], one_hot(count, rows))
    grad_z = grad_z.astype(BF16)
    main = whole.shape[1] - LANES
    whole[:, 3 * width : main] = dot_nt(hidden_t[...], grad_z)
    grad_upd = (dot(w_decode[...], grad_z) * upd_slope_t[...]).astype(BF16)
    whole[:, 2 * width : 3 * width] = dot_nt(agg_t[...], grad_upd)
    degree = slope_t.shape[1] // count
    back[...] = dot(vertex[...], grad_upd)
    for start in range(0, width, TILE):
        rows = slice(start, start + TILE)
        grad_agg = back[rows, :] * (0.5 / degree)
        grad_pre[rows, degree * count :] = (grad_agg * slope_sum_t[rows, :]).astype(BF16)
        for k in range(degree):
            here = slice(k * count, (k + 1) * count)
            grad_pre[rows, here] = (grad_agg * slope_t[rows, here].astype(F32)).astype(BF16)
    whole[:, width : 2 * width] = dot_nt(nodes_t[...], grad_pre[:, degree * count :])
    whole[:, :width] = dot_nt(picked_t[...], grad_pre[:, : degree * count])
    whole[:, main:] = jnp.zeros((width, LANES), F32)
    spot = (lax.broadcasted_iota(jnp.int32, (8, LANES), 0) == 0) & (lax.broadcasted_iota(jnp.int32, (8, LANES), 1) == 0)
    whole[0:8, main:] = jnp.where(spot, jnp.sum(term[...]), 0.0)
    if len(refs) == 3:
        return
    keep, send_first, send_rest = refs[:3]
    core, x, dom = position()
    share = width // 32

    def block(c, other, k):
        quarter = 2 * c + (1 - x if other else x)
        start = (8 * quarter + lax.bitwise_xor(dom, k)) * share
        return whole[pl.ds(pl.multiple_of(start, share), share), :]

    order = [(1, k) for k in (4, 5, 6, 7)]
    order += [(other, k) for k in (1, 2, 3) for other in (1, 0)]
    order += [(0, k) for k in (4, 5, 6, 7)] + [(1, 0), (0, 0)]
    for i, (other, k) in enumerate(order):
        keep[i * share : (i + 1) * share, :] = block(core, other, k)
        value = encoded(block(1 - core, other, k))
        if i < 4:
            send_first[i * share : (i + 1) * share, :] = value
        else:
            send_rest[(i - 4) * share : (i - 3) * share, :] = value


def far_kernel(keep, first, out):
    out[...] = encoded(keep[: out.shape[0], :] + first[...].astype(F32))


def pairs_kernel(keep, rest, *outs):
    rows = outs[0].shape[0]
    for k, out in enumerate(outs):
        out[...] = encoded(keep[(k + 2) * rows : (k + 3) * rows, :] + rest[k * rows : (k + 1) * rows, :].astype(F32))


def quads_kernel(keep, rest, far, *outs):
    rows = outs[0].shape[0]
    for k, out in enumerate(outs):
        total = keep[(k + 10) * rows : (k + 11) * rows, :] + rest[(k + 6) * rows : (k + 7) * rows, :].astype(F32)
        out[...] = encoded(total + far[k * rows : (k + 1) * rows, :].astype(F32))


def across_kernel(keep, rest, *refs):
    out = refs[-1]
    rows = out.shape[0]
    total = keep[14 * rows : 15 * rows, :] + rest[10 * rows : 11 * rows, :].astype(F32)
    for ref in refs[:-1]:
        total += ref[:rows, :].astype(F32)
    out[...] = encoded(total)


def own_kernel(keep, rest, *refs):
    out = refs[-1]
    rows = out.shape[0]
    total = keep[15 * rows :, :] + rest[11 * rows :, :].astype(F32)
    for ref in refs[:-1]:
        total += ref[ref.shape[0] - rows :, :].astype(F32)
    out[...] = encoded(total)


def join_kernel(*refs):
    start = 0
    for ref in refs[:-1]:
        refs[-1][start : start + ref.shape[0], :] = ref[...]
        start += ref.shape[0]


def pair_kernel(mine, other, after, out):
    del after
    rows = mine.shape[0]
    out[:rows, :] = mine[...]
    out[rows:, :] = other[...]


def finish_kernel(scale, *refs):
    g_send, g_recv, g_update, g_decode, loss = refs[-5:]
    pieces = refs[:-5]
    width = g_send.shape[1]
    share = width // 32
    core, x, dom = position()
    total = jnp.zeros((share, LANES), F32)
    for i, piece in enumerate(pieces):
        for j in range(piece.shape[0] // share):
            if i % 3 == 0:
                other, k = j % 2, j // 2
            else:
                other, k = i % 3 - 1, 4 + j
            quarter = 2 * (core if i < 3 else 1 - core) + (1 - x if other else x)
            start = (8 * quarter + lax.bitwise_xor(dom, k)) * share
            place = pl.ds(pl.multiple_of(start, share), share)
            value = piece[j * share : (j + 1) * share, :].astype(F32)
            g_send[place, :] = value[:, :width]
            g_recv[place, :] = value[:, width : 2 * width]
            g_update[place, :] = value[:, 2 * width : 3 * width]
            g_decode[place, :] = value[:, 3 * width : -LANES]
            total += value[:, -LANES:]
    loss[0, 0] = jnp.sum(total) * scale


def position():
    ens = lax.axis_index("ens")
    return lax.rem(ens, 2), lax.div(ens, 2), lax.axis_index("dom")


SCALAR = pl.BlockSpec(memory_space=pltpu.SMEM)


def meet(first, second):
    size = lax.axis_size("dom")
    second = lax.ppermute(second, "dom", [(i, (i + (1 if i % 2 else size - 1)) % size) for i in range(size)])
    return flip(first, "dom", 1), second


def flip(value, axis, bit):
    size = lax.axis_size(axis)
    return lax.ppermute(value, axis, [(i, i ^ bit) for i in range(size)])


def nbytes(arrays):
    return sum(x.size * x.dtype.itemsize for x in arrays)


def freed(specs, places):
    return [pl.BlockSpec(memory_space=pl.ANY) if i in places else x for i, x in enumerate(specs)]


def call(kernel, ins, outs, scratch=(), flops=0, room=4, in_hbm=0, out_hbm=0, limit=0, free_ins=(), free_outs=()):
    size = nbytes(list(ins) + list(outs))
    return pl.pallas_call(
        kernel,
        out_shape=outs,
        in_specs=freed(vmem(len(ins) - in_hbm) + [HBM] * in_hbm, free_ins),
        out_specs=freed(vmem(len(outs) - out_hbm) + [HBM] * out_hbm, free_outs),
        scratch_shapes=list(scratch),
        compiler_params=params(limit or 1.1 * size / MIB + room),
        cost_estimate=cost(flops, size),
    )(*ins)


def scalar(value):
    return jnp.reshape(value, (1,)).astype(jnp.int32)


def gathered(value):
    found = [value]
    bit = lax.axis_size("ens") // 2
    while bit:
        found = [x for v in found for x in (v, flip(v, "ens", bit))]
        bit //= 2
    return found


def summed(keep, send_first, send_rest):
    cols = keep.shape[1]
    share = keep.shape[0] // 16
    core = lambda v: flip(v, "ens", 1)
    over_x = lambda v: flip(v, "ens", 2)
    piece = lambda shares: sds((shares * share, cols), BF16)
    near, far = (1, 2, 3), (4, 5, 6, 7)
    first, rest = core(send_first), core(send_rest)
    (out,) = call(far_kernel, [keep, first], [piece(4)])
    from_x = over_x(out)
    outs = call(pairs_kernel, [keep, rest], [piece(2)] * 3)
    pairs = [flip(v, "dom", k) for k, v in zip(near, outs)]
    outs = call(quads_kernel, [keep, rest, from_x], [piece(1)] * 4)
    quads = [flip(v, "dom", k) for k, v in zip(far, outs)]
    (out,) = call(across_kernel, [keep, rest] + pairs, [piece(1)])
    got = over_x(out)
    (own,) = call(own_kernel, [keep, rest] + pairs + quads + [got], [piece(1)])

    (far_own,) = call(join_kernel, [flip(own, "dom", k) for k in far], [piece(4)])
    (pair,) = call(pair_kernel, [own, over_x(own), far_own], [piece(2)])
    (close,) = call(join_kernel, [pair] + [flip(pair, "dom", k) for k in near], [piece(8)])
    here = [close, far_own, over_x(far_own)]
    return here + [core(v) for v in here]


def per_device(
    nodes, senders, send_next, send_prev, readout_vertex_list, dec_weights, base, observed_analysis,
    w_send, w_recv, vertex_refresh_matrix, w_decode,
):
    latent = nodes[0]
    count, width = latent.shape
    halo = send_next.shape[0]
    line_span, variables = base.shape
    degree = senders.shape[0]
    fan = readout_vertex_list.shape[0]
    ext_rows = count + 2 * halo
    members = lax.axis_size("ens")
    ens, dom = lax.axis_index("ens"), lax.axis_index("dom")
    to_next, to_prev = send_next.reshape(1, halo), send_prev.reshape(1, halo)

    held = lambda shape, dtype=BF16: pltpu.VMEM(shape, dtype)
    indices = lambda: [held((1, halo), jnp.int32)] * 2
    nodes_t, first_t, second_t = call(
        lend_kernel,
        [latent, to_next, to_prev],
        [sds((width, count), BF16), sds((width, halo), BF16), sds((width, halo), BF16)],
        [held((count, width))] + indices() + [pltpu.SemaphoreType.DMA((3,))],
        flops=4 * width * count * halo,
        in_hbm=3,
        limit=56,
    )
    from_first, from_second = meet(first_t, second_t)

    core = scalar(lax.rem(ens, 2))
    block = 1024
    steps = line_span // 2 // block
    fixed = lambda shape: pl.BlockSpec(shape, lambda i, *at: (0,) * len(shape))
    tall = lambda rows: pl.BlockSpec((rows, block), lambda i, *at: (0, i))
    tall_half = lambda rows: pl.BlockSpec((rows, block), lambda i, at: (0, i + at[0] * steps))
    half_span = line_span // 2
    mat, base_t, truth_t, done = pl.pallas_call(
        decoder_kernel,
        grid_spec=pltpu.PrefetchScalarGridSpec(
            num_scalar_prefetch=1,
            grid=(steps,),
            in_specs=[tall_half(fan), tall_half(fan), HBM, HBM, pl.BlockSpec(memory_space=pl.ANY)],
            out_specs=[tall(2 * ext_rows), tall(variables), tall(variables), fixed((8, 128))],
            scratch_shapes=[held((half_span, variables)), held((half_span, variables)), pltpu.SemaphoreType.DMA((2,))],
        ),
        out_shape=[sds((2 * ext_rows, half_span), BF16)] + [sds((variables, half_span), BF16)] * 2 + [sds((8, 128), F32)],
        compiler_params=params(56),
        cost_estimate=cost(10 * ext_rows * half_span, 16e6),
    )(core, readout_vertex_list, dec_weights, base, observed_analysis, nodes_t)

    field_t, first_t, second_t, picked_t, slope_t, slope_sum_t, agg_t, upd_slope_t, hidden_t = call(
        forward_kernel,
        [nodes_t, from_first, from_second, senders, w_send, w_recv, to_next, to_prev, vertex_refresh_matrix, w_decode, done],
        [
            sds((variables, count), BF16), sds((variables, halo), BF16), sds((variables, halo), BF16),
            sds((width, degree * count), BF16), sds((width, degree * count), BF16), sds((width, count), F32),
            sds((width, count), BF16), sds((width, count), F32), sds((width, count), BF16),
        ],
        [held((width, ext_rows)), held((degree, count), jnp.int32), held((width, width)), held((width, width))] + indices() + [
            held((width, width)), held((width, variables)), held((width, degree * count)), held((width, count), F32),
            held((width, degree * count)), held((width, count), F32), held((width, count)), held((width, count), F32),
            held((width, count)), held((width, degree * count), F32),
            held((variables, count)), held((variables, halo)), held((variables, halo)),
            pltpu.SemaphoreType.DMA((10,)), pltpu.SemaphoreType.DMA((width // 128 + 7 + degree,)),
        ],
        flops=2 * degree * width * count * (ext_rows + width),
        in_hbm=11,
        out_hbm=9,
        free_ins=(1, 2),
        free_outs=(0, 1, 2),
        limit=52,
    )
    lent = meet(first_t, second_t)
    mids = gathered(field_t)

    (end,) = call(borrowed_kernel, list(lent), [sds((variables, 2 * halo), BF16)])
    ends = gathered(end)

    grads = call(
        functools.partial(readout_kernel, line_span),
        mids + ends + [mat, base_t, truth_t],
        [sds((variables, count), F32), sds((variables, 2 * halo), F32)] * 2 + [sds((8, 512), F32)],
        [held((members * variables, 2 * ext_rows)), held((2 * variables, ext_rows), F32)]
        + [held((members * variables, 512), F32)] * 2 + [held((2 * variables, 512))] * 2,
        flops=4 * members * variables * ext_rows * half_span,
        limit=24,
    )
    own_mid, own_end, pair_mid, pair_end, term = grads
    got_end = flip(pair_end, "ens", 1)
    got_mid = flip(pair_mid, "ens", 1)
    to_first, to_second = call(ends_kernel, [own_end, got_end], [sds((variables, halo), BF16)] * 2)
    from_first, from_second = meet(to_first, to_second)

    cols = 3 * width + variables + LANES
    operands = [
        own_mid, got_mid, from_first, from_second, to_next, to_prev, term, w_decode,
        vertex_refresh_matrix, nodes_t, picked_t, slope_t, slope_sum_t, agg_t, upd_slope_t, hidden_t,
    ]
    whole = sds((width, cols), F32)
    scratch = [held((width, count), F32), held((width, (degree + 1) * count))]
    flops = 2 * (degree + 3) * width * width * count
    scale = 1.0 / line_span
    if lax.axis_size("dom") != 8 or members != 4 or width % 512:
        (total,) = call(backward_kernel, operands, [whole], scratch, flops, room=16)
        total = lax.psum(total, ("ens", "dom"))
        cuts = [total[:, i * width : (i + 1) * width] for i in range(3)]
        return *cuts, total[:, 3 * width : -LANES], jnp.sum(total[:, -LANES:]) * scale
    block = width // 8
    parts = call(
        backward_kernel,
        operands,
        [sds((4 * block, cols), F32), sds((block, cols), BF16), sds((3 * block, cols), BF16)],
        [held(whole.shape, F32)] + scratch,
        flops,
        room=16,
    )
    pieces = summed(*parts)
    g_send, g_recv, g_update, g_decode, loss = pl.pallas_call(
        functools.partial(finish_kernel, scale),
        out_shape=[sds((width, width), F32)] * 3 + [sds((width, variables), F32), sds((1, 1), F32)],
        in_specs=vmem(len(pieces)),
        out_specs=vmem(4) + [SCALAR],
        compiler_params=params(14),
        cost_estimate=cost(0, 6 * width * cols),
    )(*pieces)
    return g_send, g_recv, g_update, g_decode, loss[0, 0]


def solution(mesh):
    return jax.shard_map(
        per_device,
        mesh=mesh,
        in_specs=(
            P("ens", "dom", None), P(None, "dom"), P("dom"), P("dom"), P(None, "dom"), P(None, "dom"),
            P("dom", None), P("dom", None), P(), P(), P(), P(),
        ),
        out_specs=(P(), P(), P(), P(), P()),
        check_vma=False,
    )
```
